32 devices in a mesh: seq: 8 (over z, x), chan: 4 (over y, core).
Axes of the slice: x: 2, y: 2, z: 4, core: 2. Of those that a mesh axis runs over, the one named last changes fastest.
Arguments:
- block_input: float32 [8, 2048, 768], P(None, 'seq'), may hold values from -6 to 6
- lengths: int32 [8], replicated, may hold values from 256 to 2048, as said below
- ln1_gain: float32 [768], replicated, may hold values from 0.5 to 1.5
- ln1_bias: float32 [768], replicated, may hold values from -1.75 to 1.75
- input_weight: float32 [768, 3, 768], P(None, None, 'chan'), may hold values from -0.21875 to 0.21875
- input_bias: float32 [3, 768], P(None, 'chan'), may hold values from -1.75 to 1.75
- conv_w: float32 [3, 3, 768], P(None, None, 'chan'), may hold values from -3.5 to 3.5
- conv_b: float32 [3, 768], P(None, 'chan'), may hold values from -1.75 to 1.75
- filt_w1: float32 [33, 64], replicated, may hold values from -6 to 6
- filt_b1: float32 [64], replicated, may hold values from -3.140625 to 3.140625
- filt_w2: float32 [64, 64], replicated, may hold values from -7.5 to 7.5
- filt_b2: float32 [64], replicated, may hold values from -3.140625 to 3.140625
- filt_w3: float32 [64, 768], P(None, 'chan'), may hold values from -0.125 to 0.125
- decay: float32 [768], P('chan'), may hold values from 0.00024414062 to 0.06
- skip: float32 [768], P('chan'), may hold values from -6 to 6
- output_weight: float32 [768, 768], P('chan'), may hold values from -0.21875 to 0.21875
- output_bias: float32 [768], replicated, may hold values from -1.75 to 1.75
- ln2_gain: float32 [768], replicated, may hold values from 0.5 to 1.5
- ln2_bias: float32 [768], replicated, may hold values from -1.75 to 1.75
- up_weight: float32 [768, 3072], P(None, 'chan'), may hold values from -0.21875 to 0.21875
- up_bias: float32 [3072], P('chan'), may hold values from -1.75 to 1.75
- down_weight: float32 [3072, 768], P('chan'), may hold values from -0.109375 to 0.109375
- down_bias: float32 [768], replicated, may hold values from -1.75 to 1.75
- cotangent: float32 [8, 2048, 768], P(None, 'seq'), may hold values from -6 to 6
Outputs:
- output: float32 [8, 2048, 768], P(None, 'seq')
- grad_x: float32 [8, 2048, 768], P(None, 'seq')
- grad_ln1_gain: float32 [768], replicated
- grad_ln1_bias: float32 [768], replicated
- grad_w_in: float32 [768, 3, 768], P(None, None, 'chan')
- grad_b_in: float32 [3, 768], P(None, 'chan')
- grad_conv_w: float32 [3, 3, 768], P(None, None, 'chan')
- grad_conv_b: float32 [3, 768], P(None, 'chan')
- grad_filt_w1: float32 [33, 64], replicated
- grad_filt_b1: float32 [64], replicated
- grad_filt_w2: float32 [64, 64], replicated
- grad_filt_b2: float32 [64], replicated
- grad_filt_w3: float32 [64, 768], P(None, 'chan')
- grad_decay: float32 [768], P('chan')
- grad_skip: float32 [768], P('chan')
- grad_w_out: float32 [768, 768], P('chan')
- grad_b_out: float32 [768], replicated
- grad_ln2_gain: float32 [768], replicated
- grad_ln2_bias: float32 [768], replicated
- grad_w_fc1: float32 [768, 3072], P(None, 'chan')
- grad_b_fc1: float32 [3072], P('chan')
- grad_w_fc2: float32 [3072, 768], P('chan')
- grad_b_fc2: float32 [768], replicated
The draws below stay inside these ranges and needn't reach their ends.
Inputs may be any that keep to these rules, and one draw needn't show every extreme that they name: `lengths`: each sequence is valid up to its length; exactly one sequence has the full length 2048, the others are shorter.
All inputs are finite; a program needn't handle non-finite values.
Results may differ from the reference program's by a relative error of at most 0.0003.
Values sent between devices are 32-bit elements; how exact they have to be, the bound alone decides.
No kernel may reach another device: no remote copies, remote signals or barrier semaphores. Data moves between devices by JAX's collectives and lax.ppermute only.
A program may use at most 256 MiB of HBM per device.

```python
import math
import jax
import jax.numpy as jnp
from jax import lax

D = 768
FF = 3072
FILT = 64
EMB = 33
SEQS = 8
SEQ_LEN = 2048


def draw_lengths(key, part):
    key = jax.random.fold_in(key, 11)
    length_key, pick_key = jax.random.split(key)
    longest = SEQ_LEN
    drawn = jax.random.randint(length_key, (SEQS,), longest // 8, longest)
    picked = jax.random.randint(pick_key, (), 0, SEQS)
    return jnp.where(jnp.arange(SEQS) == picked, longest, drawn).astype(jnp.int32)


def spread_weights(key, rows, cols, spread):
    return spread * jax.random.truncated_normal(key, -3.0, 3.0, (rows, cols), jnp.float32)


def draw_filt_w1(key, part):
    key = jax.random.fold_in(key, 23)
    return spread_weights(key, EMB, FILT, 2.0)


def draw_filt_w2(key, part):
    key = jax.random.fold_in(key, 37)
    return spread_weights(key, FILT, FILT, 2.5)


def block_scale(rng, dims, cuts, low, top_value):
    loudness = 1.0
    for position, blocks in cuts:
        draws = jax.random.uniform(jax.random.fold_in(jax.random.fold_in(rng, 6), position), (blocks,), jnp.float32, low / len(cuts), top_value / len(cuts))
        loudness = loudness * jnp.repeat(jnp.exp(draws), dims[position] // blocks).reshape((-1,) + (1,) * (len(dims) - 1 - position))
    return loudness


def centred(key, dims, deviation, limit, cuts=(), kind=jnp.bfloat16):
    level = block_scale(key, dims, cuts, -0.22, 0.18) if cuts else 1.0
    entries = jax.random.normal(key, dims, jnp.float32) * deviation * level
    return jnp.minimum(jnp.maximum(entries, -limit), limit).astype(kind)


def setup_inputs(seed: int = 0) -> dict:
    splits = jax.random.split(jax.random.key(seed), 25)
    block_input = centred(splits[0], (SEQS, SEQ_LEN, D), 1.0, 6.0, ((1, 8),), jnp.float32)
    lengths = draw_lengths(jax.random.fold_in(splits[24], 71), 0)
    ln1_gain = jnp.clip(1.0 + 0.1 * jax.random.normal(splits[2], (D,), jnp.float32), 0.5, 1.5)
    ln1_bias = centred(splits[3], (D,), 0.3, 1.75, (), jnp.float32)
    input_weight = centred(splits[4], (D, 3, D), D ** -0.5, 0.21875, ((2, 4),), jnp.float32)
    input_bias = centred(splits[5], (3, D), 0.3, 1.75, ((1, 4),), jnp.float32)
    conv_w = centred(splits[6], (3, 3, D), 0.6, 3.5, ((2, 4),), jnp.float32)
    conv_b = centred(splits[7], (3, D), 0.3, 1.75, ((1, 4),), jnp.float32)
    filt_w1 = draw_filt_w1(jax.random.fold_in(splits[24], 71), 0)
    filt_b1 = jnp.clip(jax.random.uniform(splits[9], (FILT,), jnp.float32, -3.140625, 3.140625), -3.140625, 3.140625)
    filt_w2 = draw_filt_w2(jax.random.fold_in(splits[24], 71), 0)
    filt_b2 = jnp.clip(jax.random.uniform(splits[11], (FILT,), jnp.float32, -3.140625, 3.140625), -3.140625, 3.140625)
    filt_w3 = centred(splits[12], (FILT, D), (FILT * 32) ** -0.5, 0.125, ((1, 4),), jnp.float32)
    decay = jnp.clip(jnp.exp(math.log(0.06) - 5.5043554 * jax.random.uniform(splits[13], (D,), jnp.float32) ** block_scale(splits[13], (D,), ((0, 4),), -0.2, 0.2)), 0.00024414062, 0.06)
    skip = centred(splits[14], (D,), 1.0, 6.0, ((0, 4),), jnp.float32)
    output_weight = centred(splits[15], (D, D), D ** -0.5, 0.21875, ((0, 4),), jnp.float32)
    output_bias = centred(splits[16], (D,), 0.3, 1.75, (), jnp.float32)
    ln2_gain = jnp.clip(1.0 + 0.1 * jax.random.normal(splits[17], (D,), jnp.float32), 0.5, 1.5)
    ln2_bias = centred(splits[18], (D,), 0.3, 1.75, (), jnp.float32)
    up_weight = centred(splits[19], (D, FF), D ** -0.5, 0.21875, ((1, 4),), jnp.float32)
    up_bias = centred(splits[20], (FF,), 0.3, 1.75, ((0, 4),), jnp.float32)
    down_weight = centred(splits[21], (FF, D), FF ** -0.5, 0.109375, ((0, 4),), jnp.float32)
    down_bias = centred(splits[22], (D,), 0.3, 1.75, (), jnp.float32)
    cotangent = centred(splits[23], (SEQS, SEQ_LEN, D), 1.0, 6.0, ((1, 8),), jnp.float32)
    return {"block_input": block_input, "lengths": lengths, "ln1_gain": ln1_gain, "ln1_bias": ln1_bias, "input_weight": input_weight, "input_bias": input_bias, "conv_w": conv_w, "conv_b": conv_b, "filt_w1": filt_w1, "filt_b1": filt_b1, "filt_w2": filt_w2, "filt_b2": filt_b2, "filt_w3": filt_w3, "decay": decay, "skip": skip, "output_weight": output_weight, "output_bias": output_bias, "ln2_gain": ln2_gain, "ln2_bias": ln2_bias, "up_weight": up_weight, "up_bias": up_bias, "down_weight": down_weight, "down_bias": down_bias, "cotangent": cotangent}


EPSILON = 1e-05
HIGH_ACCURACY = lax.Precision.HIGHEST

@jax.custom_vjp
def low(v):
    return lax.optimization_barrier(v.astype(jnp.bfloat16)).astype(jnp.float32)

@jax.custom_vjp
def low_back(v):
    return v

def low_keep(v):
    return (low(v), None)

def low_pass(kept, grad):
    return (grad,)

def back_keep(v):
    return (v, None)

def back_low(kept, grad):
    return (low(grad),)
low.defvjp(low_keep, low_pass)
low_back.defvjp(back_keep, back_low)

def layer_norm(values, gain, offset):
    average = lax.optimization_barrier(jnp.mean(values, -1, keepdims=True))
    centered = values - average
    variance = lax.optimization_barrier(jnp.mean(centered * centered, -1, keepdims=True))
    return centered * lax.rsqrt(variance + EPSILON) * gain + offset

def position_features(place_values, seq_length, emb_width):
    band_count = (emb_width - 1) // 2
    frequency = jnp.linspace(0.0001, band_count - 1, band_count).astype(place_values.dtype)
    phases = 2.0 * math.pi * place_values[:, None] * frequency[None, :] / seq_length
    return jnp.concatenate([(place_values / (seq_length - 1))[:, None], jnp.cos(phases), -jnp.sin(phases)], 1)

def implicit_filter(features, place_values, filt_w1, filt_b1, filt_w2, filt_b2, filt_w3, decay):
    first_layer = jnp.sin(jnp.dot(features, filt_w1, precision=HIGH_ACCURACY) + filt_b1)
    second_layer = jnp.sin(jnp.dot(first_layer, filt_w2, precision=HIGH_ACCURACY) + filt_b2)
    raw_kernel = jnp.dot(second_layer, filt_w3, precision=HIGH_ACCURACY)
    return raw_kernel * jnp.exp(-decay[None, :] * place_values[:, None])

def causal_conv(signal, kernel):
    length = signal.shape[1]
    spectrum = jnp.fft.rfft(signal, n=2 * length, axis=1) * jnp.fft.rfft(kernel, n=2 * length, axis=0)[None]
    return jnp.fft.irfft(spectrum, n=2 * length, axis=1)[:, :length]

def block_forward(input_rows, mask, ln1_gain, ln1_bias, input_weight, input_bias, conv_w, conv_b, filt_w1, filt_b1, filt_w2, filt_b2, filt_w3, decay, skip, output_weight, output_bias, ln2_gain, ln2_bias, up_weight, up_bias, down_weight, down_bias):
    seq_length = input_rows.shape[1]
    place_values = jnp.arange(seq_length).astype(input_rows.dtype)
    first_normed = layer_norm(input_rows, ln1_gain, ln1_bias)
    input_projected = jnp.einsum('rzt,tnu->rznu', first_normed, input_weight, precision=HIGH_ACCURACY) + input_bias
    padded = jnp.pad(input_projected, ((0, 0), (2, 0), (0, 0), (0, 0)))
    short = conv_w[0] * padded[:, :-2] + conv_w[1] * padded[:, 1:-1] + conv_w[2] * padded[:, 2:] + conv_b
    gate_out = short[:, :, 0]
    gate_in = short[:, :, 1]
    values = short[:, :, 2]
    signal = values * gate_in * mask
    features = position_features(place_values, seq_length, filt_w1.shape[0])
    kernel = implicit_filter(features, place_values, filt_w1, filt_b1, filt_w2, filt_b2, filt_w3, decay)
    mixer_output = (causal_conv(signal, kernel) + skip * signal) * gate_out
    hidden_state = input_rows + jnp.einsum('zey,yx->zex', mixer_output, output_weight, precision=HIGH_ACCURACY) + output_bias
    second_normed2 = layer_norm(hidden_state, ln2_gain, ln2_bias)
    active_units = jax.nn.gelu(jnp.einsum('wac,co->wao', second_normed2, up_weight, precision=HIGH_ACCURACY) + up_bias, approximate=False)
    return hidden_state + jnp.einsum('ziv,vm->zim', active_units, down_weight, precision=HIGH_ACCURACY) + down_bias

def reference(block_input, lengths, ln1_gain, ln1_bias, input_weight, input_bias, conv_w, conv_b, filt_w1, filt_b1, filt_w2, filt_b2, filt_w3, decay, skip, output_weight, output_bias, ln2_gain, ln2_bias, up_weight, up_bias, down_weight, down_bias, cotangent):
    mask = (jnp.arange(block_input.shape[1], dtype=jnp.int32)[None, :] < lengths[:, None]).astype(block_input.dtype)[:, :, None]

    def forward(input_rows, *weights):
        return block_forward(input_rows, mask, *weights)
    output, pull = jax.vjp(forward, block_input, ln1_gain, ln1_bias, input_weight, input_bias, conv_w, conv_b, filt_w1, filt_b1, filt_w2, filt_b2, filt_w3, decay, skip, output_weight, output_bias, ln2_gain, ln2_bias, up_weight, up_bias, down_weight, down_bias)
    grads = pull(cotangent)
    return (output, grads[0], grads[1], grads[2], grads[3], grads[4], grads[5], grads[6], grads[7], grads[8], grads[9], grads[10], grads[11], grads[12], grads[13], grads[14], grads[15], grads[16], grads[17], grads[18], grads[19], grads[20], grads[21])
```

```python
from functools import partial
import math

import jax
import jax.numpy as jnp
import ml_dtypes
import numpy as np
from jax import lax
from jax.experimental import pallas as pl
from jax.experimental.pallas import tpu as pltpu
from jax.sharding import PartitionSpec as P

EPSILON = 1e-05
HIGH_ACCURACY = lax.Precision.HIGHEST


def shifted(block, axis, distance):
    devices = range(lax.axis_size(axis))
    route = [(i - distance, i) for i in devices if i - distance in devices]
    return lax.ppermute(block, axis, route)


def layer_norm(values, gain, offset):
    average = jnp.mean(values, -1, keepdims=True)
    centered = values - average
    variance = jnp.mean(centered * centered, -1, keepdims=True)
    return centered * lax.rsqrt(variance + EPSILON) * gain + offset


def position_features(place_values, seq_length, emb_width):
    band_count = (emb_width - 1) // 2
    frequency = jnp.linspace(0.0001, band_count - 1, band_count).astype(jnp.float32)
    phases = 2.0 * math.pi * place_values[:, None] * frequency[None, :] / seq_length
    return jnp.concatenate(
        [(place_values / (seq_length - 1))[:, None], jnp.cos(phases), -jnp.sin(phases)], 1
    )


def implicit_filter(features, place_values, filt_w1, filt_b1, filt_w2, filt_b2, filt_w3, decay):
    first_layer = jnp.sin(jnp.dot(features, filt_w1, precision=HIGH_ACCURACY) + filt_b1)
    second_layer = jnp.sin(jnp.dot(first_layer, filt_w2, precision=HIGH_ACCURACY) + filt_b2)
    raw_kernel = jnp.dot(second_layer, filt_w3, precision=HIGH_ACCURACY)
    return raw_kernel * jnp.exp(-decay[None, :] * place_values[:, None])


def exact_gelu(values):
    return jax.nn.gelu(values, approximate=False)


def tables(count_rows, count_cols):
    turns = (
        jnp.arange(count_rows, dtype=jnp.int32)[:, None]
        * jnp.arange(count_cols, dtype=jnp.int32)[None, :]
        % count_rows
    )
    phases = turns.astype(jnp.float32) * (2.0 * math.pi / count_rows)
    return (jnp.cos(phases), jnp.sin(phases))


def rotate(cos_tab, sin_tab, real, imag, sign, form):
    first_part = jnp.einsum(form, cos_tab, real, precision=HIGH_ACCURACY)
    second_part = jnp.einsum(form, sin_tab, imag, precision=HIGH_ACCURACY)
    third_part = jnp.einsum(form, cos_tab, imag, precision=HIGH_ACCURACY)
    fourth_part = jnp.einsum(form, sin_tab, real, precision=HIGH_ACCURACY)
    return (first_part - sign * second_part, third_part + sign * fourth_part)


def to_spectrum(cos_tab, sin_tab, signal):
    real = jnp.einsum("wp,spc->swc", cos_tab, signal, precision=HIGH_ACCURACY)
    imag = -jnp.einsum("wp,spc->swc", sin_tab, signal, precision=HIGH_ACCURACY)
    return (real, imag)


def time_domain(cos_tab, sin_tab, real, imag):
    return jnp.einsum("wp,swc->spc", cos_tab, real, precision=HIGH_ACCURACY) - jnp.einsum(
        "wp,swc->spc", sin_tab, imag, precision=HIGH_ACCURACY
    )


def earlier_block(values):
    return jnp.pad(values, ((0, 0), (1, 0), (0, 0), (0, 0)))[:, :-1]


def later_block(values):
    return jnp.pad(values, ((0, 0), (0, 1), (0, 0), (0, 0)))[:, 1:]


def spectral_device(
    block_input,
    lengths,
    ln1_gain,
    ln1_bias,
    input_weight,
    input_bias,
    conv_w,
    conv_b,
    filt_w1,
    filt_b1,
    filt_w2,
    filt_b2,
    filt_w3,
    decay,
    skip,
    output_weight,
    output_bias,
    ln2_gain,
    ln2_bias,
    up_weight,
    up_bias,
    down_weight,
    down_bias,
    cotangent,
):
    block = block_input.shape[1]
    blocks = lax.axis_size("seq")
    share = 2 * block // blocks
    seq_index = lax.axis_index("seq")
    places = seq_index * block + jnp.arange(block, dtype=jnp.int32)
    place_values = places.astype(jnp.float32)
    mask = (places[None, :] < lengths[:, None]).astype(jnp.float32)[:, :, None]
    first_normed, norm1_pull = jax.vjp(layer_norm, block_input, ln1_gain, ln1_bias)
    input_projected = (
        jnp.einsum("spd,dkc->spkc", first_normed, input_weight, precision=HIGH_ACCURACY)
        + input_bias
    )
    rims = shifted(input_projected[:, block - 2 :], "seq", 1)
    extended = jnp.concatenate([rims, input_projected], 1)
    short = (
        conv_w[0] * extended[:, :block]
        + conv_w[1] * extended[:, 1 : block + 1]
        + conv_w[2] * extended[:, 2:]
        + conv_b
    )
    gate_out = short[:, :, 0]
    gate_in = short[:, :, 1]
    values = short[:, :, 2]
    signal = values * gate_in * mask
    cos_tab, sin_tab = tables(2 * block, block)
    block_cos, block_sin = tables(2 * blocks, blocks)
    own_freq = seq_index * share + jnp.arange(share, dtype=jnp.int32)
    parity = (1 - 2 * (own_freq % 2)).astype(jnp.float32)[:, None]
    features = position_features(place_values, blocks * block, filt_w1.shape[0])
    kernel, filter_pull = jax.vjp(
        partial(implicit_filter, features, place_values),
        filt_w1,
        filt_b1,
        filt_w2,
        filt_b2,
        filt_w3,
        decay,
    )
    signal_re, signal_im = to_spectrum(cos_tab, sin_tab, signal)
    kernel_re, kernel_im = to_spectrum(cos_tab, sin_tab, kernel[None])
    signal_re, signal_im, kernel_re, kernel_im = (
        lax.all_to_all(signal_re[:, None], "seq", split_axis=2, concat_axis=1, tiled=True),
        lax.all_to_all(signal_im[:, None], "seq", split_axis=2, concat_axis=1, tiled=True),
        lax.all_to_all(kernel_re[:, None], "seq", split_axis=2, concat_axis=1, tiled=True),
        lax.all_to_all(kernel_im[:, None], "seq", split_axis=2, concat_axis=1, tiled=True),
    )
    zq_re, zq_im = rotate(block_cos, block_sin, signal_re, signal_im, -1.0, "qk,skfc->sqfc")
    hq_re, hq_im = rotate(block_cos, block_sin, kernel_re, kernel_im, -1.0, "qk,skfc->sqfc")
    prod_re = zq_re * hq_re - zq_im * hq_im
    prod_im = zq_re * hq_im + zq_im * hq_re
    joined_re, joined_im = rotate(block_cos, block_sin, prod_re, prod_im, 1.0, "qj,sqfc->sjfc")
    joined_re = joined_re / (2 * blocks)
    joined_im = joined_im / (2 * blocks)
    folded_re = joined_re + parity * earlier_block(joined_re)
    folded_im = joined_im + parity * earlier_block(joined_im)
    folded_re, folded_im = (
        lax.all_to_all(folded_re, "seq", split_axis=1, concat_axis=2, tiled=True),
        lax.all_to_all(folded_im, "seq", split_axis=1, concat_axis=2, tiled=True),
    )
    convolved = time_domain(cos_tab, sin_tab, folded_re[:, 0], folded_im[:, 0]) / (2 * block)
    conv_sum = convolved + skip * signal
    mixer_output = conv_sum * gate_out
    partial_mix = jnp.einsum("spc,cd->spd", mixer_output, output_weight, precision=HIGH_ACCURACY)
    hidden_state = block_input + lax.psum(partial_mix, "chan") + output_bias
    second_normed2 = layer_norm(hidden_state, ln2_gain, ln2_bias)
    before = jnp.einsum("spd,df->spf", second_normed2, up_weight, precision=HIGH_ACCURACY) + up_bias
    active_units, gelu_pull = jax.vjp(exact_gelu, before)
    feed = lax.psum(
        jnp.einsum("spf,fd->spd", active_units, down_weight, precision=HIGH_ACCURACY), "chan"
    )
    output = hidden_state + feed + down_bias
    grad_b_fc2 = jnp.sum(cotangent, (0, 1))
    grad_w_fc2 = jnp.einsum("spf,spd->fd", active_units, cotangent, precision=HIGH_ACCURACY)
    grad_active = jnp.einsum("spd,fd->spf", cotangent, down_weight, precision=HIGH_ACCURACY)
    grad_before = gelu_pull(grad_active)[0]
    grad_w_fc1 = jnp.einsum("spd,spf->df", second_normed2, grad_before, precision=HIGH_ACCURACY)
    grad_b_fc1 = jnp.sum(grad_before, (0, 1))
    grad_normed2 = lax.psum(
        jnp.einsum("spf,df->spd", grad_before, up_weight, precision=HIGH_ACCURACY), "chan"
    )
    norm2_pull = jax.vjp(layer_norm, hidden_state, ln2_gain, ln2_bias)[1]
    grad_hidden_norm, grad_ln2_gain, grad_ln2_bias = norm2_pull(grad_normed2)
    grad_hidden = cotangent + grad_hidden_norm
    grad_b_out = jnp.sum(grad_hidden, (0, 1))
    grad_w_out = jnp.einsum("spc,spd->cd", mixer_output, grad_hidden, precision=HIGH_ACCURACY)
    grad_mixed = jnp.einsum("spd,cd->spc", grad_hidden, output_weight, precision=HIGH_ACCURACY)
    grad_conv = grad_mixed * gate_out
    grad_gate_out = grad_mixed * conv_sum
    grad_skip = jnp.sum(grad_conv * signal, (0, 1))
    back_re, back_im = to_spectrum(cos_tab, sin_tab, grad_conv)
    back_re = back_re / (2 * block)
    back_im = back_im / (2 * block)
    back_re, back_im = (
        lax.all_to_all(back_re[:, None], "seq", split_axis=2, concat_axis=1, tiled=True),
        lax.all_to_all(back_im[:, None], "seq", split_axis=2, concat_axis=1, tiled=True),
    )
    unfold_re = back_re + parity * later_block(back_re)
    unfold_im = back_im + parity * later_block(back_im)
    dprod_re, dprod_im = rotate(block_cos, block_sin, unfold_re, unfold_im, -1.0, "qj,sjfc->sqfc")
    dprod_re = dprod_re / (2 * blocks)
    dprod_im = dprod_im / (2 * blocks)
    dzq_re = hq_re * dprod_re + hq_im * dprod_im
    dzq_im = hq_re * dprod_im - hq_im * dprod_re
    dhq_re = jnp.sum(zq_re * dprod_re + zq_im * dprod_im, 0, keepdims=True)
    dhq_im = jnp.sum(zq_re * dprod_im - zq_im * dprod_re, 0, keepdims=True)
    dsig_re, dsig_im = rotate(block_cos, block_sin, dzq_re, dzq_im, 1.0, "qk,sqfc->skfc")
    dker_re, dker_im = rotate(block_cos, block_sin, dhq_re, dhq_im, 1.0, "qk,sqfc->skfc")
    dsig_re, dsig_im, dker_re, dker_im = (
        lax.all_to_all(dsig_re, "seq", split_axis=1, concat_axis=2, tiled=True),
        lax.all_to_all(dsig_im, "seq", split_axis=1, concat_axis=2, tiled=True),
        lax.all_to_all(dker_re, "seq", split_axis=1, concat_axis=2, tiled=True),
        lax.all_to_all(dker_im, "seq", split_axis=1, concat_axis=2, tiled=True),
    )
    grad_signal = time_domain(cos_tab, sin_tab, dsig_re[:, 0], dsig_im[:, 0]) + grad_conv * skip
    grad_kernel = time_domain(cos_tab, sin_tab, dker_re[:, 0], dker_im[:, 0])[0]
    grad_fw1, grad_fb1, grad_fw2, grad_fb2, grad_fw3, grad_decay = filter_pull(grad_kernel)
    grad_short = jnp.stack(
        [grad_gate_out, grad_signal * values * mask, grad_signal * gate_in * mask], 2
    )
    grad_conv_b = jnp.sum(grad_short, (0, 1))
    grad_conv_w = jnp.stack(
        [jnp.sum(grad_short * extended[:, offset : offset + block], (0, 1)) for offset in range(3)]
    )
    grad_extended = (
        jnp.pad(conv_w[0] * grad_short, ((0, 0), (0, 2), (0, 0), (0, 0)))
        + jnp.pad(conv_w[1] * grad_short, ((0, 0), (1, 1), (0, 0), (0, 0)))
        + jnp.pad(conv_w[2] * grad_short, ((0, 0), (2, 0), (0, 0), (0, 0)))
    )
    returned = shifted(grad_extended[:, :2], "seq", -1)
    grad_proj = grad_extended[:, 2:] + jnp.pad(returned, ((0, 0), (block - 2, 0), (0, 0), (0, 0)))
    grad_b_in = jnp.sum(grad_proj, (0, 1))
    grad_w_in = jnp.einsum("spd,spkc->dkc", first_normed, grad_proj, precision=HIGH_ACCURACY)
    grad_normed = lax.psum(
        jnp.einsum("spkc,dkc->spd", grad_proj, input_weight, precision=HIGH_ACCURACY), "chan"
    )
    grad_x_norm, grad_ln1_gain, grad_ln1_bias = norm1_pull(grad_normed)
    grad_x = grad_hidden + grad_x_norm
    (
        grad_ln1_gain,
        grad_ln1_bias,
        grad_w_in,
        grad_b_in,
        grad_conv_w,
        grad_conv_b,
        grad_fw3,
        grad_decay,
        grad_skip,
        grad_w_out,
        grad_b_out,
        grad_ln2_gain,
        grad_ln2_bias,
        grad_w_fc1,
        grad_b_fc1,
        grad_w_fc2,
        grad_b_fc2,
    ) = lax.psum(
        (
            grad_ln1_gain,
            grad_ln1_bias,
            grad_w_in,
            grad_b_in,
            grad_conv_w,
            grad_conv_b,
            grad_fw3,
            grad_decay,
            grad_skip,
            grad_w_out,
            grad_b_out,
            grad_ln2_gain,
            grad_ln2_bias,
            grad_w_fc1,
            grad_b_fc1,
            grad_w_fc2,
            grad_b_fc2,
        ),
        "seq",
    )
    grad_fw1, grad_fb1, grad_fw2, grad_fb2 = lax.psum(
        (grad_fw1, grad_fb1, grad_fw2, grad_fb2), ("seq", "chan")
    )
    return (
        output,
        grad_x,
        grad_ln1_gain,
        grad_ln1_bias,
        grad_w_in,
        grad_b_in,
        grad_conv_w,
        grad_conv_b,
        grad_fw1,
        grad_fb1,
        grad_fw2,
        grad_fb2,
        grad_fw3,
        grad_decay,
        grad_skip,
        grad_w_out,
        grad_b_out,
        grad_ln2_gain,
        grad_ln2_bias,
        grad_w_fc1,
        grad_b_fc1,
        grad_w_fc2,
        grad_b_fc2,
    )


F32 = jnp.float32
BF16 = jnp.bfloat16
NN = (((1,), (0,)), ((), ()))
NT = (((1,), (1,)), ((), ()))
TN = (((0,), (0,)), ((), ()))
VMEM_BYTES = 56 * 2**20


def parts_of(values):
    high = values.astype(BF16)
    return high, (values - high.astype(F32)).astype(BF16)


def dot_parts(left, right, dims):
    def one(a, b):
        return lax.dot_general(a, b, dims, preferred_element_type=F32)

    return one(left[0], right[0]) + (one(left[0], right[1]) + one(left[1], right[0]))


def normalise(values):
    average = jnp.mean(values, -1, keepdims=True)
    centered = values - average
    variance = jnp.mean(centered * centered, -1, keepdims=True)
    scale = lax.rsqrt(variance + EPSILON)
    return centered * scale, scale


def norm_back(unit, scale, gain, grad):
    lifted = grad * gain
    mean_one = jnp.mean(lifted, -1, keepdims=True)
    mean_two = jnp.mean(lifted * unit, -1, keepdims=True)
    return scale * (lifted - mean_one - unit * mean_two)


def column_sum(values):
    return jnp.sum(values, 0, keepdims=True)


def whole(array):
    return pl.BlockSpec(array.shape, lambda *_: (0,) * len(array.shape))


def scalar_spec():
    return pl.BlockSpec(memory_space=pltpu.SMEM)


def struct(shape, kind=F32):
    return jax.ShapeDtypeStruct(tuple(shape), kind)


def run_kernel(body, name, grid, in_specs, out_specs, out_shape, scratch, args, flops):
    moved = sum(math.prod(a.shape) * a.dtype.itemsize for a in args)
    moved += sum(math.prod(a.shape) * a.dtype.itemsize for a in out_shape)
    return pl.pallas_call(
        body,
        name=name,
        grid=grid,
        in_specs=in_specs,
        out_specs=out_specs,
        out_shape=out_shape,
        scratch_shapes=scratch,
        compiler_params=pltpu.CompilerParams(
            dimension_semantics=("arbitrary",) * len(grid), vmem_limit_bytes=VMEM_BYTES
        ),
        cost_estimate=pl.CostEstimate(flops=int(flops), bytes_accessed=int(moved), transcendentals=0),
    )(*args)


def wave_tables(block):
    angles = np.pi * np.outer(2 * np.arange(block) + 1, np.arange(block)) / (2 * block)
    table = np.concatenate([np.cos(angles), -np.sin(angles)], 0)

    def both(values):
        high = values.astype(ml_dtypes.bfloat16)
        low = (values - high.astype(np.float64)).astype(ml_dtypes.bfloat16)
        return jnp.asarray(high), jnp.asarray(low)

    return both(table) + both(table.T / block)


def parity_of(rows):
    odd = lax.broadcasted_iota(jnp.int32, (rows, 1), 0) % 2
    return (1 - 2 * odd).astype(F32)


def filter_spectrum(kernel, tables):
    blocks, block, width = kernel.shape
    table_high, table_low = tables[:2]

    def body(kernel_ref, high_ref, low_ref, out_ref, before_ref):
        @pl.when(pl.program_id(0) == 0)
        def _():
            before_ref[...] = jnp.zeros_like(before_ref)

        spectrum = dot_parts((high_ref[...], low_ref[...]), parts_of(kernel_ref[0]), NN)
        sign = parity_of(block)
        out_ref[0, :block] = spectrum[:block] - sign * before_ref[block:]
        out_ref[0, block:] = spectrum[block:] + sign * before_ref[:block]
        before_ref[...] = spectrum

    return run_kernel(
        body,
        "filter_spectrum",
        (blocks,),
        [pl.BlockSpec((1, block, width), lambda b: (b, 0, 0)), whole(table_high), whole(table_low)],
        [pl.BlockSpec((1, 2 * block, width), lambda b: (b, 0, 0))],
        [struct((blocks, 2 * block, width))],
        [pltpu.VMEM((2 * block, width), F32)],
        [kernel, table_high, table_low],
        12 * blocks * block * block * width,
    )[0]


def mixer_forward(own, length, x_parts, gain, offset, weight, bias, conv_w, conv_b, skip, spectrum, tables):
    blocks, quarter, model = x_parts[0].shape
    count = len(x_parts)
    block = quarter * count
    width = weight.shape[2]
    tile = min(32, block)

    def body(*refs):
        own_ref, length_ref = refs[:2]
        x_refs = refs[2 : 2 + count]
        refs = refs[2 + count :]
        gain_ref, offset_ref, weight_ref, bias_ref, conv_w_ref, conv_b_ref, skip_ref, k_ref = refs[:8]
        th_ref, tl_ref, ih_ref, il_ref = refs[8:12]
        nh_ref, nl_ref, proj_ref, conv_ref, s_ref = refs[12:17]
        m_refs = refs[17 : 17 + count]
        wh_ref, wl_ref, ext_ref, o_ref, mixed_ref = refs[17 + count :]
        b = pl.program_id(0)
        me = own_ref[0]

        @pl.when(b == 0)
        def _():
            for k in range(3):
                wh_ref[k], wl_ref[k] = parts_of(weight_ref[k])
            ext_ref[:, :8] = jnp.zeros((3, 8, width), F32)

        for k in range(count):
            normed = normalise(x_refs[k][0])[0] * gain_ref[...] + offset_ref[...]
            start = pl.multiple_of((me ^ k) * quarter, quarter)
            high, low = parts_of(normed)
            nh_ref[0, pl.ds(start, quarter), :] = high
            nl_ref[0, pl.ds(start, quarter), :] = low
        normed = (nh_ref[0], nl_ref[0])
        short = []
        for k in range(3):
            proj = dot_parts(normed, (wh_ref[k], wl_ref[k]), NN) + bias_ref[k : k + 1, :]
            proj_ref[0, k] = proj
            ext_ref[k, 8 : 8 + block] = proj
            short.append(
                conv_w_ref[0, k : k + 1, :] * ext_ref[k, 6 : 6 + block]
                + conv_w_ref[1, k : k + 1, :] * ext_ref[k, 7 : 7 + block]
                + conv_w_ref[2, k : k + 1, :] * proj
                + conv_b_ref[k : k + 1, :]
            )
            ext_ref[k, :8] = ext_ref[k, block : block + 8]
        places = b * block + lax.broadcasted_iota(jnp.int32, (block, 1), 0)
        mask = (places < length_ref[0]).astype(F32)
        signal = short[2] * short[1] * mask
        s_ref[b] = dot_parts((th_ref[...], tl_ref[...]), parts_of(signal), NN)
        for r in range(0, block, tile):
            lo = slice(r, r + tile)
            hi = slice(block + r, block + r + tile)

            def product(i, total, lo=lo, hi=hi):
                s_re, s_im = s_ref[i, lo], s_ref[i, hi]
                k_re, k_im = k_ref[b - i, lo], k_ref[b - i, hi]
                return total[0] + s_re * k_re - s_im * k_im, total[1] + s_re * k_im + s_im * k_re

            zero = jnp.zeros((tile, width), F32)
            o_ref[lo], o_ref[hi] = lax.fori_loop(0, b + 1, product, (zero, zero))
        conv = dot_parts((ih_ref[...], il_ref[...]), parts_of(o_ref[...]), NN) + skip_ref[...] * signal
        conv_ref[0] = conv
        mixed_ref[...] = conv * short[0]
        for k in range(count):
            start = pl.multiple_of((me ^ k) * quarter, quarter)
            m_refs[k][0] = mixed_ref[pl.ds(start, quarter), :]

    by_block = lambda *shape: pl.BlockSpec((1,) + shape, lambda b: (b,) + (0,) * len(shape))
    args = [own, length, *x_parts, gain, offset, weight, bias, conv_w, conv_b, skip, spectrum, *tables]
    in_specs = [scalar_spec(), scalar_spec()] + [by_block(quarter, model)] * count
    in_specs += [whole(a) for a in args[2 + count :]]
    s_shape = struct((blocks, 2 * block, width))
    outs = run_kernel(
        body,
        "mixer_forward",
        (blocks,),
        in_specs,
        [by_block(block, model)] * 2
        + [by_block(3, block, width), by_block(block, width), whole(s_shape)]
        + [by_block(quarter, width)] * count,
        [struct((blocks, block, model), BF16)] * 2
        + [struct((blocks, 3, block, width)), struct((blocks, block, width)), s_shape]
        + [struct((blocks, quarter, width))] * count,
        [
            pltpu.VMEM((3, model, width), BF16),
            pltpu.VMEM((3, model, width), BF16),
            pltpu.VMEM((3, block + 8, width), F32),
            pltpu.VMEM((2 * block, width), F32),
            pltpu.VMEM((block, width), F32),
        ],
        args,
        6 * blocks * block * width * (3 * model + 4 * block),
    )
    return outs[:5], outs[5:]


def hidden_forward(m_parts, weights, x_own, cotangent, bias, gain, offset):
    rows, width = m_parts[0].shape
    model = x_own.shape[1]
    count = len(m_parts)
    step = min(128, rows)

    def body(*refs):
        m_refs, w_refs = refs[:count], refs[count : 2 * count]
        x_ref, c_ref, bias_ref, gain_ref, offset_ref = refs[2 * count : 2 * count + 5]
        h_ref, nh_ref, nl_ref, th_ref, tl_ref, ch_ref, cl_ref = refs[2 * count + 5 : 2 * count + 12]
        wh_ref, wl_ref = refs[2 * count + 12 :]

        @pl.when(pl.program_id(0) == 0)
        def _():
            for k in range(count):
                wh_ref[k], wl_ref[k] = parts_of(w_refs[k][...])

        hidden = x_ref[...] + bias_ref[...]
        for k in range(count):
            hidden = hidden + dot_parts(parts_of(m_refs[k][...]), (wh_ref[k], wl_ref[k]), NN)
        h_ref[...] = hidden
        normed = normalise(hidden)[0] * gain_ref[...] + offset_ref[...]
        nh_ref[...], nl_ref[...] = parts_of(normed)
        th_ref[...], tl_ref[...] = parts_of(normed.T)
        ch_ref[...], cl_ref[...] = parts_of(c_ref[...])

    row_spec = lambda n: pl.BlockSpec((step, n), lambda r: (r, 0))
    turned = pl.BlockSpec((model, step), lambda r: (0, r))
    args = [*m_parts, *weights, x_own, cotangent, bias, gain, offset]
    return run_kernel(
        body,
        "hidden_forward",
        (rows // step,),
        [row_spec(width)] * count
        + [whole(w) for w in weights]
        + [row_spec(model)] * 2
        + [whole(bias), whole(gain), whole(offset)],
        [row_spec(model)] * 3 + [turned] * 2 + [row_spec(model)] * 2,
        [struct((rows, model))]
        + [struct((rows, model), BF16)] * 2
        + [struct((model, rows), BF16)] * 2
        + [struct((rows, model), BF16)] * 2,
        [pltpu.VMEM((count, width, model), BF16)] * 2,
        args,
        6 * rows * model * width * count,
    )


def feed_forward(normed, turned, cotangent, up, up_bias, down, sums):
    rows, model = normed[0].shape
    units = up.shape[1]
    step = min(256, units)
    first = sums is None

    def body(*refs):
        nh_ref, nl_ref, th_ref, tl_ref, ch_ref, cl_ref, up_ref, bias_ref, down_ref = refs[:9]
        feed_in, grad_in = (None, None) if first else refs[9:11]
        feed_ref, grad_ref, gup_ref, gdown_ref, gbias_ref = refs[9 if first else 11 :]

        @pl.when(pl.program_id(0) == 0)
        def _():
            if first:
                feed_ref[...] = jnp.zeros_like(feed_ref)
                grad_ref[...] = jnp.zeros_like(grad_ref)
            else:
                feed_ref[...] = feed_in[...]
                grad_ref[...] = grad_in[...]

        own_normed = (nh_ref[...], nl_ref[...])
        own_cotangent = (ch_ref[...], cl_ref[...])
        up_parts = parts_of(up_ref[...])
        down_parts = parts_of(down_ref[...])
        before = dot_parts(own_normed, up_parts, NN) + bias_ref[...]
        grad_active = dot_parts(own_cotangent, down_parts, NT)
        below = 0.5 + 0.5 * lax.erf(before * math.sqrt(0.5))
        slope = below + before * (jnp.exp(-0.5 * before * before) * (1.0 / math.sqrt(2.0 * math.pi)))
        active = before * below
        grad_before = grad_active * slope
        gbias_ref[...] = column_sum(grad_before)
        active_parts = parts_of(active)
        grad_parts = parts_of(grad_before)
        feed_ref[...] += dot_parts(active_parts, down_parts, NN)
        grad_ref[...] += dot_parts(grad_parts, up_parts, NT)
        gup_ref[...] = dot_parts((th_ref[...], tl_ref[...]), grad_parts, NN)
        gdown_ref[...] = dot_parts(active_parts, own_cotangent, TN)

    total = struct((rows, model))
    args = [*normed, *turned, *cotangent, up, up_bias, down] + ([] if first else list(sums))
    columns = pl.BlockSpec((model, step), lambda t: (0, t))
    one_row = pl.BlockSpec((1, step), lambda t: (0, t))
    some_rows = pl.BlockSpec((step, model), lambda t: (t, 0))
    outs = run_kernel(
        body,
        "feed_forward",
        (units // step,),
        [whole(a) for a in args[:6]] + [columns, one_row, some_rows] + [whole(a) for a in args[9:]],
        [whole(total), whole(total), columns, some_rows, one_row],
        [total, total, struct(up.shape), struct(down.shape), struct(up_bias.shape)],
        [],
        args,
        36 * rows * model * units,
    )
    return outs[:2], outs[2:]


def hidden_backward(hidden, feed, grad_normed, cotangent, m_parts, weights, gain, bias):
    rows, model = hidden.shape
    width = m_parts[0].shape[1]
    count = len(m_parts)
    step = min(128, rows)

    def body(*refs):
        h_ref, f_ref, g_ref, c_ref = refs[:4]
        m_refs, w_refs = refs[4 : 4 + count], refs[4 + count : 4 + 2 * count]
        gain_ref, bias_ref, out_ref, gh_ref, sum_ref = refs[4 + 2 * count : 9 + 2 * count]
        gm_refs = refs[9 + 2 * count : 9 + 3 * count]
        gw_refs = refs[9 + 3 * count : 9 + 4 * count]
        wh_ref, wl_ref = refs[9 + 4 * count :]

        @pl.when(pl.program_id(0) == 0)
        def _():
            sum_ref[...] = jnp.zeros_like(sum_ref)
            for k in range(count):
                wh_ref[k], wl_ref[k] = parts_of(w_refs[k][...])
                gw_refs[k][...] = jnp.zeros_like(gw_refs[k])

        hidden_rows, grad, above = h_ref[...], g_ref[...], c_ref[...]
        out_ref[...] = hidden_rows + f_ref[...] + bias_ref[...]
        unit, scale = normalise(hidden_rows)
        grad_hidden = above + norm_back(unit, scale, gain_ref[...], grad)
        gh_ref[...] = grad_hidden
        sum_ref[0:1] += column_sum(grad * unit)
        sum_ref[1:2] += column_sum(grad)
        sum_ref[2:3] += column_sum(grad_hidden)
        sum_ref[3:4] += column_sum(above)
        parts = parts_of(grad_hidden)
        for k in range(count):
            gm_refs[k][...] = dot_parts(parts, (wh_ref[k], wl_ref[k]), NT)
            gw_refs[k][...] += dot_parts(parts_of(m_refs[k][...]), parts, TN)

    row_spec = lambda n: pl.BlockSpec((step, n), lambda r: (r, 0))
    args = [hidden, feed, grad_normed, cotangent, *m_parts, *weights, gain, bias]
    sums = struct((8, model))
    outs = run_kernel(
        body,
        "hidden_backward",
        (rows // step,),
        [row_spec(model)] * 4 + [row_spec(width)] * count + [whole(w) for w in weights] + [whole(gain), whole(bias)],
        [row_spec(model)] * 2 + [whole(sums)] + [row_spec(width)] * count + [whole(w) for w in weights],
        [struct((rows, model))] * 2
        + [sums]
        + [struct((rows, width))] * count
        + [struct(w.shape) for w in weights],
        [pltpu.VMEM((count, width, model), BF16)] * 2,
        args,
        12 * rows * model * width * count,
    )
    return outs[:3], outs[3 : 3 + count], outs[3 + count :]


def mixer_backward(own, length, gm_parts, proj, conv, s_spec, k_spec, conv_w, conv_b, skip, weight, tables):
    blocks, quarter, width = gm_parts[0].shape
    count = len(gm_parts)
    block = quarter * count
    model = weight.shape[1]
    tile = min(32, block)

    def body(*refs):
        own_ref, length_ref = refs[:2]
        gm_refs = refs[2 : 2 + count]
        refs = refs[2 + count :]
        proj_ref, rim_ref, conv_ref, k_ref, conv_w_ref, conv_b_ref, skip_ref, weight_ref = refs[:8]
        th_ref, tl_ref, ih_ref, il_ref = refs[8:12]
        g_ref, gp_ref, sum_ref = refs[12:15]
        gn_refs = refs[15 : 15 + count]
        wh_ref, wl_ref, ext_ref, gs_ref, o_ref, rows_ref, gn_ref = refs[15 + count :]
        step = pl.program_id(0)
        b = blocks - 1 - step
        me = own_ref[0]

        @pl.when(step == 0)
        def _():
            for k in range(3):
                wh_ref[k], wl_ref[k] = parts_of(weight_ref[k])
            gs_ref[:, block:] = jnp.zeros((3, 8, width), F32)
            sum_ref[...] = jnp.zeros_like(sum_ref)

        for k in range(count):
            start = pl.multiple_of((me ^ k) * quarter, quarter)
            rows_ref[pl.ds(start, quarter), :] = gm_refs[k][0]
        inside = (b > 0).astype(F32)
        short = []
        for k in range(3):
            ext_ref[k, :8] = rim_ref[0, k] * inside
            ext_ref[k, 8:] = proj_ref[0, k]
            short.append(
                conv_w_ref[0, k : k + 1, :] * ext_ref[k, 6 : 6 + block]
                + conv_w_ref[1, k : k + 1, :] * ext_ref[k, 7 : 7 + block]
                + conv_w_ref[2, k : k + 1, :] * proj_ref[0, k]
                + conv_b_ref[k : k + 1, :]
            )
        places = b * block + lax.broadcasted_iota(jnp.int32, (block, 1), 0)
        mask = (places < length_ref[0]).astype(F32)
        gate_in, values = short[1] * mask, short[2] * mask
        grad_mixed = rows_ref[...]
        grad_conv = grad_mixed * short[0]
        gs_ref[0, :block] = grad_mixed * conv_ref[0]
        g_ref[b] = dot_parts((th_ref[...], tl_ref[...]), parts_of(grad_conv), NN)
        for r in range(0, block, tile):
            lo = slice(r, r + tile)
            hi = slice(block + r, block + r + tile)

            def product(j, total, lo=lo, hi=hi):
                g_re, g_im = g_ref[j, lo], g_ref[j, hi]
                k_re, k_im = k_ref[j - b, lo], k_ref[j - b, hi]
                return total[0] + g_re * k_re + g_im * k_im, total[1] + g_im * k_re - g_re * k_im

            zero = jnp.zeros((tile, width), F32)
            o_ref[lo], o_ref[hi] = lax.fori_loop(b, blocks, product, (zero, zero))
        grad_signal = dot_parts((ih_ref[...], il_ref[...]), parts_of(o_ref[...]), NN)
        grad_signal = grad_signal + skip_ref[...] * grad_conv
        gs_ref[1, :block] = grad_signal * values
        gs_ref[2, :block] = grad_signal * gate_in
        sum_ref[0:1] += column_sum(grad_conv * short[2] * gate_in)
        normed_grad = jnp.zeros((block, model), F32)
        for k in range(3):
            grad_short = gs_ref[k, :block]
            sum_ref[1 + k : 2 + k] += column_sum(grad_short)
            for t in range(3):
                row = 4 + 3 * t + k
                sum_ref[row : row + 1] += column_sum(grad_short * ext_ref[k, 6 + t : 6 + t + block])
            grad_proj = (
                conv_w_ref[2, k : k + 1, :] * grad_short
                + conv_w_ref[1, k : k + 1, :] * gs_ref[k, 1 : 1 + block]
                + conv_w_ref[0, k : k + 1, :] * gs_ref[k, 2 : 2 + block]
            )
            sum_ref[13 + k : 14 + k] += column_sum(grad_proj)
            gp_ref[0, k] = grad_proj
            normed_grad = normed_grad + dot_parts(parts_of(grad_proj), (wh_ref[k], wl_ref[k]), NT)
            gs_ref[k, block:] = gs_ref[k, :8]
        gn_ref[...] = normed_grad
        for k in range(count):
            start = pl.multiple_of((me ^ k) * quarter, quarter)
            gn_refs[k][0] = gn_ref[pl.ds(start, quarter), :]

    last = blocks - 1
    by_block = lambda *shape: pl.BlockSpec((1,) + shape, lambda s: (last - s,) + (0,) * len(shape))
    rim = pl.BlockSpec((1, 3, 8, width), lambda s: (jnp.maximum(last - s - 1, 0), 0, block // 8 - 1, 0))
    fixed = [k_spec, conv_w, conv_b, skip, weight, *tables]
    spectra = struct((blocks, 2 * block, width))
    sums = struct((16, width))
    outs = run_kernel(
        body,
        "mixer_backward",
        (blocks,),
        [scalar_spec(), scalar_spec()]
        + [by_block(quarter, width)] * count
        + [by_block(3, block, width), rim, by_block(block, width)]
        + [whole(a) for a in fixed],
        [whole(spectra), by_block(3, block, width), whole(sums)] + [by_block(quarter, model)] * count,
        [spectra, struct((blocks, 3, block, width)), sums] + [struct((blocks, quarter, model))] * count,
        [
            pltpu.VMEM((3, model, width), BF16),
            pltpu.VMEM((3, model, width), BF16),
            pltpu.VMEM((3, block + 8, width), F32),
            pltpu.VMEM((3, block + 8, width), F32),
            pltpu.VMEM((2 * block, width), F32),
            pltpu.VMEM((block, width), F32),
            pltpu.VMEM((block, model), F32),
        ],
        [own, length, *gm_parts, proj, proj, conv, *fixed],
        6 * blocks * block * width * (3 * model + 4 * block),
    )
    return outs[:3], outs[3:]


def filter_backward(s_spec, g_spec, tables):
    blocks, double, width = s_spec.shape
    block = double // 2
    tile = min(32, block)
    inverse = tables[2:]

    def body(s_ref, g_ref, ih_ref, il_ref, out_ref, after_ref, o_ref):
        m = blocks - 1 - pl.program_id(0)

        @pl.when(m == blocks - 1)
        def _():
            after_ref[...] = jnp.zeros_like(after_ref)

        sign = parity_of(tile)
        for r in range(0, block, tile):
            lo = slice(r, r + tile)
            hi = slice(block + r, block + r + tile)

            def product(j, total, lo=lo, hi=hi):
                g_re, g_im = g_ref[j, lo], g_ref[j, hi]
                s_re, s_im = s_ref[j - m, lo], s_ref[j - m, hi]
                return total[0] + g_re * s_re + g_im * s_im, total[1] + g_im * s_re - g_re * s_im

            zero = jnp.zeros((tile, width), F32)
            re, im = lax.fori_loop(m, blocks, product, (zero, zero))
            o_ref[lo] = re + sign * after_ref[hi]
            o_ref[hi] = im - sign * after_ref[lo]
            after_ref[lo], after_ref[hi] = re, im
        out_ref[0] = dot_parts((ih_ref[...], il_ref[...]), parts_of(o_ref[...]), NN)

    return run_kernel(
        body,
        "filter_backward",
        (blocks,),
        [whole(s_spec), whole(g_spec), whole(inverse[0]), whole(inverse[1])],
        [pl.BlockSpec((1, block, width), lambda s: (blocks - 1 - s, 0, 0))],
        [struct((blocks, block, width))],
        [pltpu.VMEM((double, width), F32)] * 2,
        [s_spec, g_spec, *inverse],
        12 * blocks * block * block * width,
    )[0]


def input_weight_grad(normed_high, normed_low, grad_proj):
    blocks, block, model = normed_high.shape
    width = grad_proj.shape[3]

    def body(nh_ref, nl_ref, gp_ref, out_ref):
        @pl.when(pl.program_id(0) == 0)
        def _():
            out_ref[...] = jnp.zeros_like(out_ref)

        normed = (nh_ref[0], nl_ref[0])
        for k in range(3):
            out_ref[k] += dot_parts(normed, parts_of(gp_ref[0, k]), TN)

    by_block = lambda *shape: pl.BlockSpec((1,) + shape, lambda b: (b,) + (0,) * len(shape))
    out = struct((3, model, width))
    return run_kernel(
        body,
        "input_weight_grad",
        (blocks,),
        [by_block(block, model)] * 2 + [by_block(3, block, width)],
        [whole(out)],
        [out],
        [],
        [normed_high, normed_low, grad_proj],
        18 * blocks * block * model * width,
    )[0]


def input_backward(grad_pieces, x_own, grad_hidden, gain):
    rows, model = x_own.shape
    count = len(grad_pieces)
    step = min(128, rows)

    def body(*refs):
        piece_refs = refs[:count]
        x_ref, gh_ref, gain_ref, out_ref, sum_ref = refs[count:]

        @pl.when(pl.program_id(0) == 0)
        def _():
            sum_ref[...] = jnp.zeros_like(sum_ref)

        grad = sum(r[...] for r in piece_refs)
        unit, scale = normalise(x_ref[...])
        out_ref[...] = gh_ref[...] + norm_back(unit, scale, gain_ref[...], grad)
        sum_ref[0:1] += column_sum(grad * unit)
        sum_ref[1:2] += column_sum(grad)

    row_spec = pl.BlockSpec((step, model), lambda r: (r, 0))
    sums = struct((8, model))
    return run_kernel(
        body,
        "input_backward",
        (rows // step,),
        [row_spec] * (count + 2) + [whole(gain)],
        [row_spec, whole(sums)],
        [struct((rows, model)), sums],
        [],
        [*grad_pieces, x_own, grad_hidden, gain],
        20 * rows * model,
    )


def put_together(own, pieces):
    groups, quarter, model = pieces[0].shape
    count = len(pieces)

    def body(own_ref, *refs):
        for k in range(count):
            start = pl.multiple_of((own_ref[0] ^ k) * quarter, quarter)
            refs[count][0, pl.ds(start, quarter), :] = refs[k][0]

    by_group = lambda n: pl.BlockSpec((1, n, model), lambda s: (s, 0, 0))
    return run_kernel(
        body,
        "put_together",
        (groups,),
        [scalar_spec()] + [by_group(quarter)] * count,
        [by_group(quarter * count)],
        [struct((groups, quarter * count, model))],
        [],
        [own, *pieces],
        0,
    )[0]


def swap(values, axis, bit):
    size = lax.axis_size(axis)
    return lax.ppermute(values, axis, [(i, i ^ bit) for i in range(size)])


def total_over(values, axis):
    bit = 1
    while bit < lax.axis_size(axis):
        values = values + swap(values, axis, bit)
        bit *= 2
    return values


def transpose_blocks(values):
    return lax.all_to_all(values, "seq", split_axis=0, concat_axis=0, tiled=True)


def spread(values):
    far = swap(values, "chan", 2)
    return [values, swap(values, "chan", 1), far, swap(far, "chan", 1)]


def collect(pieces):
    far = pieces[2] + swap(pieces[3], "chan", 1)
    return [pieces[0], swap(pieces[1], "chan", 1), swap(far, "chan", 2)]


def pack(arrays):
    flat = jnp.concatenate([a.reshape(-1) for a in arrays])
    return jnp.pad(flat, (0, -flat.shape[0] % 1024))


def unpack(flat, arrays):
    out = []
    start = 0
    for a in arrays:
        size = math.prod(a.shape)
        out.append(flat[start : start + size].reshape(a.shape))
        start += size
    return out


def sequence_device(
    block_input,
    lengths,
    ln1_gain,
    ln1_bias,
    input_weight,
    input_bias,
    conv_w,
    conv_b,
    filt_w1,
    filt_b1,
    filt_w2,
    filt_b2,
    filt_w3,
    decay,
    skip,
    output_weight,
    output_bias,
    ln2_gain,
    ln2_bias,
    up_weight,
    up_bias,
    down_weight,
    down_bias,
    cotangent,
):
    blocks, block, model = block_input.shape
    count = lax.axis_size("chan")
    quarter = block // count
    rows = blocks * quarter
    width = decay.shape[0]
    seq_length = blocks * block
    seq_index = lax.axis_index("seq")
    chan_index = lax.axis_index("chan")
    own = chan_index.astype(jnp.int32).reshape(1)
    length = lax.dynamic_slice(lengths, (seq_index,), (1,))
    tables = wave_tables(block)
    row = lambda v: v.reshape(1, -1)

    def own_rows(values):
        part = lax.dynamic_slice_in_dim(values, chan_index * quarter, quarter, 1)
        return transpose_blocks(part)

    x_own = own_rows(block_input)
    x_parts = spread(x_own)
    x_own, cotangent_home = lax.optimization_barrier((x_own, cotangent))
    cot_own = own_rows(cotangent_home).reshape(rows, model)
    x_rows = x_own.reshape(rows, model)

    up_parts = spread(up_weight)
    late, down_home, out_home = lax.optimization_barrier((x_parts[2], down_weight, output_weight))
    x_parts = [x_parts[0], x_parts[1], late, x_parts[3]]
    down_parts = spread(down_home)
    out_parts = spread(out_home)
    up_bias_parts = [swap(up_bias, "chan", k) if k else up_bias for k in range(count)]

    place_values = jnp.arange(seq_length, dtype=jnp.int32).astype(F32)
    features = position_features(place_values, seq_length, filt_w1.shape[0])
    kernel, filter_pull = jax.vjp(
        partial(implicit_filter, features, place_values), filt_w1, filt_b1, filt_w2, filt_b2, filt_w3, decay
    )
    k_spec = filter_spectrum(kernel.reshape(blocks, block, width), tables)

    weight = jnp.transpose(input_weight, (1, 0, 2))
    (normed_high, normed_low, proj, conv, s_spec), mixed = mixer_forward(
        own, length, x_parts, row(ln1_gain), row(ln1_bias), weight, input_bias, conv_w, conv_b, row(skip), k_spec, tables
    )
    mixed = [m if k == 0 else swap(m, "chan", k) for k, m in enumerate(mixed)]
    mixed = [m.reshape(rows, width) for m in mixed]

    hidden, *rest = hidden_forward(
        mixed, out_parts, x_rows, cot_own, row(output_bias), row(ln2_gain), row(ln2_bias)
    )
    normed2, turned, cot_parts = rest[0:2], rest[2:4], rest[4:6]
    sums = None
    grads_up, grads_down, grads_up_bias = [None] * count, [None] * count, [None] * count
    for k in (1, 0, 3, 2):
        sums, (grads_up[k], grads_down[k], grads_up_bias[k]) = feed_forward(
            normed2, turned, cot_parts, up_parts[k], row(up_bias_parts[k]), down_parts[k], sums
        )
    (out_rows, grad_hidden, sums2), grad_mixed, grads_out = hidden_backward(
        hidden, sums[0], sums[1], cot_own, mixed, out_parts, row(ln2_gain), row(down_bias)
    )

    grad_mixed = [g.reshape(blocks, quarter, width) for g in grad_mixed]
    grad_mixed = [g if k == 0 else swap(g, "chan", k) for k, g in enumerate(grad_mixed)]
    (g_spec, grad_proj, mixer_sums), grad_normed = mixer_backward(
        own, length, grad_mixed, proj, conv, s_spec, k_spec, conv_w, conv_b, row(skip), weight, tables
    )

    def to_home(values):
        part = transpose_blocks(values.reshape(blocks, quarter, model))
        return put_together(own, spread(part))

    output = to_home(out_rows)
    grad_down = sum(collect(grads_down))
    grad_up = sum(collect(grads_up))
    grad_out = sum(collect(grads_out))
    grad_down, grad_up, grad_out = lax.psum((grad_down, grad_up, grad_out), "seq")

    pieces = [p.reshape(rows, model) for p in collect(grad_normed)]
    grad_x_rows, sums1 = input_backward(pieces, x_rows, grad_hidden, row(ln1_gain))
    grad_x = to_home(grad_x_rows)

    grad_in = input_weight_grad(normed_high, normed_low, grad_proj)
    grad_in = lax.psum(grad_in, "seq")
    grad_in = jnp.transpose(grad_in, (1, 0, 2))

    grad_kernel = filter_backward(s_spec, g_spec, tables).reshape(seq_length, width)
    grad_fw1, grad_fb1, grad_fw2, grad_fb2, grad_fw3, grad_decay = filter_pull(grad_kernel)

    up_bias_grads = jnp.take(
        jnp.concatenate(grads_up_bias, 0), jnp.arange(count, dtype=jnp.int32) ^ chan_index, axis=0
    )
    shared = [sums1[0], sums1[1], *[sums2[i] for i in range(4)], up_bias_grads, grad_fw1, grad_fb1, grad_fw2, grad_fb2]
    split = [mixer_sums, grad_fw3, grad_decay]
    shared_flat = total_over(pack(shared), "chan")
    flat = total_over(jnp.concatenate([shared_flat, pack(split)]), "seq")
    cut = shared_flat.shape[0]
    grad_ln1_gain, grad_ln1_bias, grad_ln2_gain, grad_ln2_bias, grad_b_out, grad_b_fc2, up_bias_grads, *filt = unpack(
        flat[:cut], shared
    )
    mixer_sums, grad_fw3, grad_decay = unpack(flat[cut:], split)
    grad_b_fc1 = lax.dynamic_slice_in_dim(up_bias_grads, chan_index, 1, 0)[0]
    grad_skip = mixer_sums[0]
    grad_conv_b = mixer_sums[1:4]
    grad_conv_w = mixer_sums[4:13].reshape(3, 3, width)
    grad_b_in = mixer_sums[13:16]
    return (
        output,
        grad_x,
        grad_ln1_gain,
        grad_ln1_bias,
        grad_in,
        grad_b_in,
        grad_conv_w,
        grad_conv_b,
        *filt,
        grad_fw3,
        grad_decay,
        grad_skip,
        grad_out,
        grad_b_out,
        grad_ln2_gain,
        grad_ln2_bias,
        grad_up,
        grad_b_fc1,
        grad_down,
        grad_b_fc2,
    )


def solution(mesh):
    in_specs = (
        P(None, "seq", None),
        P(),
        P(),
        P(),
        P(None, None, "chan"),
        P(None, "chan"),
        P(None, None, "chan"),
        P(None, "chan"),
        P(),
        P(),
        P(),
        P(),
        P(None, "chan"),
        P("chan"),
        P("chan"),
        P("chan", None),
        P(),
        P(),
        P(),
        P(None, "chan"),
        P("chan"),
        P("chan", None),
        P(),
        P(None, "seq", None),
    )
    out_specs = (
        P(None, "seq", None),
        P(None, "seq", None),
        P(),
        P(),
        P(None, None, "chan"),
        P(None, "chan"),
        P(None, None, "chan"),
        P(None, "chan"),
        P(),
        P(),
        P(),
        P(),
        P(None, "chan"),
        P("chan"),
        P("chan"),
        P("chan", None),
        P(),
        P(),
        P(),
        P(None, "chan"),
        P("chan"),
        P("chan", None),
        P(),
    )
    chan = mesh.shape["chan"]

    def step(*arrays):
        sequences, seq_length = arrays[0].shape[:2]
        whole_sequences = sequences == mesh.shape["seq"] and chan == 4 and seq_length % (64 * sequences) == 0
        body = sequence_device if whole_sequences else spectral_device
        return jax.shard_map(
            body, mesh=mesh, in_specs=in_specs, out_specs=out_specs, check_vma=False
        )(*arrays)

    return step
```

```python
from functools import partial
import math

import jax
import jax.numpy as jnp
import ml_dtypes
import numpy as np
from jax import lax
from jax.experimental import pallas as pl
from jax.experimental.pallas import tpu as pltpu
from jax.sharding import PartitionSpec as P

EPSILON = 1e-05
HIGH_ACCURACY = lax.Precision.HIGHEST


def shifted(block, axis, distance):
    devices = range(lax.axis_size(axis))
    route = [(i - distance, i) for i in devices if i - distance in devices]
    return lax.ppermute(block, axis, route)


def layer_norm(values, gain, offset):
    average = jnp.mean(values, -1, keepdims=True)
    centered = values - average
    variance = jnp.mean(centered * centered, -1, keepdims=True)
    return centered * lax.rsqrt(variance + EPSILON) * gain + offset


def position_features(place_values, seq_length, emb_width):
    band_count = (emb_width - 1) // 2
    frequency = jnp.linspace(0.0001, band_count - 1, band_count).astype(jnp.float32)
    phases = 2.0 * math.pi * place_values[:, None] * frequency[None, :] / seq_length
    return jnp.concatenate(
        [(place_values / (seq_length - 1))[:, None], jnp.cos(phases), -jnp.sin(phases)], 1
    )


def implicit_filter(features, place_values, filt_w1, filt_b1, filt_w2, filt_b2, filt_w3, decay):
    first_layer = jnp.sin(jnp.dot(features, filt_w1, precision=HIGH_ACCURACY) + filt_b1)
    second_layer = jnp.sin(jnp.dot(first_layer, filt_w2, precision=HIGH_ACCURACY) + filt_b2)
    raw_kernel = jnp.dot(second_layer, filt_w3, precision=HIGH_ACCURACY)
    return raw_kernel * jnp.exp(-decay[None, :] * place_values[:, None])


def exact_gelu(values):
    return jax.nn.gelu(values, approximate=False)


def tables(count_rows, count_cols):
    turns = (
        jnp.arange(count_rows, dtype=jnp.int32)[:, None]
        * jnp.arange(count_cols, dtype=jnp.int32)[None, :]
        % count_rows
    )
    phases = turns.astype(jnp.float32) * (2.0 * math.pi / count_rows)
    return (jnp.cos(phases), jnp.sin(phases))


def rotate(cos_tab, sin_tab, real, imag, sign, form):
    first_part = jnp.einsum(form, cos_tab, real, precision=HIGH_ACCURACY)
    second_part = jnp.einsum(form, sin_tab, imag, precision=HIGH_ACCURACY)
    third_part = jnp.einsum(form, cos_tab, imag, precision=HIGH_ACCURACY)
    fourth_part = jnp.einsum(form, sin_tab, real, precision=HIGH_ACCURACY)
    return (first_part - sign * second_part, third_part + sign * fourth_part)


def to_spectrum(cos_tab, sin_tab, signal):
    real = jnp.einsum("wp,spc->swc", cos_tab, signal, precision=HIGH_ACCURACY)
    imag = -jnp.einsum("wp,spc->swc", sin_tab, signal, precision=HIGH_ACCURACY)
    return (real, imag)


def time_domain(cos_tab, sin_tab, real, imag):
    return jnp.einsum("wp,swc->spc", cos_tab, real, precision=HIGH_ACCURACY) - jnp.einsum(
        "wp,swc->spc", sin_tab, imag, precision=HIGH_ACCURACY
    )


def earlier_block(values):
    return jnp.pad(values, ((0, 0), (1, 0), (0, 0), (0, 0)))[:, :-1]


def later_block(values):
    return jnp.pad(values, ((0, 0), (0, 1), (0, 0), (0, 0)))[:, 1:]


def spectral_device(
    block_input,
    lengths,
    ln1_gain,
    ln1_bias,
    input_weight,
    input_bias,
    conv_w,
    conv_b,
    filt_w1,
    filt_b1,
    filt_w2,
    filt_b2,
    filt_w3,
    decay,
    skip,
    output_weight,
    output_bias,
    ln2_gain,
    ln2_bias,
    up_weight,
    up_bias,
    down_weight,
    down_bias,
    cotangent,
):
    block = block_input.shape[1]
    blocks = lax.axis_size("seq")
    share = 2 * block // blocks
    seq_index = lax.axis_index("seq")
    places = seq_index * block + jnp.arange(block, dtype=jnp.int32)
    place_values = places.astype(jnp.float32)
    mask = (places[None, :] < lengths[:, None]).astype(jnp.float32)[:, :, None]
    first_normed, norm1_pull = jax.vjp(layer_norm, block_input, ln1_gain, ln1_bias)
    input_projected = (
        jnp.einsum("spd,dkc->spkc", first_normed, input_weight, precision=HIGH_ACCURACY)
        + input_bias
    )
    rims = shifted(input_projected[:, block - 2 :], "seq", 1)
    extended = jnp.concatenate([rims, input_projected], 1)
    short = (
        conv_w[0] * extended[:, :block]
        + conv_w[1] * extended[:, 1 : block + 1]
        + conv_w[2] * extended[:, 2:]
        + conv_b
    )
    gate_out = short[:, :, 0]
    gate_in = short[:, :, 1]
    values = short[:, :, 2]
    signal = values * gate_in * mask
    cos_tab, sin_tab = tables(2 * block, block)
    block_cos, block_sin = tables(2 * blocks, blocks)
    own_freq = seq_index * share + jnp.arange(share, dtype=jnp.int32)
    parity = (1 - 2 * (own_freq % 2)).astype(jnp.float32)[:, None]
    features = position_features(place_values, blocks * block, filt_w1.shape[0])
    kernel, filter_pull = jax.vjp(
        partial(implicit_filter, features, place_values),
        filt_w1,
        filt_b1,
        filt_w2,
        filt_b2,
        filt_w3,
        decay,
    )
    signal_re, signal_im = to_spectrum(cos_tab, sin_tab, signal)
    kernel_re, kernel_im = to_spectrum(cos_tab, sin_tab, kernel[None])
    signal_re, signal_im, kernel_re, kernel_im = (
        lax.all_to_all(signal_re[:, None], "seq", split_axis=2, concat_axis=1, tiled=True),
        lax.all_to_all(signal_im[:, None], "seq", split_axis=2, concat_axis=1, tiled=True),
        lax.all_to_all(kernel_re[:, None], "seq", split_axis=2, concat_axis=1, tiled=True),
        lax.all_to_all(kernel_im[:, None], "seq", split_axis=2, concat_axis=1, tiled=True),
    )
    zq_re, zq_im = rotate(block_cos, block_sin, signal_re, signal_im, -1.0, "qk,skfc->sqfc")
    hq_re, hq_im = rotate(block_cos, block_sin, kernel_re, kernel_im, -1.0, "qk,skfc->sqfc")
    prod_re = zq_re * hq_re - zq_im * hq_im
    prod_im = zq_re * hq_im + zq_im * hq_re
    joined_re, joined_im = rotate(block_cos, block_sin, prod_re, prod_im, 1.0, "qj,sqfc->sjfc")
    joined_re = joined_re / (2 * blocks)
    joined_im = joined_im / (2 * blocks)
    folded_re = joined_re + parity * earlier_block(joined_re)
    folded_im = joined_im + parity * earlier_block(joined_im)
    folded_re, folded_im = (
        lax.all_to_all(folded_re, "seq", split_axis=1, concat_axis=2, tiled=True),
        lax.all_to_all(folded_im, "seq", split_axis=1, concat_axis=2, tiled=True),
    )
    convolved = time_domain(cos_tab, sin_tab, folded_re[:, 0], folded_im[:, 0]) / (2 * block)
    conv_sum = convolved + skip * signal
    mixer_output = conv_sum * gate_out
    partial_mix = jnp.einsum("spc,cd->spd", mixer_output, output_weight, precision=HIGH_ACCURACY)
    hidden_state = block_input + lax.psum(partial_mix, "chan") + output_bias
    second_normed2 = layer_norm(hidden_state, ln2_gain, ln2_bias)
    before = jnp.einsum("spd,df->spf", second_normed2, up_weight, precision=HIGH_ACCURACY) + up_bias
    active_units, gelu_pull = jax.vjp(exact_gelu, before)
    feed = lax.psum(
        jnp.einsum("spf,fd->spd", active_units, down_weight, precision=HIGH_ACCURACY), "chan"
    )
    output = hidden_state + feed + down_bias
    grad_b_fc2 = jnp.sum(cotangent, (0, 1))
    grad_w_fc2 = jnp.einsum("spf,spd->fd", active_units, cotangent, precision=HIGH_ACCURACY)
    grad_active = jnp.einsum("spd,fd->spf", cotangent, down_weight, precision=HIGH_ACCURACY)
    grad_before = gelu_pull(grad_active)[0]
    grad_w_fc1 = jnp.einsum("spd,spf->df", second_normed2, grad_before, precision=HIGH_ACCURACY)
    grad_b_fc1 = jnp.sum(grad_before, (0, 1))
    grad_normed2 = lax.psum(
        jnp.einsum("spf,df->spd", grad_before, up_weight, precision=HIGH_ACCURACY), "chan"
    )
    norm2_pull = jax.vjp(layer_norm, hidden_state, ln2_gain, ln2_bias)[1]
    grad_hidden_norm, grad_ln2_gain, grad_ln2_bias = norm2_pull(grad_normed2)
    grad_hidden = cotangent + grad_hidden_norm
    grad_b_out = jnp.sum(grad_hidden, (0, 1))
    grad_w_out = jnp.einsum("spc,spd->cd", mixer_output, grad_hidden, precision=HIGH_ACCURACY)
    grad_mixed = jnp.einsum("spd,cd->spc", grad_hidden, output_weight, precision=HIGH_ACCURACY)
    grad_conv = grad_mixed * gate_out
    grad_gate_out = grad_mixed * conv_sum
    grad_skip = jnp.sum(grad_conv * signal, (0, 1))
    back_re, back_im = to_spectrum(cos_tab, sin_tab, grad_conv)
    back_re = back_re / (2 * block)
    back_im = back_im / (2 * block)
    back_re, back_im = (
        lax.all_to_all(back_re[:, None], "seq", split_axis=2, concat_axis=1, tiled=True),
        lax.all_to_all(back_im[:, None], "seq", split_axis=2, concat_axis=1, tiled=True),
    )
    unfold_re = back_re + parity * later_block(back_re)
    unfold_im = back_im + parity * later_block(back_im)
    dprod_re, dprod_im = rotate(block_cos, block_sin, unfold_re, unfold_im, -1.0, "qj,sjfc->sqfc")
    dprod_re = dprod_re / (2 * blocks)
    dprod_im = dprod_im / (2 * blocks)
    dzq_re = hq_re * dprod_re + hq_im * dprod_im
    dzq_im = hq_re * dprod_im - hq_im * dprod_re
    dhq_re = jnp.sum(zq_re * dprod_re + zq_im * dprod_im, 0, keepdims=True)
    dhq_im = jnp.sum(zq_re * dprod_im - zq_im * dprod_re, 0, keepdims=True)
    dsig_re, dsig_im = rotate(block_cos, block_sin, dzq_re, dzq_im, 1.0, "qk,sqfc->skfc")
    dker_re, dker_im = rotate(block_cos, block_sin, dhq_re, dhq_im, 1.0, "qk,sqfc->skfc")
    dsig_re, dsig_im, dker_re, dker_im = (
        lax.all_to_all(dsig_re, "seq", split_axis=1, concat_axis=2, tiled=True),
        lax.all_to_all(dsig_im, "seq", split_axis=1, concat_axis=2, tiled=True),
        lax.all_to_all(dker_re, "seq", split_axis=1, concat_axis=2, tiled=True),
        lax.all_to_all(dker_im, "seq", split_axis=1, concat_axis=2, tiled=True),
    )
    grad_signal = time_domain(cos_tab, sin_tab, dsig_re[:, 0], dsig_im[:, 0]) + grad_conv * skip
    grad_kernel = time_domain(cos_tab, sin_tab, dker_re[:, 0], dker_im[:, 0])[0]
    grad_fw1, grad_fb1, grad_fw2, grad_fb2, grad_fw3, grad_decay = filter_pull(grad_kernel)
    grad_short = jnp.stack(
        [grad_gate_out, grad_signal * values * mask, grad_signal * gate_in * mask], 2
    )
    grad_conv_b = jnp.sum(grad_short, (0, 1))
    grad_conv_w = jnp.stack(
        [jnp.sum(grad_short * extended[:, offset : offset + block], (0, 1)) for offset in range(3)]
    )
    grad_extended = (
        jnp.pad(conv_w[0] * grad_short, ((0, 0), (0, 2), (0, 0), (0, 0)))
        + jnp.pad(conv_w[1] * grad_short, ((0, 0), (1, 1), (0, 0), (0, 0)))
        + jnp.pad(conv_w[2] * grad_short, ((0, 0), (2, 0), (0, 0), (0, 0)))
    )
    returned = shifted(grad_extended[:, :2], "seq", -1)
    grad_proj = grad_extended[:, 2:] + jnp.pad(returned, ((0, 0), (block - 2, 0), (0, 0), (0, 0)))
    grad_b_in = jnp.sum(grad_proj, (0, 1))
    grad_w_in = jnp.einsum("spd,spkc->dkc", first_normed, grad_proj, precision=HIGH_ACCURACY)
    grad_normed = lax.psum(
        jnp.einsum("spkc,dkc->spd", grad_proj, input_weight, precision=HIGH_ACCURACY), "chan"
    )
    grad_x_norm, grad_ln1_gain, grad_ln1_bias = norm1_pull(grad_normed)
    grad_x = grad_hidden + grad_x_norm
    (
        grad_ln1_gain,
        grad_ln1_bias,
        grad_w_in,
        grad_b_in,
        grad_conv_w,
        grad_conv_b,
        grad_fw3,
        grad_decay,
        grad_skip,
        grad_w_out,
        grad_b_out,
        grad_ln2_gain,
        grad_ln2_bias,
        grad_w_fc1,
        grad_b_fc1,
        grad_w_fc2,
        grad_b_fc2,
    ) = lax.psum(
        (
            grad_ln1_gain,
            grad_ln1_bias,
            grad_w_in,
            grad_b_in,
            grad_conv_w,
            grad_conv_b,
            grad_fw3,
            grad_decay,
            grad_skip,
            grad_w_out,
            grad_b_out,
            grad_ln2_gain,
            grad_ln2_bias,
            grad_w_fc1,
            grad_b_fc1,
            grad_w_fc2,
            grad_b_fc2,
        ),
        "seq",
    )
    grad_fw1, grad_fb1, grad_fw2, grad_fb2 = lax.psum(
        (grad_fw1, grad_fb1, grad_fw2, grad_fb2), ("seq", "chan")
    )
    return (
        output,
        grad_x,
        grad_ln1_gain,
        grad_ln1_bias,
        grad_w_in,
        grad_b_in,
        grad_conv_w,
        grad_conv_b,
        grad_fw1,
        grad_fb1,
        grad_fw2,
        grad_fb2,
        grad_fw3,
        grad_decay,
        grad_skip,
        grad_w_out,
        grad_b_out,
        grad_ln2_gain,
        grad_ln2_bias,
        grad_w_fc1,
        grad_b_fc1,
        grad_w_fc2,
        grad_b_fc2,
    )


F32 = jnp.float32
BF16 = jnp.bfloat16
NN = (((1,), (0,)), ((), ()))
NT = (((1,), (1,)), ((), ()))
TN = (((0,), (0,)), ((), ()))
VMEM_BYTES = 56 * 2**20


def parts_of(values):
    high = values.astype(BF16)
    return high, (values - high.astype(F32)).astype(BF16)


def dot_parts(left, right, dims):
    def one(a, b):
        return lax.dot_general(a, b, dims, preferred_element_type=F32)

    return one(left[0], right[0]) + (one(left[0], right[1]) + one(left[1], right[0]))


def normalise(values):
    average = jnp.mean(values, -1, keepdims=True)
    centered = values - average
    variance = jnp.mean(centered * centered, -1, keepdims=True)
    scale = lax.rsqrt(variance + EPSILON)
    return centered * scale, scale


def norm_back(unit, scale, gain, grad):
    lifted = grad * gain
    mean_one = jnp.mean(lifted, -1, keepdims=True)
    mean_two = jnp.mean(lifted * unit, -1, keepdims=True)
    return scale * (lifted - mean_one - unit * mean_two)


def column_sum(values):
    return jnp.sum(values, 0, keepdims=True)


def whole(array):
    return pl.BlockSpec(array.shape, lambda *_: (0,) * len(array.shape))


def scalar_spec():
    return pl.BlockSpec(memory_space=pltpu.SMEM)


def struct(shape, kind=F32):
    return jax.ShapeDtypeStruct(tuple(shape), kind)


def run_kernel(body, name, grid, in_specs, out_specs, out_shape, scratch, args, micros):
    return pl.pallas_call(
        body,
        name=name,
        grid=grid,
        in_specs=in_specs,
        out_specs=out_specs,
        out_shape=out_shape,
        scratch_shapes=scratch,
        compiler_params=pltpu.CompilerParams(
            dimension_semantics=("arbitrary",) * len(grid), vmem_limit_bytes=VMEM_BYTES
        ),
        cost_estimate=pl.CostEstimate(
            flops=int(micros * 1.15e9), bytes_accessed=int(micros * 3.6e6), transcendentals=0
        ),
    )(*args)


def wave_tables(block):
    angles = np.pi * np.outer(2 * np.arange(block) + 1, np.arange(block)) / (2 * block)
    table = np.concatenate([np.cos(angles), -np.sin(angles)], 0)

    def both(values):
        high = values.astype(ml_dtypes.bfloat16)
        low = (values - high.astype(np.float64)).astype(ml_dtypes.bfloat16)
        return jnp.asarray(high), jnp.asarray(low)

    return both(table) + both(table.T / block)


def parity_of(rows):
    odd = lax.broadcasted_iota(jnp.int32, (rows, 1), 0) % 2
    return (1 - 2 * odd).astype(F32)


def filter_spectrum(kernel, tables):
    blocks, block, width = kernel.shape
    table_high, table_low = tables[:2]

    def body(kernel_ref, high_ref, low_ref, out_ref, before_ref):
        @pl.when(pl.program_id(0) == 0)
        def _():
            before_ref[...] = jnp.zeros_like(before_ref)

        spectrum = dot_parts((high_ref[...], low_ref[...]), parts_of(kernel_ref[0]), NN)
        sign = parity_of(block)
        out_ref[0, :block] = spectrum[:block] - sign * before_ref[block:]
        out_ref[0, block:] = spectrum[block:] + sign * before_ref[:block]
        before_ref[...] = spectrum

    return run_kernel(
        body,
        "filter_spectrum",
        (blocks,),
        [pl.BlockSpec((1, block, width), lambda b: (b, 0, 0)), whole(table_high), whole(table_low)],
        [pl.BlockSpec((1, 2 * block, width), lambda b: (b, 0, 0))],
        [struct((blocks, 2 * block, width))],
        [pltpu.VMEM((2 * block, width), F32)],
        [kernel, table_high, table_low],
        8,
    )[0]


def mixer_forward(own, length, x_parts, gain, offset, weight, bias, conv_w, conv_b, skip, spectrum, tables):
    blocks, quarter, model = x_parts[0].shape
    count = len(x_parts)
    block = quarter * count
    width = weight.shape[2]
    tile = min(32, block)
    pair = 2 - blocks % 2
    span = pair * block

    def body(*refs):
        own_ref, length_ref = refs[:2]
        x_refs = refs[2 : 2 + count]
        refs = refs[2 + count :]
        gain_ref, offset_ref, weight_ref, bias_ref, conv_w_ref, conv_b_ref, skip_ref, k_ref = refs[:8]
        th_ref, tl_ref, ih_ref, il_ref = refs[8:12]
        nh_ref, nl_ref, proj_ref, conv_ref, s_ref = refs[12:17]
        m_refs = refs[17 : 17 + count]
        wh_ref, wl_ref, ext_ref, o_ref, mixed_ref = refs[17 + count :]
        step = pl.program_id(0)
        me = own_ref[0]

        @pl.when(step == 0)
        def _():
            for k in range(3):
                wh_ref[k], wl_ref[k] = parts_of(weight_ref[k])
            ext_ref[:, :8] = jnp.zeros((3, 8, width), F32)

        for u in range(pair):
            for k in range(count):
                normed = normalise(x_refs[k][u])[0] * gain_ref[...] + offset_ref[...]
                start = pl.multiple_of(u * block + (me ^ k) * quarter, quarter)
                high, low = parts_of(normed)
                nh_ref[0, pl.ds(start, quarter), :] = high
                nl_ref[0, pl.ds(start, quarter), :] = low
        normed = (nh_ref[0], nl_ref[0])
        short = []
        for k in range(3):
            proj = dot_parts(normed, (wh_ref[k], wl_ref[k]), NN) + bias_ref[k : k + 1, :]
            proj_ref[0, k] = proj
            ext_ref[k, 8:] = proj
            short.append(
                conv_w_ref[0, k : k + 1, :] * ext_ref[k, 6 : 6 + span]
                + conv_w_ref[1, k : k + 1, :] * ext_ref[k, 7 : 7 + span]
                + conv_w_ref[2, k : k + 1, :] * proj
                + conv_b_ref[k : k + 1, :]
            )
            ext_ref[k, :8] = ext_ref[k, span:]
        places = step * span + lax.broadcasted_iota(jnp.int32, (span, 1), 0)
        mask = (places < length_ref[0]).astype(F32)
        signal = short[2] * short[1] * mask
        for u in range(pair):
            part = signal[u * block : (u + 1) * block]
            s_ref[step * pair + u] = dot_parts((th_ref[...], tl_ref[...]), parts_of(part), NN)
        for u in range(pair):
            b = step * pair + u
            for r in range(0, block, tile):
                lo = slice(r, r + tile)
                hi = slice(block + r, block + r + tile)

                def product(i, total, b=b, lo=lo, hi=hi):
                    s_re, s_im = s_ref[i, lo], s_ref[i, hi]
                    k_re, k_im = k_ref[b - i, lo], k_ref[b - i, hi]
                    return total[0] + s_re * k_re - s_im * k_im, total[1] + s_re * k_im + s_im * k_re

                zero = jnp.zeros((tile, width), F32)
                o_ref[u, lo], o_ref[u, hi] = lax.fori_loop(0, b + 1, product, (zero, zero))
        inverse = (ih_ref[...], il_ref[...])
        conv = jnp.concatenate([dot_parts(inverse, parts_of(o_ref[u]), NN) for u in range(pair)], 0)
        conv = conv + skip_ref[...] * signal
        conv_ref[0] = conv
        mixed_ref[...] = conv * short[0]
        for u in range(pair):
            for k in range(count):
                start = pl.multiple_of(u * block + (me ^ k) * quarter, quarter)
                m_refs[k][u] = mixed_ref[pl.ds(start, quarter), :]

    by_block = lambda *shape: pl.BlockSpec((1,) + shape, lambda b: (b,) + (0,) * len(shape))
    args = [own, length, *x_parts, gain, offset, weight, bias, conv_w, conv_b, skip, spectrum, *tables]
    by_pair = lambda n: pl.BlockSpec((pair, quarter, n), lambda b: (b, 0, 0))
    in_specs = [scalar_spec(), scalar_spec()] + [by_pair(model)] * count
    in_specs += [whole(a) for a in args[2 + count :]]
    s_shape = struct((blocks, 2 * block, width))
    outs = run_kernel(
        body,
        "mixer_forward",
        (blocks // pair,),
        in_specs,
        [by_block(span, model)] * 2
        + [by_block(3, span, width), by_block(span, width), whole(s_shape)]
        + [by_pair(width)] * count,
        [struct((blocks // pair, span, model), BF16)] * 2
        + [struct((blocks // pair, 3, span, width)), struct((blocks // pair, span, width)), s_shape]
        + [struct((blocks, quarter, width))] * count,
        [
            pltpu.VMEM((3, model, width), BF16),
            pltpu.VMEM((3, model, width), BF16),
            pltpu.VMEM((3, span + 8, width), F32),
            pltpu.VMEM((pair, 2 * block, width), F32),
            pltpu.VMEM((span, width), F32),
        ],
        args,
        36,
    )
    return outs[:5], list(outs[5:])


def hidden_forward(m_parts, weights, x_own, cotangent, bias, gain, offset):
    rows, width = m_parts[0].shape
    model = x_own.shape[1]
    count = len(m_parts)
    step = min(128, rows)

    def body(*refs):
        m_refs, w_refs = refs[:count], refs[count : 2 * count]
        x_ref, c_ref, bias_ref, gain_ref, offset_ref = refs[2 * count : 2 * count + 5]
        h_ref, nh_ref, nl_ref, th_ref, tl_ref, ch_ref, cl_ref = refs[2 * count + 5 : 2 * count + 12]
        wh_ref, wl_ref = refs[2 * count + 12 :]

        @pl.when(pl.program_id(0) == 0)
        def _():
            for k in range(count):
                wh_ref[k], wl_ref[k] = parts_of(w_refs[k][...])

        hidden = x_ref[...] + bias_ref[...]
        for k in range(count):
            hidden = hidden + dot_parts(parts_of(m_refs[k][...]), (wh_ref[k], wl_ref[k]), NN)
        h_ref[...] = hidden
        normed = normalise(hidden)[0] * gain_ref[...] + offset_ref[...]
        nh_ref[...], nl_ref[...] = parts_of(normed)
        th_ref[...], tl_ref[...] = parts_of(normed.T)
        ch_ref[...], cl_ref[...] = parts_of(c_ref[...])

    row_spec = lambda n: pl.BlockSpec((step, n), lambda r: (r, 0))
    turned = pl.BlockSpec((model, step), lambda r: (0, r))
    args = [*m_parts, *weights, x_own, cotangent, bias, gain, offset]
    return run_kernel(
        body,
        "hidden_forward",
        (rows // step,),
        [row_spec(width)] * count
        + [whole(w) for w in weights]
        + [row_spec(model)] * 2
        + [whole(bias), whole(gain), whole(offset)],
        [row_spec(model)] * 3 + [turned] * 2 + [row_spec(model)] * 2,
        [struct((rows, model))]
        + [struct((rows, model), BF16)] * 2
        + [struct((model, rows), BF16)] * 2
        + [struct((rows, model), BF16)] * 2,
        [pltpu.VMEM((count, width, model), BF16)] * 2,
        args,
        9,
    )


def feed_forward(side, normed, turned, cotangent, up, up_bias, down, sums):
    rows, model = normed[0].shape
    units = up_bias.shape[1]
    step = min(256, units)
    first = sums is None
    pieces = len(up)

    def body(side_ref, *refs):
        nh_ref, nl_ref, th_ref, tl_ref, ch_ref, cl_ref, bias_ref = refs[:7]
        up_refs, down_refs = refs[7 : 7 + pieces], refs[7 + pieces : 7 + 2 * pieces]
        refs = refs[7 + 2 * pieces :]
        feed_in, grad_in = (None, None) if first else refs[:2]
        feed_ref, grad_ref, gup_ref, gdown_ref, gbias_ref = refs[0 if first else 2 :]

        @pl.when(pl.program_id(0) == 0)
        def _():
            if first:
                feed_ref[...] = jnp.zeros_like(feed_ref)
                grad_ref[...] = jnp.zeros_like(grad_ref)
            else:
                feed_ref[...] = feed_in[...]
                grad_ref[...] = grad_in[...]

        def in_order(halves, axis):
            if pieces == 1:
                return halves[0][...]
            mine, other = halves[0][...], halves[1][...]
            low = side_ref[0] == 0
            return jnp.concatenate([jnp.where(low, mine, other), jnp.where(low, other, mine)], axis)

        own_normed = (nh_ref[...], nl_ref[...])
        own_cotangent = (ch_ref[...], cl_ref[...])
        up_parts = parts_of(in_order(up_refs, 0))
        down_parts = parts_of(in_order(down_refs, 1))
        before = dot_parts(own_normed, up_parts, NN) + bias_ref[...]
        grad_active = dot_parts(own_cotangent, down_parts, NT)
        below = 0.5 + 0.5 * lax.erf(before * math.sqrt(0.5))
        slope = below + before * (jnp.exp(-0.5 * before * before) * (1.0 / math.sqrt(2.0 * math.pi)))
        active = before * below
        grad_before = grad_active * slope
        gbias_ref[...] = column_sum(grad_before)
        active_parts = parts_of(active)
        grad_parts = parts_of(grad_before)
        feed_ref[...] += dot_parts(active_parts, down_parts, NN)
        grad_ref[...] += dot_parts(grad_parts, up_parts, NT)
        gup_ref[...] = dot_parts((th_ref[...], tl_ref[...]), grad_parts, NN)
        gdown_ref[...] = dot_parts(active_parts, own_cotangent, TN)

    total = struct((rows, model))
    args = [side, *normed, *turned, *cotangent, up_bias, *up, *down] + ([] if first else list(sums))
    columns = lambda n: pl.BlockSpec((n, step), lambda t: (0, t))
    some_rows = lambda n: pl.BlockSpec((step, n), lambda t: (t, 0))
    outs = run_kernel(
        body,
        "feed_forward",
        (units // step,),
        [scalar_spec()]
        + [whole(a) for a in args[1:7]]
        + [columns(1)]
        + [columns(model // pieces)] * pieces
        + [some_rows(model // pieces)] * pieces
        + [whole(a) for a in args[8 + 2 * pieces :]],
        [whole(total), whole(total), columns(model), some_rows(model), columns(1)],
        [total, total, struct((model, units)), struct((units, model)), struct(up_bias.shape)],
        [],
        args,
        18,
    )
    return outs[:2], outs[2:]


def hidden_backward(hidden, feed, grad_normed, cotangent, m_parts, weights, gain, bias):
    rows, model = hidden.shape
    width = m_parts[0].shape[1]
    count = len(m_parts)
    step = min(128, rows)

    def body(*refs):
        h_ref, f_ref, g_ref, c_ref = refs[:4]
        m_refs, w_refs = refs[4 : 4 + count], refs[4 + count : 4 + 2 * count]
        gain_ref, bias_ref, out_ref, gh_ref, sum_ref = refs[4 + 2 * count : 9 + 2 * count]
        gm_refs, refs = refs[9 + 2 * count : 9 + 3 * count], refs[9 + 3 * count :]
        gw_refs, (wh_ref, wl_ref) = refs[:2], refs[2:]

        @pl.when(pl.program_id(0) == 0)
        def _():
            sum_ref[...] = jnp.zeros_like(sum_ref)
            for k in range(count):
                wh_ref[k], wl_ref[k] = parts_of(w_refs[k][...])
            for k in range(2):
                gw_refs[k][...] = jnp.zeros_like(gw_refs[k])

        hidden_rows, grad, above = h_ref[...], g_ref[...], c_ref[...]
        out_ref[...] = hidden_rows + f_ref[...] + bias_ref[...]
        unit, scale = normalise(hidden_rows)
        grad_hidden = above + norm_back(unit, scale, gain_ref[...], grad)
        gh_ref[...] = grad_hidden
        sum_ref[0:1] += column_sum(grad * unit)
        sum_ref[1:2] += column_sum(grad)
        sum_ref[2:3] += column_sum(grad_hidden)
        sum_ref[3:4] += column_sum(above)
        parts = parts_of(grad_hidden)
        for k in range(count):
            gm_refs[k][...] = dot_parts(parts, (wh_ref[k], wl_ref[k]), NT)
            gw_refs[k // 2][k % 2] += dot_parts(parts_of(m_refs[k][...]), parts, TN)

    row_spec = lambda n: pl.BlockSpec((step, n), lambda r: (r, 0))
    args = [hidden, feed, grad_normed, cotangent, *m_parts, *weights, gain, bias]
    sums, pair = struct((8, model)), struct((2, width, model))
    outs = run_kernel(
        body,
        "hidden_backward",
        (rows // step,),
        [row_spec(model)] * 4 + [row_spec(width)] * count + [whole(w) for w in weights] + [whole(gain), whole(bias)],
        [row_spec(model)] * 2
        + [whole(sums)]
        + [row_spec(width)] * count
        + [whole(pair)] * 2,
        [struct((rows, model))] * 2 + [sums] + [struct((rows, width))] * count + [pair] * 2,
        [pltpu.VMEM((count, width, model), BF16)] * 2,
        args,
        15,
    )
    return outs[:3], list(outs[3 : 3 + count]), outs[3 + count :]


def mixer_backward(own, length, gm_parts, proj, conv, s_spec, k_spec, conv_w, conv_b, skip, weight, tables):
    blocks, quarter, width = gm_parts[0].shape
    count = len(gm_parts)
    block = quarter * count
    model = weight.shape[1]
    tile = min(32, block)
    pair = 2 - blocks % 2
    span = pair * block

    def body(*refs):
        own_ref, length_ref = refs[:2]
        gm_refs = refs[2 : 2 + count]
        refs = refs[2 + count :]
        proj_ref, rim_ref, conv_ref, k_ref, conv_w_ref, conv_b_ref, skip_ref, weight_ref = refs[:8]
        th_ref, tl_ref, ih_ref, il_ref = refs[8:12]
        g_ref, gp_ref, sum_ref = refs[12:15]
        gn_refs = refs[15 : 15 + count]
        wh_ref, wl_ref, ext_ref, gs_ref, o_ref, rows_ref, gn_ref = refs[15 + count :]
        step = pl.program_id(0)
        slot = blocks // pair - 1 - step
        me = own_ref[0]

        @pl.when(step == 0)
        def _():
            for k in range(3):
                wh_ref[k], wl_ref[k] = parts_of(weight_ref[k])
            gs_ref[:, span:] = jnp.zeros((3, 8, width), F32)
            sum_ref[...] = jnp.zeros_like(sum_ref)

        for u in range(pair):
            for k in range(count):
                start = pl.multiple_of(u * block + (me ^ k) * quarter, quarter)
                rows_ref[pl.ds(start, quarter), :] = gm_refs[k][u]
        inside = (slot > 0).astype(F32)
        short = []
        for k in range(3):
            ext_ref[k, :8] = rim_ref[0, k] * inside
            ext_ref[k, 8:] = proj_ref[0, k]
            short.append(
                conv_w_ref[0, k : k + 1, :] * ext_ref[k, 6 : 6 + span]
                + conv_w_ref[1, k : k + 1, :] * ext_ref[k, 7 : 7 + span]
                + conv_w_ref[2, k : k + 1, :] * proj_ref[0, k]
                + conv_b_ref[k : k + 1, :]
            )
        places = slot * span + lax.broadcasted_iota(jnp.int32, (span, 1), 0)
        mask = (places < length_ref[0]).astype(F32)
        gate_in, values = short[1] * mask, short[2] * mask
        grad_mixed = rows_ref[...]
        grad_conv = grad_mixed * short[0]
        gs_ref[0, :span] = grad_mixed * conv_ref[0]
        for u in range(pair):
            part = grad_conv[u * block : (u + 1) * block]
            g_ref[slot * pair + u] = dot_parts((th_ref[...], tl_ref[...]), parts_of(part), NN)
        for u in range(pair):
            b = slot * pair + u
            for r in range(0, block, tile):
                lo = slice(r, r + tile)
                hi = slice(block + r, block + r + tile)

                def product(j, total, b=b, lo=lo, hi=hi):
                    g_re, g_im = g_ref[j, lo], g_ref[j, hi]
                    k_re, k_im = k_ref[j - b, lo], k_ref[j - b, hi]
                    return total[0] + g_re * k_re + g_im * k_im, total[1] + g_im * k_re - g_re * k_im

                zero = jnp.zeros((tile, width), F32)
                o_ref[u, lo], o_ref[u, hi] = lax.fori_loop(b, blocks, product, (zero, zero))
        inverse = (ih_ref[...], il_ref[...])
        grad_signal = jnp.concatenate([dot_parts(inverse, parts_of(o_ref[u]), NN) for u in range(pair)], 0)
        grad_signal = grad_signal + skip_ref[...] * grad_conv
        gs_ref[1, :span] = grad_signal * values
        gs_ref[2, :span] = grad_signal * gate_in
        sum_ref[0:1] += column_sum(grad_conv * short[2] * gate_in)
        normed_grad = jnp.zeros((span, model), F32)
        for k in range(3):
            grad_short = gs_ref[k, :span]
            sum_ref[1 + k : 2 + k] += column_sum(grad_short)
            for t in range(3):
                row = 4 + 3 * t + k
                sum_ref[row : row + 1] += column_sum(grad_short * ext_ref[k, 6 + t : 6 + t + span])
            grad_proj = (
                conv_w_ref[2, k : k + 1, :] * grad_short
                + conv_w_ref[1, k : k + 1, :] * gs_ref[k, 1 : 1 + span]
                + conv_w_ref[0, k : k + 1, :] * gs_ref[k, 2 : 2 + span]
            )
            sum_ref[13 + k : 14 + k] += column_sum(grad_proj)
            gp_ref[0, k] = grad_proj
            normed_grad = normed_grad + dot_parts(parts_of(grad_proj), (wh_ref[k], wl_ref[k]), NT)
            gs_ref[k, span:] = gs_ref[k, :8]
        gn_ref[...] = normed_grad
        for u in range(pair):
            for k in range(count):
                start = pl.multiple_of(u * block + (me ^ k) * quarter, quarter)
                gn_refs[k][u] = gn_ref[pl.ds(start, quarter), :]

    last = blocks // pair - 1
    by_block = lambda *shape: pl.BlockSpec((1,) + shape, lambda s: (last - s,) + (0,) * len(shape))
    rim = pl.BlockSpec((1, 3, 8, width), lambda s: (jnp.maximum(last - s - 1, 0), 0, span // 8 - 1, 0))
    by_pair = lambda n: pl.BlockSpec((pair, quarter, n), lambda s: (last - s, 0, 0))
    fixed = [k_spec, conv_w, conv_b, skip, weight, *tables]
    spectra = struct((blocks, 2 * block, width))
    sums = struct((16, width))
    outs = run_kernel(
        body,
        "mixer_backward",
        (blocks // pair,),
        [scalar_spec(), scalar_spec()]
        + [by_pair(width)] * count
        + [by_block(3, span, width), rim, by_block(span, width)]
        + [whole(a) for a in fixed],
        [whole(spectra), by_block(3, span, width), whole(sums)] + [by_pair(model)] * count,
        [spectra, struct((blocks // pair, 3, span, width)), sums] + [struct((blocks, quarter, model))] * count,
        [
            pltpu.VMEM((3, model, width), BF16),
            pltpu.VMEM((3, model, width), BF16),
            pltpu.VMEM((3, span + 8, width), F32),
            pltpu.VMEM((3, span + 8, width), F32),
            pltpu.VMEM((pair, 2 * block, width), F32),
            pltpu.VMEM((span, width), F32),
            pltpu.VMEM((span, model), F32),
        ],
        [own, length, *gm_parts, proj, proj, conv, *fixed],
        35,
    )
    return outs[:3], list(outs[3:])


def filter_backward(s_spec, g_spec, tables):
    blocks, double, width = s_spec.shape
    block = double // 2
    tile = min(32, block)
    inverse = tables[2:]

    def body(s_ref, g_ref, ih_ref, il_ref, out_ref, after_ref, o_ref):
        m = blocks - 1 - pl.program_id(0)

        @pl.when(m == blocks - 1)
        def _():
            after_ref[...] = jnp.zeros_like(after_ref)

        sign = parity_of(tile)
        for r in range(0, block, tile):
            lo = slice(r, r + tile)
            hi = slice(block + r, block + r + tile)

            def product(j, total, lo=lo, hi=hi):
                g_re, g_im = g_ref[j, lo], g_ref[j, hi]
                s_re, s_im = s_ref[j - m, lo], s_ref[j - m, hi]
                return total[0] + g_re * s_re + g_im * s_im, total[1] + g_im * s_re - g_re * s_im

            zero = jnp.zeros((tile, width), F32)
            re, im = lax.fori_loop(m, blocks, product, (zero, zero))
            o_ref[lo] = re + sign * after_ref[hi]
            o_ref[hi] = im - sign * after_ref[lo]
            after_ref[lo], after_ref[hi] = re, im
        out_ref[0] = dot_parts((ih_ref[...], il_ref[...]), parts_of(o_ref[...]), NN)

    return run_kernel(
        body,
        "filter_backward",
        (blocks,),
        [whole(s_spec), whole(g_spec), whole(inverse[0]), whole(inverse[1])],
        [pl.BlockSpec((1, block, width), lambda s: (blocks - 1 - s, 0, 0))],
        [struct((blocks, block, width))],
        [pltpu.VMEM((double, width), F32)] * 2,
        [s_spec, g_spec, *inverse],
        13,
    )[0]


def input_weight_grad(normed_high, normed_low, grad_proj):
    blocks, block, model = normed_high.shape
    width = grad_proj.shape[3]

    def body(nh_ref, nl_ref, gp_ref, out_ref):
        @pl.when(pl.program_id(0) == 0)
        def _():
            out_ref[...] = jnp.zeros_like(out_ref)

        normed = (nh_ref[0], nl_ref[0])
        for k in range(3):
            out_ref[k] += dot_parts(parts_of(gp_ref[0, k]), normed, TN)

    by_block = lambda *shape: pl.BlockSpec((1,) + shape, lambda b: (b,) + (0,) * len(shape))
    out = struct((3, width, model))
    return run_kernel(
        body,
        "input_weight_grad",
        (blocks,),
        [by_block(block, model)] * 2 + [by_block(3, block, width)],
        [whole(out)],
        [out],
        [],
        [normed_high, normed_low, grad_proj],
        12,
    )[0]


def input_backward(grad_pieces, x_own, grad_hidden, gain):
    rows, model = x_own.shape
    count = len(grad_pieces)
    step = min(128, rows)

    def body(*refs):
        piece_refs = refs[:count]
        x_ref, gh_ref, gain_ref, out_ref, sum_ref = refs[count:]

        @pl.when(pl.program_id(0) == 0)
        def _():
            sum_ref[...] = jnp.zeros_like(sum_ref)

        grad = sum(r[...] for r in piece_refs)
        unit, scale = normalise(x_ref[...])
        out_ref[...] = gh_ref[...] + norm_back(unit, scale, gain_ref[...], grad)
        sum_ref[0:1] += column_sum(grad * unit)
        sum_ref[1:2] += column_sum(grad)

    row_spec = pl.BlockSpec((step, model), lambda r: (r, 0))
    sums = struct((8, model))
    return run_kernel(
        body,
        "input_backward",
        (rows // step,),
        [row_spec] * (count + 2) + [whole(gain)],
        [row_spec, whole(sums)],
        [struct((rows, model)), sums],
        [],
        [*grad_pieces, x_own, grad_hidden, gain],
        5,
    )


def put_together(own, pieces):
    groups, quarter, model = pieces[0].shape
    count = len(pieces)

    def body(own_ref, *refs):
        for k in range(count):
            start = pl.multiple_of((own_ref[0] ^ k) * quarter, quarter)
            refs[count][0, pl.ds(start, quarter), :] = refs[k][0]

    by_group = lambda n: pl.BlockSpec((1, n, model), lambda s: (s, 0, 0))
    return run_kernel(
        body,
        "put_together",
        (groups,),
        [scalar_spec()] + [by_group(quarter)] * count,
        [by_group(quarter * count)],
        [struct((groups, quarter * count, model))],
        [],
        [own, *pieces],
        8,
    )[0]


def swap(values, axis, bit):
    size = lax.axis_size(axis)
    return lax.ppermute(values, axis, [(i, i ^ bit) for i in range(size)])


def total_over(values, axis):
    bit = 1
    while bit < lax.axis_size(axis):
        values = values + swap(values, axis, bit)
        bit *= 2
    return values


def meet(*values):
    return lax.optimization_barrier(values)


def split_rows(values, axis, bit):
    mine = (lax.axis_index(axis) // bit) % 2
    half = values.shape[0] // 2
    leaving = lax.dynamic_slice_in_dim(values, (1 - mine) * half, half, 0)
    staying = lax.dynamic_slice_in_dim(values, mine * half, half, 0)
    return leaving, staying


def join_rows(values, other, axis, bit):
    first = (lax.axis_index(axis) // bit) % 2 == 0
    return jnp.concatenate([jnp.where(first, values, other), jnp.where(first, other, values)], 0)


def transpose_blocks(values):
    return lax.all_to_all(values, "seq", split_axis=0, concat_axis=0, tiled=True)


def spread(values):
    far = swap(values, "chan", 2)
    return [values, swap(values, "chan", 1), far, swap(far, "chan", 1)]


def collect(pieces):
    far = pieces[2] + swap(pieces[3], "chan", 1)
    return [pieces[0], swap(pieces[1], "chan", 1), swap(far, "chan", 2)]


def pack(arrays):
    flat = jnp.concatenate([a.reshape(-1) for a in arrays])
    return jnp.pad(flat, (0, -flat.shape[0] % 1024))


def unpack(flat, arrays):
    out = []
    start = 0
    for a in arrays:
        size = math.prod(a.shape)
        out.append(flat[start : start + size].reshape(a.shape))
        start += size
    return out


def sequence_device(
    block_input,
    lengths,
    ln1_gain,
    ln1_bias,
    input_weight,
    input_bias,
    conv_w,
    conv_b,
    filt_w1,
    filt_b1,
    filt_w2,
    filt_b2,
    filt_w3,
    decay,
    skip,
    output_weight,
    output_bias,
    ln2_gain,
    ln2_bias,
    up_weight,
    up_bias,
    down_weight,
    down_bias,
    cotangent,
):
    blocks, block, model = block_input.shape
    count = lax.axis_size("chan")
    quarter = block // count
    rows = blocks * quarter
    width = decay.shape[0]
    seq_length = blocks * block
    seq_index = lax.axis_index("seq")
    chan_index = lax.axis_index("chan")
    own = chan_index.astype(jnp.int32).reshape(1)
    length = lax.dynamic_slice(lengths, (seq_index,), (1,))
    tables = wave_tables(block)
    row = lambda v: v.reshape(1, -1)

    def own_rows(values):
        part = lax.dynamic_slice_in_dim(values, chan_index * quarter, quarter, 1)
        return transpose_blocks(part)

    place_values = jnp.arange(seq_length, dtype=jnp.int32).astype(F32)
    features = position_features(place_values, seq_length, filt_w1.shape[0])
    kernel, filter_pull = jax.vjp(
        partial(implicit_filter, features, place_values), filt_w1, filt_b1, filt_w2, filt_b2, filt_w3, decay
    )
    k_spec = filter_spectrum(kernel.reshape(blocks, block, width), tables)
    weight = jnp.transpose(input_weight, (1, 0, 2))

    x_own = own_rows(block_input)
    side = (seq_index % 2).astype(jnp.int32)

    def half_of(values, axis):
        half = values.shape[axis] // 2
        return lax.dynamic_slice_in_dim(values, side * half, half, axis)

    up_far = swap(half_of(up_weight, 0), "chan", 2)
    up_bias_parts = [swap(up_bias, "chan", k) if k else up_bias for k in range(count)]
    x_own, k_spec, weight, up_far, up_bias_parts, cotangent_home = meet(
        x_own, k_spec, weight, up_far, up_bias_parts, cotangent
    )
    x_far = swap(x_own, "chan", 2)
    x_parts = [x_own, swap(x_own, "chan", 1), x_far, swap(x_far, "chan", 1)]
    cot_own = own_rows(cotangent_home)
    x_rows = x_own.reshape(rows, model)
    x_parts[2], out_home, down_home, up_far = meet(x_parts[2], output_weight, down_weight, up_far)
    out_far = swap(out_home, "chan", 2)
    down_far = swap(half_of(down_home, 1), "chan", 2)
    up_other = swap(up_far, "seq", 1)
    x_parts[0], cot_own = meet(x_parts[0], cot_own)
    cot_own = cot_own.reshape(rows, model)

    (normed_high, normed_low, proj, conv, s_spec), mixed = mixer_forward(
        own, length, x_parts, row(ln1_gain), row(ln1_bias), weight, input_bias, conv_w, conv_b, row(skip), k_spec, tables
    )
    *mixed, down_far, out_far, up_other = meet(*mixed, down_far, out_far, up_other)
    mixed = [m if k == 0 else swap(m, "chan", k) for k, m in enumerate(mixed)]
    down_other = swap(down_far, "seq", 1)
    out_3 = swap(out_far, "chan", 1)
    *mixed, out_3 = meet(*mixed, out_3)
    out_parts = [output_weight, swap(output_weight, "chan", 1), out_far, out_3]
    up_parts = [[up_weight], [swap(up_weight, "chan", 1)], [up_far, up_other]]
    up_parts.append([swap(u, "chan", 1) for u in up_parts[2]])
    down_parts = [[down_weight], [swap(down_weight, "chan", 1)], [down_far, down_other]]
    down_parts.append([swap(d, "chan", 1) for d in down_parts[2]])
    mixed = [m.reshape(rows, width) for m in mixed]

    hidden, *rest = hidden_forward(
        mixed, out_parts, x_rows, cot_own, row(output_bias), row(ln2_gain), row(ln2_bias)
    )
    normed2, turned, cot_parts = rest[0:2], rest[2:4], rest[4:6]

    def units(k, sums):
        return feed_forward(
            side.reshape(1), normed2, turned, cot_parts, up_parts[k], row(up_bias_parts[k]), down_parts[k], sums
        )

    bias_grads = [None] * count
    sums, (up_3, down_3, bias_grads[3]) = units(3, None)
    up_3, down_3 = swap(up_3, "chan", 1), swap(down_3, "chan", 1)
    sums, (up_2, down_2, bias_grads[2]) = units(2, sums)
    *sums, far_up, far_down = meet(*sums, up_2 + up_3, down_2 + down_3)

    third = model // 3
    half = far_down.shape[0] // 2
    far_ups = [swap(far_up[:third], "chan", 2)]
    leaving, staying = split_rows(far_down, "seq", 1)
    came = [swap(leaving[: half // 2], "seq", 1)]
    sums, (up_1, down_1, bias_grads[1]) = units(1, sums)
    *sums, far_ups[0], came[0], up_1, down_1 = meet(*sums, far_ups[0], came[0], up_1, down_1)
    up_1, down_1 = swap(up_1, "chan", 1), swap(down_1, "chan", 1)
    far_ups.append(swap(far_up[third : 2 * third], "chan", 2))
    came.append(swap(leaving[half // 2 :], "seq", 1))
    sums, (up_0, down_0, bias_grads[0]) = units(0, sums)
    *sums, far_ups[1], far_down, up_1, down_1 = meet(
        *sums, far_ups[1], staying + jnp.concatenate(came, 0), up_1, down_1
    )
    far_ups.append(swap(far_up[2 * third :], "chan", 2))
    leaving, far_staying = split_rows(far_down, "seq", 2)
    far_came = swap(leaving, "seq", 2)
    leaving_0, staying_0 = split_rows(down_0, "seq", 1)
    leaving_1, staying_1 = split_rows(down_1, "seq", 1)
    near_came = swap(leaving_0 + leaving_1, "seq", 1)
    (out_rows, grad_hidden, sums2), grad_mixed, (out_near, out_far) = hidden_backward(
        hidden, sums[0], sums[1], cot_own, mixed, out_parts, row(ln2_gain), row(down_bias)
    )
    grad_hidden, far_ups[2], far_came, grad_mixed, out_rows = meet(
        grad_hidden, far_ups[2], far_came, grad_mixed, out_rows
    )

    grad_mixed = [g.reshape(blocks, quarter, width) for g in grad_mixed]
    grad_mixed = [g if k == 0 else swap(g, "chan", k) for k, g in enumerate(grad_mixed)]
    leaving, far_staying = split_rows(far_staying + far_came, "seq", 4)
    far_came = swap(leaving, "seq", 4)
    out_blocks = transpose_blocks(out_rows.reshape(blocks, quarter, model))
    grad_up = up_0 + up_1 + jnp.concatenate(far_ups, 0)
    grad_mixed, grad_up, out_far, near_came = meet(grad_mixed, grad_up, out_far, near_came)

    up_leaving, up_staying = split_rows(grad_up, "seq", 1)
    up_came = swap(up_leaving, "seq", 1)
    leaving, near_staying = split_rows(staying_0 + staying_1 + near_came, "seq", 2)
    near_came = swap(leaving, "seq", 2)
    out_far = swap(out_far, "chan", 2)
    (g_spec, grad_proj, mixer_sums), grad_normed = mixer_backward(
        own, length, grad_mixed, proj, conv, s_spec, k_spec, conv_w, conv_b, row(skip), weight, tables
    )
    grad_normed, grad_proj, out_far, near_came, up_came, out_blocks, far_came = meet(
        grad_normed, grad_proj, out_far, near_came, up_came, out_blocks, far_came
    )

    grad_normed[3], grad_normed[1] = swap(grad_normed[3], "chan", 1), swap(grad_normed[1], "chan", 1)
    far_down = swap(far_staying + far_came, "chan", 2)
    leaving, near_staying = split_rows(near_staying + near_came, "seq", 4)
    up_leaving, up_staying = split_rows(up_staying + up_came, "seq", 2)
    far_normed, grad_proj, leaving, up_leaving = meet(
        grad_normed[2] + grad_normed[3], grad_proj, leaving, up_leaving
    )
    far_normed = swap(far_normed, "chan", 2)
    near_came, up_came = swap(leaving, "seq", 4), swap(up_leaving, "seq", 2)
    grad_in = input_weight_grad(normed_high, normed_low, grad_proj)
    grad_out = out_near[0] + out_far[0] + swap(out_near[1] + out_far[1], "chan", 1)
    g_spec, grad_in, grad_out, near_came, far_down, up_came = meet(
        g_spec, grad_in, grad_out, near_came, far_down, up_came
    )

    grad_down = near_staying + near_came + far_down
    down_came = swap(grad_down, "seq", 4)
    up_leaving, up_staying = split_rows(up_staying + up_came, "seq", 4)
    up_came = swap(up_leaving, "seq", 4)
    mixer_leaving, mixer_staying = split_rows(
        jnp.concatenate([grad_in.reshape(-1, model), grad_out], 0), "seq", 1
    )
    mixer_came = swap(mixer_leaving, "seq", 1)
    grad_kernel = filter_backward(s_spec, g_spec, tables).reshape(seq_length, width)
    far_normed, grad_kernel, down_came, up_came = meet(far_normed, grad_kernel, down_came, up_came)

    pieces = [p.reshape(rows, model) for p in (grad_normed[0], grad_normed[1], far_normed)]
    grad_x_rows, sums1 = input_backward(pieces, x_rows, grad_hidden, row(ln1_gain))
    grad_x_rows, grad_kernel, out_blocks, mixer_came, down_came, up_came, sums1 = meet(
        grad_x_rows, grad_kernel, out_blocks, mixer_came, down_came, up_came, sums1
    )

    grad_x_blocks = transpose_blocks(grad_x_rows.reshape(blocks, quarter, model))
    leaving, staying = split_rows(mixer_staying + mixer_came, "seq", 2)
    came = swap(leaving, "seq", 2)
    grad_up, grad_down = up_staying + up_came, join_rows(grad_down, down_came, "seq", 4)
    down_came, up_came = swap(grad_down, "seq", 2), swap(grad_up, "seq", 4)
    out_far, out_near = swap(out_blocks, "chan", 2), swap(out_blocks, "chan", 1)
    grad_fw1, grad_fb1, grad_fw2, grad_fb2, grad_fw3, grad_decay = filter_pull(grad_kernel)
    grad_x_blocks, came, up_came, down_came, grad_fw3, out_far, out_near = meet(
        grad_x_blocks, came, up_came, down_came, grad_fw3, out_far, out_near
    )

    grad_x_far = swap(grad_x_blocks, "chan", 2)
    out_side = swap(out_far, "chan", 1)
    leaving, staying = split_rows(staying + came, "seq", 4)
    came = swap(leaving, "seq", 4)
    grad_up, grad_down = join_rows(grad_up, up_came, "seq", 4), join_rows(grad_down, down_came, "seq", 2)
    down_came, up_came = swap(grad_down, "seq", 1), swap(grad_up, "seq", 2)
    up_bias_grads = jnp.take(
        jnp.concatenate(bias_grads, 0), jnp.arange(count, dtype=jnp.int32) ^ chan_index, axis=0
    )
    shared = [sums1[0], sums1[1], *[sums2[i] for i in range(4)], up_bias_grads, grad_fw1, grad_fb1, grad_fw2, grad_fb2]
    split = [mixer_sums, grad_fw3, grad_decay]
    shared_flat, split_flat = pack(shared), pack(split)
    came, up_came, out_side, shared_flat, grad_x_blocks = meet(came, up_came, out_side, shared_flat, grad_x_blocks)

    mixer_grads = staying + came
    came = swap(mixer_grads, "seq", 4)
    grad_up = join_rows(grad_up, up_came, "seq", 2)
    up_came = swap(grad_up, "seq", 1)
    side_flat = swap(shared_flat, "chan", 1)
    output = put_together(own, [out_blocks, out_near, out_far, out_side])
    came, grad_x_far, output, side_flat, grad_x_blocks = meet(came, grad_x_far, output, side_flat, grad_x_blocks)

    mixer_grads = join_rows(mixer_grads, came, "seq", 4)
    came = swap(mixer_grads, "seq", 2)
    grad_x_near, grad_x_side = swap(grad_x_blocks, "chan", 1), swap(grad_x_far, "chan", 1)
    shared_flat = shared_flat + side_flat
    side_flat = swap(shared_flat, "chan", 2)
    came, grad_x_near, grad_x_side, side_flat, up_came, down_came = meet(
        came, grad_x_near, grad_x_side, side_flat, up_came, down_came
    )

    flat = jnp.concatenate([shared_flat + side_flat, split_flat])
    mixer_grads = join_rows(mixer_grads, came, "seq", 2)
    side_flat, came = swap(flat, "seq", 2), swap(mixer_grads, "seq", 1)
    grad_x = put_together(own, [grad_x_blocks, grad_x_near, grad_x_far, grad_x_side])
    grad_down = join_rows(grad_down, down_came, "seq", 1)
    side_flat, grad_x, grad_down = meet(side_flat, grad_x, grad_down)
    flat = flat + side_flat
    flat = flat + swap(flat, "seq", 4)
    flat = flat + swap(flat, "seq", 1)
    mixer_grads = join_rows(mixer_grads, came, "seq", 1)
    grad_up = join_rows(grad_up, up_came, "seq", 1)
    grad_in = jnp.transpose(mixer_grads[: 3 * width].reshape(3, width, model), (2, 0, 1))
    grad_out = mixer_grads[3 * width :]

    cut = shared_flat.shape[0]
    grad_ln1_gain, grad_ln1_bias, grad_ln2_gain, grad_ln2_bias, grad_b_out, grad_b_fc2, up_bias_grads, *filt = unpack(
        flat[:cut], shared
    )
    mixer_sums, grad_fw3, grad_decay = unpack(flat[cut:], split)
    grad_b_fc1 = lax.dynamic_slice_in_dim(up_bias_grads, chan_index, 1, 0)[0]
    grad_skip = mixer_sums[0]
    grad_conv_b = mixer_sums[1:4]
    grad_conv_w = mixer_sums[4:13].reshape(3, 3, width)
    grad_b_in = mixer_sums[13:16]
    return (
        output,
        grad_x,
        grad_ln1_gain,
        grad_ln1_bias,
        grad_in,
        grad_b_in,
        grad_conv_w,
        grad_conv_b,
        *filt,
        grad_fw3,
        grad_decay,
        grad_skip,
        grad_out,
        grad_b_out,
        grad_ln2_gain,
        grad_ln2_bias,
        grad_up,
        grad_b_fc1,
        grad_down,
        grad_b_fc2,
    )


def solution(mesh):
    in_specs = (
        P(None, "seq", None),
        P(),
        P(),
        P(),
        P(None, None, "chan"),
        P(None, "chan"),
        P(None, None, "chan"),
        P(None, "chan"),
        P(),
        P(),
        P(),
        P(),
        P(None, "chan"),
        P("chan"),
        P("chan"),
        P("chan", None),
        P(),
        P(),
        P(),
        P(None, "chan"),
        P("chan"),
        P("chan", None),
        P(),
        P(None, "seq", None),
    )
    out_specs = (
        P(None, "seq", None),
        P(None, "seq", None),
        P(),
        P(),
        P(None, None, "chan"),
        P(None, "chan"),
        P(None, None, "chan"),
        P(None, "chan"),
        P(),
        P(),
        P(),
        P(),
        P(None, "chan"),
        P("chan"),
        P("chan"),
        P("chan", None),
        P(),
        P(),
        P(),
        P(None, "chan"),
        P("chan"),
        P("chan", None),
        P(),
    )
    chan = mesh.shape["chan"]

    def step(*arrays):
        sequences, seq_length = arrays[0].shape[:2]
        whole_sequences = sequences == mesh.shape["seq"] and chan == 4 and seq_length % (64 * sequences) == 0
        body = sequence_device if whole_sequences else spectral_device
        return jax.shard_map(
            body, mesh=mesh, in_specs=in_specs, out_specs=out_specs, check_vma=False
        )(*arrays)

    return step
```

```python
from functools import partial
import math

import jax
import jax.numpy as jnp
import ml_dtypes
import numpy as np
from jax import lax
from jax.experimental import pallas as pl
from jax.experimental.pallas import tpu as pltpu
from jax.sharding import PartitionSpec as P

EPSILON = 1e-05
HIGH_ACCURACY = lax.Precision.HIGHEST


def shifted(block, axis, distance):
    devices = range(lax.axis_size(axis))
    route = [(i - distance, i) for i in devices if i - distance in devices]
    return lax.ppermute(block, axis, route)


def layer_norm(values, gain, offset):
    average = jnp.mean(values, -1, keepdims=True)
    centered = values - average
    variance = jnp.mean(centered * centered, -1, keepdims=True)
    return centered * lax.rsqrt(variance + EPSILON) * gain + offset


def position_features(place_values, seq_length, emb_width):
    band_count = (emb_width - 1) // 2
    frequency = jnp.linspace(0.0001, band_count - 1, band_count).astype(jnp.float32)
    phases = 2.0 * math.pi * place_values[:, None] * frequency[None, :] / seq_length
    return jnp.concatenate(
        [(place_values / (seq_length - 1))[:, None], jnp.cos(phases), -jnp.sin(phases)], 1
    )


def implicit_filter(features, place_values, filt_w1, filt_b1, filt_w2, filt_b2, filt_w3, decay):
    first_layer = jnp.sin(jnp.dot(features, filt_w1, precision=HIGH_ACCURACY) + filt_b1)
    second_layer = jnp.sin(jnp.dot(first_layer, filt_w2, precision=HIGH_ACCURACY) + filt_b2)
    raw_kernel = jnp.dot(second_layer, filt_w3, precision=HIGH_ACCURACY)
    return raw_kernel * jnp.exp(-decay[None, :] * place_values[:, None])


def exact_gelu(values):
    return jax.nn.gelu(values, approximate=False)


def tables(count_rows, count_cols):
    turns = (
        jnp.arange(count_rows, dtype=jnp.int32)[:, None]
        * jnp.arange(count_cols, dtype=jnp.int32)[None, :]
        % count_rows
    )
    phases = turns.astype(jnp.float32) * (2.0 * math.pi / count_rows)
    return (jnp.cos(phases), jnp.sin(phases))


def rotate(cos_tab, sin_tab, real, imag, sign, form):
    first_part = jnp.einsum(form, cos_tab, real, precision=HIGH_ACCURACY)
    second_part = jnp.einsum(form, sin_tab, imag, precision=HIGH_ACCURACY)
    third_part = jnp.einsum(form, cos_tab, imag, precision=HIGH_ACCURACY)
    fourth_part = jnp.einsum(form, sin_tab, real, precision=HIGH_ACCURACY)
    return (first_part - sign * second_part, third_part + sign * fourth_part)


def to_spectrum(cos_tab, sin_tab, signal):
    real = jnp.einsum("wp,spc->swc", cos_tab, signal, precision=HIGH_ACCURACY)
    imag = -jnp.einsum("wp,spc->swc", sin_tab, signal, precision=HIGH_ACCURACY)
    return (real, imag)


def time_domain(cos_tab, sin_tab, real, imag):
    return jnp.einsum("wp,swc->spc", cos_tab, real, precision=HIGH_ACCURACY) - jnp.einsum(
        "wp,swc->spc", sin_tab, imag, precision=HIGH_ACCURACY
    )


def earlier_block(values):
    return jnp.pad(values, ((0, 0), (1, 0), (0, 0), (0, 0)))[:, :-1]


def later_block(values):
    return jnp.pad(values, ((0, 0), (0, 1), (0, 0), (0, 0)))[:, 1:]


def spectral_device(
    block_input,
    lengths,
    ln1_gain,
    ln1_bias,
    input_weight,
    input_bias,
    conv_w,
    conv_b,
    filt_w1,
    filt_b1,
    filt_w2,
    filt_b2,
    filt_w3,
    decay,
    skip,
    output_weight,
    output_bias,
    ln2_gain,
    ln2_bias,
    up_weight,
    up_bias,
    down_weight,
    down_bias,
    cotangent,
):
    block = block_input.shape[1]
    blocks = lax.axis_size("seq")
    share = 2 * block // blocks
    seq_index = lax.axis_index("seq")
    places = seq_index * block + jnp.arange(block, dtype=jnp.int32)
    place_values = places.astype(jnp.float32)
    mask = (places[None, :] < lengths[:, None]).astype(jnp.float32)[:, :, None]
    first_normed, norm1_pull = jax.vjp(layer_norm, block_input, ln1_gain, ln1_bias)
    input_projected = (
        jnp.einsum("spd,dkc->spkc", first_normed, input_weight, precision=HIGH_ACCURACY)
        + input_bias
    )
    rims = shifted(input_projected[:, block - 2 :], "seq", 1)
    extended = jnp.concatenate([rims, input_projected], 1)
    short = (
        conv_w[0] * extended[:, :block]
        + conv_w[1] * extended[:, 1 : block + 1]
        + conv_w[2] * extended[:, 2:]
        + conv_b
    )
    gate_out = short[:, :, 0]
    gate_in = short[:, :, 1]
    values = short[:, :, 2]
    signal = values * gate_in * mask
    cos_tab, sin_tab = tables(2 * block, block)
    block_cos, block_sin = tables(2 * blocks, blocks)
    own_freq = seq_index * share + jnp.arange(share, dtype=jnp.int32)
    parity = (1 - 2 * (own_freq % 2)).astype(jnp.float32)[:, None]
    features = position_features(place_values, blocks * block, filt_w1.shape[0])
    kernel, filter_pull = jax.vjp(
        partial(implicit_filter, features, place_values),
        filt_w1,
        filt_b1,
        filt_w2,
        filt_b2,
        filt_w3,
        decay,
    )
    signal_re, signal_im = to_spectrum(cos_tab, sin_tab, signal)
    kernel_re, kernel_im = to_spectrum(cos_tab, sin_tab, kernel[None])
    signal_re, signal_im, kernel_re, kernel_im = (
        lax.all_to_all(signal_re[:, None], "seq", split_axis=2, concat_axis=1, tiled=True),
        lax.all_to_all(signal_im[:, None], "seq", split_axis=2, concat_axis=1, tiled=True),
        lax.all_to_all(kernel_re[:, None], "seq", split_axis=2, concat_axis=1, tiled=True),
        lax.all_to_all(kernel_im[:, None], "seq", split_axis=2, concat_axis=1, tiled=True),
    )
    zq_re, zq_im = rotate(block_cos, block_sin, signal_re, signal_im, -1.0, "qk,skfc->sqfc")
    hq_re, hq_im = rotate(block_cos, block_sin, kernel_re, kernel_im, -1.0, "qk,skfc->sqfc")
    prod_re = zq_re * hq_re - zq_im * hq_im
    prod_im = zq_re * hq_im + zq_im * hq_re
    joined_re, joined_im = rotate(block_cos, block_sin, prod_re, prod_im, 1.0, "qj,sqfc->sjfc")
    joined_re = joined_re / (2 * blocks)
    joined_im = joined_im / (2 * blocks)
    folded_re = joined_re + parity * earlier_block(joined_re)
    folded_im = joined_im + parity * earlier_block(joined_im)
    folded_re, folded_im = (
        lax.all_to_all(folded_re, "seq", split_axis=1, concat_axis=2, tiled=True),
        lax.all_to_all(folded_im, "seq", split_axis=1, concat_axis=2, tiled=True),
    )
    convolved = time_domain(cos_tab, sin_tab, folded_re[:, 0], folded_im[:, 0]) / (2 * block)
    conv_sum = convolved + skip * signal
    mixer_output = conv_sum * gate_out
    partial_mix = jnp.einsum("spc,cd->spd", mixer_output, output_weight, precision=HIGH_ACCURACY)
    hidden_state = block_input + lax.psum(partial_mix, "chan") + output_bias
    second_normed2 = layer_norm(hidden_state, ln2_gain, ln2_bias)
    before = jnp.einsum("spd,df->spf", second_normed2, up_weight, precision=HIGH_ACCURACY) + up_bias
    active_units, gelu_pull = jax.vjp(exact_gelu, before)
    feed = lax.psum(
        jnp.einsum("spf,fd->spd", active_units, down_weight, precision=HIGH_ACCURACY), "chan"
    )
    output = hidden_state + feed + down_bias
    grad_b_fc2 = jnp.sum(cotangent, (0, 1))
    grad_w_fc2 = jnp.einsum("spf,spd->fd", active_units, cotangent, precision=HIGH_ACCURACY)
    grad_active = jnp.einsum("spd,fd->spf", cotangent, down_weight, precision=HIGH_ACCURACY)
    grad_before = gelu_pull(grad_active)[0]
    grad_w_fc1 = jnp.einsum("spd,spf->df", second_normed2, grad_before, precision=HIGH_ACCURACY)
    grad_b_fc1 = jnp.sum(grad_before, (0, 1))
    grad_normed2 = lax.psum(
        jnp.einsum("spf,df->spd", grad_before, up_weight, precision=HIGH_ACCURACY), "chan"
    )
    norm2_pull = jax.vjp(layer_norm, hidden_state, ln2_gain, ln2_bias)[1]
    grad_hidden_norm, grad_ln2_gain, grad_ln2_bias = norm2_pull(grad_normed2)
    grad_hidden = cotangent + grad_hidden_norm
    grad_b_out = jnp.sum(grad_hidden, (0, 1))
    grad_w_out = jnp.einsum("spc,spd->cd", mixer_output, grad_hidden, precision=HIGH_ACCURACY)
    grad_mixed = jnp.einsum("spd,cd->spc", grad_hidden, output_weight, precision=HIGH_ACCURACY)
    grad_conv = grad_mixed * gate_out
    grad_gate_out = grad_mixed * conv_sum
    grad_skip = jnp.sum(grad_conv * signal, (0, 1))
    back_re, back_im = to_spectrum(cos_tab, sin_tab, grad_conv)
    back_re = back_re / (2 * block)
    back_im = back_im / (2 * block)
    back_re, back_im = (
        lax.all_to_all(back_re[:, None], "seq", split_axis=2, concat_axis=1, tiled=True),
        lax.all_to_all(back_im[:, None], "seq", split_axis=2, concat_axis=1, tiled=True),
    )
    unfold_re = back_re + parity * later_block(back_re)
    unfold_im = back_im + parity * later_block(back_im)
    dprod_re, dprod_im = rotate(block_cos, block_sin, unfold_re, unfold_im, -1.0, "qj,sjfc->sqfc")
    dprod_re = dprod_re / (2 * blocks)
    dprod_im = dprod_im / (2 * blocks)
    dzq_re = hq_re * dprod_re + hq_im * dprod_im
    dzq_im = hq_re * dprod_im - hq_im * dprod_re
    dhq_re = jnp.sum(zq_re * dprod_re + zq_im * dprod_im, 0, keepdims=True)
    dhq_im = jnp.sum(zq_re * dprod_im - zq_im * dprod_re, 0, keepdims=True)
    dsig_re, dsig_im = rotate(block_cos, block_sin, dzq_re, dzq_im, 1.0, "qk,sqfc->skfc")
    dker_re, dker_im = rotate(block_cos, block_sin, dhq_re, dhq_im, 1.0, "qk,sqfc->skfc")
    dsig_re, dsig_im, dker_re, dker_im = (
        lax.all_to_all(dsig_re, "seq", split_axis=1, concat_axis=2, tiled=True),
        lax.all_to_all(dsig_im, "seq", split_axis=1, concat_axis=2, tiled=True),
        lax.all_to_all(dker_re, "seq", split_axis=1, concat_axis=2, tiled=True),
        lax.all_to_all(dker_im, "seq", split_axis=1, concat_axis=2, tiled=True),
    )
    grad_signal = time_domain(cos_tab, sin_tab, dsig_re[:, 0], dsig_im[:, 0]) + grad_conv * skip
    grad_kernel = time_domain(cos_tab, sin_tab, dker_re[:, 0], dker_im[:, 0])[0]
    grad_fw1, grad_fb1, grad_fw2, grad_fb2, grad_fw3, grad_decay = filter_pull(grad_kernel)
    grad_short = jnp.stack(
        [grad_gate_out, grad_signal * values * mask, grad_signal * gate_in * mask], 2
    )
    grad_conv_b = jnp.sum(grad_short, (0, 1))
    grad_conv_w = jnp.stack(
        [jnp.sum(grad_short * extended[:, offset : offset + block], (0, 1)) for offset in range(3)]
    )
    grad_extended = (
        jnp.pad(conv_w[0] * grad_short, ((0, 0), (0, 2), (0, 0), (0, 0)))
        + jnp.pad(conv_w[1] * grad_short, ((0, 0), (1, 1), (0, 0), (0, 0)))
        + jnp.pad(conv_w[2] * grad_short, ((0, 0), (2, 0), (0, 0), (0, 0)))
    )
    returned = shifted(grad_extended[:, :2], "seq", -1)
    grad_proj = grad_extended[:, 2:] + jnp.pad(returned, ((0, 0), (block - 2, 0), (0, 0), (0, 0)))
    grad_b_in = jnp.sum(grad_proj, (0, 1))
    grad_w_in = jnp.einsum("spd,spkc->dkc", first_normed, grad_proj, precision=HIGH_ACCURACY)
    grad_normed = lax.psum(
        jnp.einsum("spkc,dkc->spd", grad_proj, input_weight, precision=HIGH_ACCURACY), "chan"
    )
    grad_x_norm, grad_ln1_gain, grad_ln1_bias = norm1_pull(grad_normed)
    grad_x = grad_hidden + grad_x_norm
    (
        grad_ln1_gain,
        grad_ln1_bias,
        grad_w_in,
        grad_b_in,
        grad_conv_w,
        grad_conv_b,
        grad_fw3,
        grad_decay,
        grad_skip,
        grad_w_out,
        grad_b_out,
        grad_ln2_gain,
        grad_ln2_bias,
        grad_w_fc1,
        grad_b_fc1,
        grad_w_fc2,
        grad_b_fc2,
    ) = lax.psum(
        (
            grad_ln1_gain,
            grad_ln1_bias,
            grad_w_in,
            grad_b_in,
            grad_conv_w,
            grad_conv_b,
            grad_fw3,
            grad_decay,
            grad_skip,
            grad_w_out,
            grad_b_out,
            grad_ln2_gain,
            grad_ln2_bias,
            grad_w_fc1,
            grad_b_fc1,
            grad_w_fc2,
            grad_b_fc2,
        ),
        "seq",
    )
    grad_fw1, grad_fb1, grad_fw2, grad_fb2 = lax.psum(
        (grad_fw1, grad_fb1, grad_fw2, grad_fb2), ("seq", "chan")
    )
    return (
        output,
        grad_x,
        grad_ln1_gain,
        grad_ln1_bias,
        grad_w_in,
        grad_b_in,
        grad_conv_w,
        grad_conv_b,
        grad_fw1,
        grad_fb1,
        grad_fw2,
        grad_fb2,
        grad_fw3,
        grad_decay,
        grad_skip,
        grad_w_out,
        grad_b_out,
        grad_ln2_gain,
        grad_ln2_bias,
        grad_w_fc1,
        grad_b_fc1,
        grad_w_fc2,
        grad_b_fc2,
    )


F32 = jnp.float32
BF16 = jnp.bfloat16
NN = (((1,), (0,)), ((), ()))
NT = (((1,), (1,)), ((), ()))
TN = (((0,), (0,)), ((), ()))
VMEM_BYTES = 56 * 2**20


def parts_of(values):
    high = values.astype(BF16)
    return high, (values - high.astype(F32)).astype(BF16)


def dot_parts(left, right, dims):
    def one(a, b):
        return lax.dot_general(a, b, dims, preferred_element_type=F32)

    return one(left[0], right[0]) + (one(left[0], right[1]) + one(left[1], right[0]))


def normalise(values):
    average = jnp.mean(values, -1, keepdims=True)
    centered = values - average
    variance = jnp.mean(centered * centered, -1, keepdims=True)
    scale = lax.rsqrt(variance + EPSILON)
    return centered * scale, scale


def norm_back(unit, scale, gain, grad):
    lifted = grad * gain
    mean_one = jnp.mean(lifted, -1, keepdims=True)
    mean_two = jnp.mean(lifted * unit, -1, keepdims=True)
    return scale * (lifted - mean_one - unit * mean_two)


def fold(rows):
    half = rows.shape[0] // 2
    return jnp.concatenate([rows[:half], rows[half:]], 1)


def unfold(folded):
    width = folded.shape[1] // 2
    return jnp.concatenate([folded[:, :width], folded[:, width:]], 0)


def column_sum(values):
    return jnp.sum(values, 0, keepdims=True)


def whole(array):
    return pl.BlockSpec(array.shape, lambda *_: (0,) * len(array.shape))


def scalar_spec():
    return pl.BlockSpec(memory_space=pltpu.SMEM)


def struct(shape, kind=F32):
    return jax.ShapeDtypeStruct(tuple(shape), kind)


def run_kernel(body, name, grid, in_specs, out_specs, out_shape, scratch, args, micros):
    return pl.pallas_call(
        body,
        name=name,
        grid=grid,
        in_specs=in_specs,
        out_specs=out_specs,
        out_shape=out_shape,
        scratch_shapes=scratch,
        compiler_params=pltpu.CompilerParams(
            dimension_semantics=("arbitrary",) * len(grid), vmem_limit_bytes=VMEM_BYTES
        ),
        cost_estimate=pl.CostEstimate(
            flops=int(micros * 1.15e9), bytes_accessed=int(micros * 3.6e6), transcendentals=0
        ),
    )(*args)


def wave_tables(block):
    angles = np.pi * np.outer(2 * np.arange(block) + 1, np.arange(block)) / (2 * block)
    table = np.concatenate([np.cos(angles), -np.sin(angles)], 0)

    def both(values):
        high = values.astype(ml_dtypes.bfloat16)
        low = (values - high.astype(np.float64)).astype(ml_dtypes.bfloat16)
        return jnp.asarray(high), jnp.asarray(low)

    return both(table) + both(table.T / block)


def parity_of(rows):
    odd = lax.broadcasted_iota(jnp.int32, (rows, 1), 0) % 2
    return (1 - 2 * odd).astype(F32)


def filter_spectrum(kernel, tables):
    blocks, block, width = kernel.shape
    table_high, table_low = tables[:2]

    def body(kernel_ref, high_ref, low_ref, out_ref, before_ref):
        @pl.when(pl.program_id(0) == 0)
        def _():
            before_ref[...] = jnp.zeros_like(before_ref)

        spectrum = dot_parts((high_ref[...], low_ref[...]), parts_of(kernel_ref[0]), NN)
        sign = parity_of(block)
        out_ref[0, :block] = spectrum[:block] - sign * before_ref[block:]
        out_ref[0, block:] = spectrum[block:] + sign * before_ref[:block]
        before_ref[...] = spectrum

    return run_kernel(
        body,
        "filter_spectrum",
        (blocks,),
        [pl.BlockSpec((1, block, width), lambda b: (b, 0, 0)), whole(table_high), whole(table_low)],
        [pl.BlockSpec((1, 2 * block, width), lambda b: (b, 0, 0))],
        [struct((blocks, 2 * block, width))],
        [pltpu.VMEM((2 * block, width), F32)],
        [kernel, table_high, table_low],
        8,
    )[0]


def mixer_forward(own, length, x_parts, gain, offset, weight, bias, conv_w, conv_b, skip, spectrum, tables):
    blocks, quarter, model = x_parts[0].shape
    count = len(x_parts)
    block = quarter * count
    width = weight.shape[2]
    tile = min(32, block)
    pair = 2 - blocks % 2
    span = pair * block

    def body(*refs):
        own_ref, length_ref = refs[:2]
        x_refs = refs[2 : 2 + count]
        refs = refs[2 + count :]
        gain_ref, offset_ref, weight_ref, bias_ref, conv_w_ref, conv_b_ref, skip_ref, k_ref = refs[:8]
        th_ref, tl_ref, ih_ref, il_ref = refs[8:12]
        nh_ref, nl_ref, proj_ref, conv_ref, s_ref = refs[12:17]
        m_refs = refs[17 : 17 + count]
        wh_ref, wl_ref, ext_ref, o_ref, mixed_ref = refs[17 + count :]
        step = pl.program_id(0)
        me = own_ref[0]

        @pl.when(step == 0)
        def _():
            for k in range(3):
                wh_ref[k], wl_ref[k] = parts_of(weight_ref[k])
            ext_ref[:, :8] = jnp.zeros((3, 8, width), F32)

        for u in range(pair):
            for k in range(count):
                normed = normalise(x_refs[k][u])[0] * gain_ref[...] + offset_ref[...]
                start = pl.multiple_of(u * block + (me ^ k) * quarter, quarter)
                high, low = parts_of(normed)
                nh_ref[0, pl.ds(start, quarter), :] = high
                nl_ref[0, pl.ds(start, quarter), :] = low
        normed = (nh_ref[0], nl_ref[0])
        short = []
        for k in range(3):
            proj = dot_parts(normed, (wh_ref[k], wl_ref[k]), NN) + bias_ref[k : k + 1, :]
            proj_ref[0, k] = proj
            ext_ref[k, 8:] = proj
            short.append(
                conv_w_ref[0, k : k + 1, :] * ext_ref[k, 6 : 6 + span]
                + conv_w_ref[1, k : k + 1, :] * ext_ref[k, 7 : 7 + span]
                + conv_w_ref[2, k : k + 1, :] * proj
                + conv_b_ref[k : k + 1, :]
            )
            ext_ref[k, :8] = ext_ref[k, span:]
        places = step * span + lax.broadcasted_iota(jnp.int32, (span, 1), 0)
        mask = (places < length_ref[0]).astype(F32)
        signal = short[2] * short[1] * mask
        for u in range(pair):
            part = signal[u * block : (u + 1) * block]
            s_ref[step * pair + u] = dot_parts((th_ref[...], tl_ref[...]), parts_of(part), NN)
        for u in range(pair):
            b = step * pair + u
            for r in range(0, block, tile):
                lo = slice(r, r + tile)
                hi = slice(block + r, block + r + tile)

                def product(i, total, b=b, lo=lo, hi=hi):
                    s_re, s_im = s_ref[i, lo], s_ref[i, hi]
                    k_re, k_im = k_ref[b - i, lo], k_ref[b - i, hi]
                    return total[0] + s_re * k_re - s_im * k_im, total[1] + s_re * k_im + s_im * k_re

                zero = jnp.zeros((tile, width), F32)
                o_ref[u, lo], o_ref[u, hi] = lax.fori_loop(0, b + 1, product, (zero, zero))
        inverse = (ih_ref[...], il_ref[...])
        conv = jnp.concatenate([dot_parts(inverse, parts_of(o_ref[u]), NN) for u in range(pair)], 0)
        conv = conv + skip_ref[...] * signal
        conv_ref[0] = conv
        mixed_ref[...] = conv * short[0]
        for u in range(pair):
            for k in range(count):
                start = pl.multiple_of(u * block + (me ^ k) * quarter, quarter)
                m_refs[k][u] = fold(mixed_ref[pl.ds(start, quarter), :])

    by_block = lambda *shape: pl.BlockSpec((1,) + shape, lambda b: (b,) + (0,) * len(shape))
    args = [own, length, *x_parts, gain, offset, weight, bias, conv_w, conv_b, skip, spectrum, *tables]
    by_pair = lambda n: pl.BlockSpec((pair, quarter, n), lambda b: (b, 0, 0))
    in_specs = [scalar_spec(), scalar_spec()] + [by_pair(model)] * count
    in_specs += [whole(a) for a in args[2 + count :]]
    folded = pl.BlockSpec((pair, quarter // 2, 2 * width), lambda b: (b, 0, 0))
    s_shape = struct((blocks, 2 * block, width))
    outs = run_kernel(
        body,
        "mixer_forward",
        (blocks // pair,),
        in_specs,
        [by_block(span, model)] * 2
        + [by_block(3, span, width), by_block(span, width), whole(s_shape)]
        + [folded] * count,
        [struct((blocks // pair, span, model), BF16)] * 2
        + [struct((blocks // pair, 3, span, width)), struct((blocks // pair, span, width)), s_shape]
        + [struct((blocks, quarter // 2, 2 * width))] * count,
        [
            pltpu.VMEM((3, model, width), BF16),
            pltpu.VMEM((3, model, width), BF16),
            pltpu.VMEM((3, span + 8, width), F32),
            pltpu.VMEM((pair, 2 * block, width), F32),
            pltpu.VMEM((span, width), F32),
        ],
        args,
        36,
    )
    return outs[:5], list(outs[5:])


def hidden_forward(m_parts, weights, x_own, cotangent, bias, gain, offset):
    blocks, half, width = m_parts[0].shape
    rows, model = x_own.shape
    width = width // 2
    count = len(m_parts)
    group = math.gcd(blocks, max(128 // half, 1))
    step = 2 * half * group

    def body(*refs):
        m_refs, w_refs = refs[:count], refs[count : 2 * count]
        x_ref, c_ref, bias_ref, gain_ref, offset_ref = refs[2 * count : 2 * count + 5]
        h_ref, nh_ref, nl_ref, th_ref, tl_ref, ch_ref, cl_ref = refs[2 * count + 5 : 2 * count + 12]
        wh_ref, wl_ref = refs[2 * count + 12 :]

        @pl.when(pl.program_id(0) == 0)
        def _():
            for k in range(count):
                wh_ref[k], wl_ref[k] = parts_of(w_refs[k][...])

        hidden = x_ref[...] + bias_ref[...]
        for k in range(count):
            mixed = jnp.concatenate([unfold(m_refs[k][u]) for u in range(group)], 0)
            hidden = hidden + dot_parts(parts_of(mixed), (wh_ref[k], wl_ref[k]), NN)
        h_ref[...] = hidden
        normed = normalise(hidden)[0] * gain_ref[...] + offset_ref[...]
        nh_ref[...], nl_ref[...] = parts_of(normed)
        th_ref[...], tl_ref[...] = parts_of(normed.T)
        ch_ref[...], cl_ref[...] = parts_of(c_ref[...])

    row_spec = lambda n: pl.BlockSpec((step, n), lambda r: (r, 0))
    turned = pl.BlockSpec((model, step), lambda r: (0, r))
    args = [*m_parts, *weights, x_own, cotangent, bias, gain, offset]
    return run_kernel(
        body,
        "hidden_forward",
        (rows // step,),
        [pl.BlockSpec((group, half, 2 * width), lambda r: (r, 0, 0))] * count
        + [whole(w) for w in weights]
        + [row_spec(model)] * 2
        + [whole(bias), whole(gain), whole(offset)],
        [row_spec(model)] * 3 + [turned] * 2 + [row_spec(model)] * 2,
        [struct((rows, model))]
        + [struct((rows, model), BF16)] * 2
        + [struct((model, rows), BF16)] * 2
        + [struct((rows, model), BF16)] * 2,
        [pltpu.VMEM((count, width, model), BF16)] * 2,
        args,
        9,
    )


def feed_forward(side, normed, turned, cotangent, up, up_bias, down, sums):
    rows, model = normed[0].shape
    units = up_bias.shape[1]
    step = min(256, units)
    first = sums is None
    pieces = len(up)

    def body(side_ref, *refs):
        nh_ref, nl_ref, th_ref, tl_ref, ch_ref, cl_ref, bias_ref = refs[:7]
        up_refs, down_refs = refs[7 : 7 + pieces], refs[7 + pieces : 7 + 2 * pieces]
        refs = refs[7 + 2 * pieces :]
        feed_in, grad_in = (None, None) if first else refs[:2]
        feed_ref, grad_ref, gup_ref, gdown_ref, gbias_ref = refs[0 if first else 2 :]

        @pl.when(pl.program_id(0) == 0)
        def _():
            if first:
                feed_ref[...] = jnp.zeros_like(feed_ref)
                grad_ref[...] = jnp.zeros_like(grad_ref)
            else:
                feed_ref[...] = feed_in[...]
                grad_ref[...] = grad_in[...]

        def in_order(halves, axis):
            if pieces == 1:
                return halves[0][...]
            mine, other = halves[0][...], halves[1][...]
            low = side_ref[0] == 0
            return jnp.concatenate([jnp.where(low, mine, other), jnp.where(low, other, mine)], axis)

        own_normed = (nh_ref[...], nl_ref[...])
        own_cotangent = (ch_ref[...], cl_ref[...])
        up_parts = parts_of(in_order(up_refs, 0))
        down_parts = parts_of(in_order(down_refs, 1))
        before = dot_parts(own_normed, up_parts, NN) + bias_ref[...]
        grad_active = dot_parts(own_cotangent, down_parts, NT)
        below = 0.5 + 0.5 * lax.erf(before * math.sqrt(0.5))
        slope = below + before * (jnp.exp(-0.5 * before * before) * (1.0 / math.sqrt(2.0 * math.pi)))
        active = before * below
        grad_before = grad_active * slope
        gbias_ref[...] = column_sum(grad_before)
        active_parts = parts_of(active)
        grad_parts = parts_of(grad_before)
        feed_ref[...] += dot_parts(active_parts, down_parts, NN)
        grad_ref[...] += dot_parts(grad_parts, up_parts, NT)
        gup_ref[...] = dot_parts((th_ref[...], tl_ref[...]), grad_parts, NN)
        gdown_ref[...] = dot_parts(active_parts, own_cotangent, TN)

    total = struct((rows, model))
    args = [side, *normed, *turned, *cotangent, up_bias, *up, *down] + ([] if first else list(sums))
    columns = lambda n: pl.BlockSpec((n, step), lambda t: (0, t))
    some_rows = lambda n: pl.BlockSpec((step, n), lambda t: (t, 0))
    outs = run_kernel(
        body,
        "feed_forward",
        (units // step,),
        [scalar_spec()]
        + [whole(a) for a in args[1:7]]
        + [columns(1)]
        + [columns(model // pieces)] * pieces
        + [some_rows(model // pieces)] * pieces
        + [whole(a) for a in args[8 + 2 * pieces :]],
        [whole(total), whole(total), columns(model), some_rows(model), columns(1)],
        [total, total, struct((model, units)), struct((units, model)), struct(up_bias.shape)],
        [],
        args,
        18,
    )
    return outs[:2], outs[2:]


def hidden_backward(hidden, feed, grad_normed, cotangent, m_parts, weights, gain, bias):
    rows, model = hidden.shape
    blocks, half, width = m_parts[0].shape
    width = width // 2
    count = len(m_parts)
    group = math.gcd(blocks, max(128 // half, 1))
    step = 2 * half * group

    def body(*refs):
        h_ref, f_ref, g_ref, c_ref = refs[:4]
        m_refs, w_refs = refs[4 : 4 + count], refs[4 + count : 4 + 2 * count]
        gain_ref, bias_ref, out_ref, gh_ref, sum_ref = refs[4 + 2 * count : 9 + 2 * count]
        gm_refs, refs = refs[9 + 2 * count : 9 + 3 * count], refs[9 + 3 * count :]
        gw_refs, (wh_ref, wl_ref) = refs[:2], refs[2:]

        @pl.when(pl.program_id(0) == 0)
        def _():
            sum_ref[...] = jnp.zeros_like(sum_ref)
            for k in range(count):
                wh_ref[k], wl_ref[k] = parts_of(w_refs[k][...])
            for k in range(2):
                gw_refs[k][...] = jnp.zeros_like(gw_refs[k])

        hidden_rows, grad, above = h_ref[...], g_ref[...], c_ref[...]
        out_ref[...] = hidden_rows + f_ref[...] + bias_ref[...]
        unit, scale = normalise(hidden_rows)
        grad_hidden = above + norm_back(unit, scale, gain_ref[...], grad)
        gh_ref[...] = grad_hidden
        sum_ref[0:1] += column_sum(grad * unit)
        sum_ref[1:2] += column_sum(grad)
        sum_ref[2:3] += column_sum(grad_hidden)
        sum_ref[3:4] += column_sum(above)
        parts = parts_of(grad_hidden)
        for k in range(count):
            grad_mixed = dot_parts(parts, (wh_ref[k], wl_ref[k]), NT)
            for u in range(group):
                gm_refs[k][u] = fold(grad_mixed[u * 2 * half : (u + 1) * 2 * half])
            mixed = jnp.concatenate([unfold(m_refs[k][u]) for u in range(group)], 0)
            gw_refs[k // 2][k % 2] += dot_parts(parts_of(mixed), parts, TN)

    folded = pl.BlockSpec((group, half, 2 * width), lambda r: (r, 0, 0))
    row_spec = lambda n: pl.BlockSpec((step, n), lambda r: (r, 0))
    args = [hidden, feed, grad_normed, cotangent, *m_parts, *weights, gain, bias]
    sums, pair = struct((8, model)), struct((2, width, model))
    outs = run_kernel(
        body,
        "hidden_backward",
        (rows // step,),
        [row_spec(model)] * 4 + [folded] * count + [whole(w) for w in weights] + [whole(gain), whole(bias)],
        [row_spec(model)] * 2
        + [whole(sums)]
        + [folded] * count
        + [whole(pair)] * 2,
        [struct((rows, model))] * 2 + [sums] + [struct((blocks, half, 2 * width))] * count + [pair] * 2,
        [pltpu.VMEM((count, width, model), BF16)] * 2,
        args,
        15,
    )
    return outs[:3], list(outs[3 : 3 + count]), outs[3 + count :]


def mixer_backward(own, length, gm_parts, proj, conv, s_spec, k_spec, conv_w, conv_b, skip, weight, tables):
    blocks, quarter, width = gm_parts[0].shape
    quarter, width = 2 * quarter, width // 2
    count = len(gm_parts)
    block = quarter * count
    model = weight.shape[1]
    tile = min(32, block)
    pair = 2 - blocks % 2
    span = pair * block

    def body(*refs):
        own_ref, length_ref = refs[:2]
        gm_refs = refs[2 : 2 + count]
        refs = refs[2 + count :]
        proj_ref, rim_ref, conv_ref, k_ref, conv_w_ref, conv_b_ref, skip_ref, weight_ref = refs[:8]
        th_ref, tl_ref, ih_ref, il_ref = refs[8:12]
        g_ref, gp_ref, sum_ref = refs[12:15]
        gn_refs = refs[15 : 15 + count]
        wh_ref, wl_ref, ext_ref, gs_ref, o_ref, rows_ref, gn_ref = refs[15 + count :]
        step = pl.program_id(0)
        slot = blocks // pair - 1 - step
        me = own_ref[0]

        @pl.when(step == 0)
        def _():
            for k in range(3):
                wh_ref[k], wl_ref[k] = parts_of(weight_ref[k])
            gs_ref[:, span:] = jnp.zeros((3, 8, width), F32)
            sum_ref[...] = jnp.zeros_like(sum_ref)

        for u in range(pair):
            for k in range(count):
                start = pl.multiple_of(u * block + (me ^ k) * quarter, quarter)
                rows_ref[pl.ds(start, quarter), :] = unfold(gm_refs[k][u])
        inside = (slot > 0).astype(F32)
        short = []
        for k in range(3):
            ext_ref[k, :8] = rim_ref[0, k] * inside
            ext_ref[k, 8:] = proj_ref[0, k]
            short.append(
                conv_w_ref[0, k : k + 1, :] * ext_ref[k, 6 : 6 + span]
                + conv_w_ref[1, k : k + 1, :] * ext_ref[k, 7 : 7 + span]
                + conv_w_ref[2, k : k + 1, :] * proj_ref[0, k]
                + conv_b_ref[k : k + 1, :]
            )
        places = slot * span + lax.broadcasted_iota(jnp.int32, (span, 1), 0)
        mask = (places < length_ref[0]).astype(F32)
        gate_in, values = short[1] * mask, short[2] * mask
        grad_mixed = rows_ref[...]
        grad_conv = grad_mixed * short[0]
        gs_ref[0, :span] = grad_mixed * conv_ref[0]
        for u in range(pair):
            part = grad_conv[u * block : (u + 1) * block]
            g_ref[slot * pair + u] = dot_parts((th_ref[...], tl_ref[...]), parts_of(part), NN)
        for u in range(pair):
            b = slot * pair + u
            for r in range(0, block, tile):
                lo = slice(r, r + tile)
                hi = slice(block + r, block + r + tile)

                def product(j, total, b=b, lo=lo, hi=hi):
                    g_re, g_im = g_ref[j, lo], g_ref[j, hi]
                    k_re, k_im = k_ref[j - b, lo], k_ref[j - b, hi]
                    return total[0] + g_re * k_re + g_im * k_im, total[1] + g_im * k_re - g_re * k_im

                zero = jnp.zeros((tile, width), F32)
                o_ref[u, lo], o_ref[u, hi] = lax.fori_loop(b, blocks, product, (zero, zero))
        inverse = (ih_ref[...], il_ref[...])
        grad_signal = jnp.concatenate([dot_parts(inverse, parts_of(o_ref[u]), NN) for u in range(pair)], 0)
        grad_signal = grad_signal + skip_ref[...] * grad_conv
        gs_ref[1, :span] = grad_signal * values
        gs_ref[2, :span] = grad_signal * gate_in
        sum_ref[0:1] += column_sum(grad_conv * short[2] * gate_in)
        normed_grad = jnp.zeros((span, model), F32)
        for k in range(3):
            grad_short = gs_ref[k, :span]
            sum_ref[1 + k : 2 + k] += column_sum(grad_short)
            for t in range(3):
                row = 4 + 3 * t + k
                sum_ref[row : row + 1] += column_sum(grad_short * ext_ref[k, 6 + t : 6 + t + span])
            grad_proj = (
                conv_w_ref[2, k : k + 1, :] * grad_short
                + conv_w_ref[1, k : k + 1, :] * gs_ref[k, 1 : 1 + span]
                + conv_w_ref[0, k : k + 1, :] * gs_ref[k, 2 : 2 + span]
            )
            sum_ref[13 + k : 14 + k] += column_sum(grad_proj)
            gp_ref[0, k] = grad_proj
            normed_grad = normed_grad + dot_parts(parts_of(grad_proj), (wh_ref[k], wl_ref[k]), NT)
            gs_ref[k, span:] = gs_ref[k, :8]
        gn_ref[...] = normed_grad
        for u in range(pair):
            for k in range(count):
                start = pl.multiple_of(u * block + (me ^ k) * quarter, quarter)
                gn_refs[k][u] = gn_ref[pl.ds(start, quarter), :]

    last = blocks // pair - 1
    by_block = lambda *shape: pl.BlockSpec((1,) + shape, lambda s: (last - s,) + (0,) * len(shape))
    rim = pl.BlockSpec((1, 3, 8, width), lambda s: (jnp.maximum(last - s - 1, 0), 0, span // 8 - 1, 0))
    by_pair = lambda n: pl.BlockSpec((pair, quarter, n), lambda s: (last - s, 0, 0))
    fixed = [k_spec, conv_w, conv_b, skip, weight, *tables]
    spectra = struct((blocks, 2 * block, width))
    sums = struct((16, width))
    outs = run_kernel(
        body,
        "mixer_backward",
        (blocks // pair,),
        [scalar_spec(), scalar_spec()]
        + [pl.BlockSpec((pair, quarter // 2, 2 * width), lambda s: (last - s, 0, 0))] * count
        + [by_block(3, span, width), rim, by_block(span, width)]
        + [whole(a) for a in fixed],
        [whole(spectra), by_block(3, span, width), whole(sums)] + [by_pair(model)] * count,
        [spectra, struct((blocks // pair, 3, span, width)), sums] + [struct((blocks, quarter, model))] * count,
        [
            pltpu.VMEM((3, model, width), BF16),
            pltpu.VMEM((3, model, width), BF16),
            pltpu.VMEM((3, span + 8, width), F32),
            pltpu.VMEM((3, span + 8, width), F32),
            pltpu.VMEM((pair, 2 * block, width), F32),
            pltpu.VMEM((span, width), F32),
            pltpu.VMEM((span, model), F32),
        ],
        [own, length, *gm_parts, proj, proj, conv, *fixed],
        35,
    )
    return outs[:3], list(outs[3:])


def filter_backward(s_spec, g_spec, tables):
    blocks, double, width = s_spec.shape
    block = double // 2
    tile = min(32, block)
    inverse = tables[2:]

    def body(s_ref, g_ref, ih_ref, il_ref, out_ref, after_ref, o_ref):
        m = blocks - 1 - pl.program_id(0)

        @pl.when(m == blocks - 1)
        def _():
            after_ref[...] = jnp.zeros_like(after_ref)

        sign = parity_of(tile)
        for r in range(0, block, tile):
            lo = slice(r, r + tile)
            hi = slice(block + r, block + r + tile)

            def product(j, total, lo=lo, hi=hi):
                g_re, g_im = g_ref[j, lo], g_ref[j, hi]
                s_re, s_im = s_ref[j - m, lo], s_ref[j - m, hi]
                return total[0] + g_re * s_re + g_im * s_im, total[1] + g_im * s_re - g_re * s_im

            zero = jnp.zeros((tile, width), F32)
            re, im = lax.fori_loop(m, blocks, product, (zero, zero))
            o_ref[lo] = re + sign * after_ref[hi]
            o_ref[hi] = im - sign * after_ref[lo]
            after_ref[lo], after_ref[hi] = re, im
        out_ref[0] = dot_parts((ih_ref[...], il_ref[...]), parts_of(o_ref[...]), NN)

    return run_kernel(
        body,
        "filter_backward",
        (blocks,),
        [whole(s_spec), whole(g_spec), whole(inverse[0]), whole(inverse[1])],
        [pl.BlockSpec((1, block, width), lambda s: (blocks - 1 - s, 0, 0))],
        [struct((blocks, block, width))],
        [pltpu.VMEM((double, width), F32)] * 2,
        [s_spec, g_spec, *inverse],
        13,
    )[0]


def input_weight_grad(normed_high, normed_low, grad_proj):
    blocks, block, model = normed_high.shape
    width = grad_proj.shape[3]

    def body(nh_ref, nl_ref, gp_ref, out_ref):
        @pl.when(pl.program_id(0) == 0)
        def _():
            out_ref[...] = jnp.zeros_like(out_ref)

        normed = (nh_ref[0], nl_ref[0])
        for k in range(3):
            out_ref[k] += dot_parts(parts_of(gp_ref[0, k]), normed, TN)

    by_block = lambda *shape: pl.BlockSpec((1,) + shape, lambda b: (b,) + (0,) * len(shape))
    out = struct((3, width, model))
    return run_kernel(
        body,
        "input_weight_grad",
        (blocks,),
        [by_block(block, model)] * 2 + [by_block(3, block, width)],
        [whole(out)],
        [out],
        [],
        [normed_high, normed_low, grad_proj],
        12,
    )[0]


def input_backward(grad_pieces, x_own, grad_hidden, gain):
    rows, model = x_own.shape
    count = len(grad_pieces)
    step = min(256, rows)

    def body(*refs):
        piece_refs = refs[:count]
        x_ref, gh_ref, gain_ref, out_ref, sum_ref = refs[count:]

        @pl.when(pl.program_id(0) == 0)
        def _():
            sum_ref[...] = jnp.zeros_like(sum_ref)

        grad = sum(r[...] for r in piece_refs)
        unit, scale = normalise(x_ref[...])
        out_ref[...] = gh_ref[...] + norm_back(unit, scale, gain_ref[...], grad)
        sum_ref[0:1] += column_sum(grad * unit)
        sum_ref[1:2] += column_sum(grad)

    row_spec = pl.BlockSpec((step, model), lambda r: (r, 0))
    sums = struct((8, model))
    return run_kernel(
        body,
        "input_backward",
        (rows // step,),
        [row_spec] * (count + 2) + [whole(gain)],
        [row_spec, whole(sums)],
        [struct((rows, model)), sums],
        [],
        [*grad_pieces, x_own, grad_hidden, gain],
        5,
    )


def put_together(own, pieces):
    groups, quarter, model = pieces[0].shape
    count = len(pieces)
    pair = 2 - groups % 2

    def body(own_ref, *refs):
        for u in range(pair):
            for k in range(count):
                start = pl.multiple_of((own_ref[0] ^ k) * quarter, quarter)
                refs[count][u, pl.ds(start, quarter), :] = refs[k][u]

    by_group = lambda n: pl.BlockSpec((pair, n, model), lambda s: (s, 0, 0))
    return run_kernel(
        body,
        "put_together",
        (groups // pair,),
        [scalar_spec()] + [by_group(quarter)] * count,
        [by_group(quarter * count)],
        [struct((groups, quarter * count, model))],
        [],
        [own, *pieces],
        8,
    )[0]


def swap(values, axis, bit):
    size = lax.axis_size(axis)
    return lax.ppermute(values, axis, [(i, i ^ bit) for i in range(size)])


def total_over(values, axis):
    bit = 1
    while bit < lax.axis_size(axis):
        values = values + swap(values, axis, bit)
        bit *= 2
    return values


def meet(*values):
    return lax.optimization_barrier(values)


def split_rows(values, axis, bit):
    mine = (lax.axis_index(axis) // bit) % 2
    half = values.shape[0] // 2
    leaving = lax.dynamic_slice_in_dim(values, (1 - mine) * half, half, 0)
    staying = lax.dynamic_slice_in_dim(values, mine * half, half, 0)
    return leaving, staying


def join_rows(values, other, axis, bit):
    first = (lax.axis_index(axis) // bit) % 2 == 0
    return jnp.concatenate([jnp.where(first, values, other), jnp.where(first, other, values)], 0)


def transpose_blocks(values):
    return lax.all_to_all(values, "seq", split_axis=0, concat_axis=0, tiled=True)


def spread(values):
    far = swap(values, "chan", 2)
    return [values, swap(values, "chan", 1), far, swap(far, "chan", 1)]


def collect(pieces):
    far = pieces[2] + swap(pieces[3], "chan", 1)
    return [pieces[0], swap(pieces[1], "chan", 1), swap(far, "chan", 2)]


def pack(arrays):
    flat = jnp.concatenate([a.reshape(-1) for a in arrays])
    return jnp.pad(flat, (0, -flat.shape[0] % 1024))


def unpack(flat, arrays):
    out = []
    start = 0
    for a in arrays:
        size = math.prod(a.shape)
        out.append(flat[start : start + size].reshape(a.shape))
        start += size
    return out


def sequence_device(
    block_input,
    lengths,
    ln1_gain,
    ln1_bias,
    input_weight,
    input_bias,
    conv_w,
    conv_b,
    filt_w1,
    filt_b1,
    filt_w2,
    filt_b2,
    filt_w3,
    decay,
    skip,
    output_weight,
    output_bias,
    ln2_gain,
    ln2_bias,
    up_weight,
    up_bias,
    down_weight,
    down_bias,
    cotangent,
):
    blocks, block, model = block_input.shape
    count = lax.axis_size("chan")
    quarter = block // count
    rows = blocks * quarter
    width = decay.shape[0]
    seq_length = blocks * block
    seq_index = lax.axis_index("seq")
    chan_index = lax.axis_index("chan")
    own = chan_index.astype(jnp.int32).reshape(1)
    length = lax.dynamic_slice(lengths, (seq_index,), (1,))
    tables = wave_tables(block)
    row = lambda v: v.reshape(1, -1)

    def own_rows(values):
        part = lax.dynamic_slice_in_dim(values, chan_index * quarter, quarter, 1)
        return transpose_blocks(part)

    place_values = jnp.arange(seq_length, dtype=jnp.int32).astype(F32)
    features = position_features(place_values, seq_length, filt_w1.shape[0])
    kernel, filter_pull = jax.vjp(
        partial(implicit_filter, features, place_values), filt_w1, filt_b1, filt_w2, filt_b2, filt_w3, decay
    )
    k_spec = filter_spectrum(kernel.reshape(blocks, block, width), tables)
    weight = jnp.transpose(input_weight, (1, 0, 2))

    x_own = own_rows(block_input)
    side = (seq_index % 2).astype(jnp.int32)

    def half_of(values, axis):
        half = values.shape[axis] // 2
        return lax.dynamic_slice_in_dim(values, side * half, half, axis)

    up_far = swap(half_of(up_weight, 0), "chan", 2)
    up_bias_parts = [swap(up_bias, "chan", k) if k else up_bias for k in range(count)]
    x_own, k_spec, weight, up_far, up_bias_parts, cotangent_home = meet(
        x_own, k_spec, weight, up_far, up_bias_parts, cotangent
    )
    x_far = swap(x_own, "chan", 2)
    x_parts = [x_own, swap(x_own, "chan", 1), x_far, swap(x_far, "chan", 1)]
    cot_own = own_rows(cotangent_home)
    x_rows = x_own.reshape(rows, model)
    x_parts[2], out_home, down_home, up_far = meet(x_parts[2], output_weight, down_weight, up_far)
    out_far = swap(out_home, "chan", 2)
    down_far = swap(half_of(down_home, 1), "chan", 2)
    up_other = swap(up_far, "seq", 1)
    x_parts[0], cot_own = meet(x_parts[0], cot_own)
    cot_own = cot_own.reshape(rows, model)

    (normed_high, normed_low, proj, conv, s_spec), mixed = mixer_forward(
        own, length, x_parts, row(ln1_gain), row(ln1_bias), weight, input_bias, conv_w, conv_b, row(skip), k_spec, tables
    )
    *mixed, down_far, out_far, up_other = meet(*mixed, down_far, out_far, up_other)
    mixed = [m if k == 0 else swap(m, "chan", k) for k, m in enumerate(mixed)]
    down_other = swap(down_far, "seq", 1)
    out_3 = swap(out_far, "chan", 1)
    *mixed, out_3 = meet(*mixed, out_3)
    out_parts = [output_weight, swap(output_weight, "chan", 1), out_far, out_3]
    up_parts = [[up_weight], [swap(up_weight, "chan", 1)], [up_far, up_other]]
    up_parts.append([swap(u, "chan", 1) for u in up_parts[2]])
    down_side = swap(down_far, "chan", 1)

    hidden, *rest = hidden_forward(
        mixed, out_parts, x_rows, cot_own, row(output_bias), row(ln2_gain), row(ln2_bias)
    )
    rest, down_other, down_side = meet(rest, down_other, down_side)
    normed2, turned, cot_parts = rest[0:2], rest[2:4], rest[4:6]
    down_parts = [[down_weight], [swap(down_weight, "chan", 1)], [down_far, down_other]]
    down_parts.append([down_side, swap(down_other, "chan", 1)])

    def units(k, sums):
        return feed_forward(
            side.reshape(1), normed2, turned, cot_parts, up_parts[k], row(up_bias_parts[k]), down_parts[k], sums
        )

    bias_grads = [None] * count
    sums, (up_3, down_3, bias_grads[3]) = units(3, None)
    up_3, down_3 = swap(up_3, "chan", 1), swap(down_3, "chan", 1)
    sums, (up_2, down_2, bias_grads[2]) = units(2, sums)
    *sums, up_2, up_3, down_2, down_3 = meet(*sums, up_2, up_3, down_2, down_3)

    third = model // 3
    far_up = lambda i: up_2[i * third : (i + 1) * third] + up_3[i * third : (i + 1) * third]
    leaving_2, staying_2 = split_rows(down_2, "seq", 1)
    leaving_3, staying_3 = split_rows(down_3, "seq", 1)
    half = leaving_2.shape[0] // 2
    far_ups = [swap(far_up(0), "chan", 2)]
    came = [swap(leaving_2[:half] + leaving_3[:half], "seq", 1)]
    sums, (up_1, down_1, bias_grads[1]) = units(1, sums)
    *sums, far_ups[0], came[0], up_1, down_1 = meet(*sums, far_ups[0], came[0], up_1, down_1)
    up_1, down_1 = swap(up_1, "chan", 1), swap(down_1, "chan", 1)
    far_ups.append(swap(far_up(1), "chan", 2))
    came.append(swap(leaving_2[half:] + leaving_3[half:], "seq", 1))
    sums, (up_0, down_0, bias_grads[0]) = units(0, sums)
    *sums, far_ups[1], came[1], up_1, down_1 = meet(*sums, far_ups[1], came[1], up_1, down_1)
    far_ups.append(swap(far_up(2), "chan", 2))
    leaving, far_staying = split_rows(staying_2 + staying_3 + jnp.concatenate(came, 0), "seq", 2)
    far_came = swap(leaving, "seq", 2)
    leaving_0, staying_0 = split_rows(down_0, "seq", 1)
    leaving_1, staying_1 = split_rows(down_1, "seq", 1)
    near_came = swap(leaving_0 + leaving_1, "seq", 1)
    (out_rows, grad_hidden, sums2), grad_mixed, (out_near, out_far) = hidden_backward(
        hidden, sums[0], sums[1], cot_own, mixed, out_parts, row(ln2_gain), row(down_bias)
    )
    grad_hidden, far_ups[2], far_came, grad_mixed, out_rows = meet(
        grad_hidden, far_ups[2], far_came, grad_mixed, out_rows
    )

    grad_mixed = [g if k == 0 else swap(g, "chan", k) for k, g in enumerate(grad_mixed)]
    leaving, far_staying = split_rows(far_staying + far_came, "seq", 4)
    far_came = swap(leaving, "seq", 4)
    out_blocks = transpose_blocks(out_rows.reshape(blocks, quarter, model))
    grad_up = up_0 + up_1 + jnp.concatenate(far_ups, 0)
    up_leaving, up_staying = split_rows(grad_up, "seq", 1)
    grad_mixed, up_leaving, up_staying, out_far, near_came = meet(
        grad_mixed, up_leaving, up_staying, out_far, near_came
    )

    up_came = swap(up_leaving, "seq", 1)
    leaving, near_staying = split_rows(staying_0 + staying_1 + near_came, "seq", 2)
    near_came = swap(leaving, "seq", 2)
    out_far = swap(out_far, "chan", 2)
    (g_spec, grad_proj, mixer_sums), grad_normed = mixer_backward(
        own, length, grad_mixed, proj, conv, s_spec, k_spec, conv_w, conv_b, row(skip), weight, tables
    )
    grad_normed, grad_proj, out_far, near_came, up_came, out_blocks, far_came = meet(
        grad_normed, grad_proj, out_far, near_came, up_came, out_blocks, far_came
    )

    grad_normed[3], grad_normed[1] = swap(grad_normed[3], "chan", 1), swap(grad_normed[1], "chan", 1)
    far_down = swap(far_staying + far_came, "chan", 2)
    leaving, near_staying = split_rows(near_staying + near_came, "seq", 4)
    up_leaving, up_staying = split_rows(up_staying + up_came, "seq", 2)
    far_normed, grad_proj, leaving, up_leaving = meet(
        grad_normed[2] + grad_normed[3], grad_proj, leaving, up_leaving
    )
    far_normed = swap(far_normed, "chan", 2)
    near_came, up_came = swap(leaving, "seq", 4), swap(up_leaving, "seq", 2)
    grad_in = input_weight_grad(normed_high, normed_low, grad_proj)
    grad_out = out_near[0] + out_far[0] + swap(out_near[1] + out_far[1], "chan", 1)
    g_spec, grad_in, grad_out, near_came, far_down, up_came = meet(
        g_spec, grad_in, grad_out, near_came, far_down, up_came
    )

    grad_down = near_staying + near_came + far_down
    down_came = swap(grad_down, "seq", 4)
    up_leaving, up_staying = split_rows(up_staying + up_came, "seq", 4)
    up_came = swap(up_leaving, "seq", 4)
    mixer_leaving, mixer_staying = split_rows(
        jnp.concatenate([grad_in.reshape(-1, model), grad_out], 0), "seq", 1
    )
    mixer_came = swap(mixer_leaving, "seq", 1)
    grad_kernel = filter_backward(s_spec, g_spec, tables).reshape(seq_length, width)
    far_normed, grad_kernel, down_came, up_came = meet(far_normed, grad_kernel, down_came, up_came)

    pieces = [p.reshape(rows, model) for p in (grad_normed[0], grad_normed[1], far_normed)]
    grad_x_rows, sums1 = input_backward(pieces, x_rows, grad_hidden, row(ln1_gain))
    grad_x_rows, grad_kernel, out_blocks, mixer_came, down_came, up_came, sums1 = meet(
        grad_x_rows, grad_kernel, out_blocks, mixer_came, down_came, up_came, sums1
    )

    grad_x_blocks = transpose_blocks(grad_x_rows.reshape(blocks, quarter, model))
    leaving, staying = split_rows(mixer_staying + mixer_came, "seq", 2)
    came = swap(leaving, "seq", 2)
    grad_up, grad_down = up_staying + up_came, join_rows(grad_down, down_came, "seq", 4)
    down_came, up_came = swap(grad_down, "seq", 2), swap(grad_up, "seq", 4)
    out_far, out_near = swap(out_blocks, "chan", 2), swap(out_blocks, "chan", 1)
    grad_fw1, grad_fb1, grad_fw2, grad_fb2, grad_fw3, grad_decay = filter_pull(grad_kernel)
    grad_x_blocks, came, up_came, down_came, grad_fw3, out_far, out_near = meet(
        grad_x_blocks, came, up_came, down_came, grad_fw3, out_far, out_near
    )

    grad_x_far = swap(grad_x_blocks, "chan", 2)
    out_side = swap(out_far, "chan", 1)
    leaving, staying = split_rows(staying + came, "seq", 4)
    came = swap(leaving, "seq", 4)
    grad_up, grad_down = join_rows(grad_up, up_came, "seq", 4), join_rows(grad_down, down_came, "seq", 2)
    down_came, up_came = swap(grad_down, "seq", 1), swap(grad_up, "seq", 2)
    up_bias_grads = jnp.take(
        jnp.concatenate(bias_grads, 0), jnp.arange(count, dtype=jnp.int32) ^ chan_index, axis=0
    )
    shared = [sums1[0], sums1[1], *[sums2[i] for i in range(4)], up_bias_grads, grad_fw1, grad_fb1, grad_fw2, grad_fb2]
    split = [mixer_sums, grad_fw3, grad_decay]
    shared_flat, split_flat = pack(shared), pack(split)
    came, up_came, out_side, shared_flat, grad_x_blocks = meet(came, up_came, out_side, shared_flat, grad_x_blocks)

    mixer_grads = staying + came
    came = swap(mixer_grads, "seq", 4)
    grad_up = join_rows(grad_up, up_came, "seq", 2)
    up_came = swap(grad_up, "seq", 1)
    side_flat = swap(shared_flat, "chan", 1)
    output = put_together(own, [out_blocks, out_near, out_far, out_side])
    came, grad_x_far, output, side_flat, grad_x_blocks = meet(came, grad_x_far, output, side_flat, grad_x_blocks)

    mixer_grads = join_rows(mixer_grads, came, "seq", 4)
    came = swap(mixer_grads, "seq", 2)
    grad_x_near, grad_x_side = swap(grad_x_blocks, "chan", 1), swap(grad_x_far, "chan", 1)
    shared_flat = shared_flat + side_flat
    side_flat = swap(shared_flat, "chan", 2)
    came, grad_x_near, grad_x_side, side_flat, up_came, down_came = meet(
        came, grad_x_near, grad_x_side, side_flat, up_came, down_came
    )

    flat = jnp.concatenate([shared_flat + side_flat, split_flat])
    mixer_grads = join_rows(mixer_grads, came, "seq", 2)
    side_flat, came = swap(flat, "seq", 2), swap(mixer_grads, "seq", 1)
    grad_x = put_together(own, [grad_x_blocks, grad_x_near, grad_x_far, grad_x_side])
    grad_down = join_rows(grad_down, down_came, "seq", 1)
    side_flat, grad_x, grad_down = meet(side_flat, grad_x, grad_down)
    flat = flat + side_flat
    flat = flat + swap(flat, "seq", 4)
    flat = flat + swap(flat, "seq", 1)
    mixer_grads = join_rows(mixer_grads, came, "seq", 1)
    grad_up = join_rows(grad_up, up_came, "seq", 1)
    grad_in = jnp.transpose(mixer_grads[: 3 * width].reshape(3, width, model), (2, 0, 1))
    grad_out = mixer_grads[3 * width :]

    cut = shared_flat.shape[0]
    grad_ln1_gain, grad_ln1_bias, grad_ln2_gain, grad_ln2_bias, grad_b_out, grad_b_fc2, up_bias_grads, *filt = unpack(
        flat[:cut], shared
    )
    mixer_sums, grad_fw3, grad_decay = unpack(flat[cut:], split)
    grad_b_fc1 = lax.dynamic_slice_in_dim(up_bias_grads, chan_index, 1, 0)[0]
    grad_skip = mixer_sums[0]
    grad_conv_b = mixer_sums[1:4]
    grad_conv_w = mixer_sums[4:13].reshape(3, 3, width)
    grad_b_in = mixer_sums[13:16]
    return (
        output,
        grad_x,
        grad_ln1_gain,
        grad_ln1_bias,
        grad_in,
        grad_b_in,
        grad_conv_w,
        grad_conv_b,
        *filt,
        grad_fw3,
        grad_decay,
        grad_skip,
        grad_out,
        grad_b_out,
        grad_ln2_gain,
        grad_ln2_bias,
        grad_up,
        grad_b_fc1,
        grad_down,
        grad_b_fc2,
    )


def solution(mesh):
    in_specs = (
        P(None, "seq", None),
        P(),
        P(),
        P(),
        P(None, None, "chan"),
        P(None, "chan"),
        P(None, None, "chan"),
        P(None, "chan"),
        P(),
        P(),
        P(),
        P(),
        P(None, "chan"),
        P("chan"),
        P("chan"),
        P("chan", None),
        P(),
        P(),
        P(),
        P(None, "chan"),
        P("chan"),
        P("chan", None),
        P(),
        P(None, "seq", None),
    )
    out_specs = (
        P(None, "seq", None),
        P(None, "seq", None),
        P(),
        P(),
        P(None, None, "chan"),
        P(None, "chan"),
        P(None, None, "chan"),
        P(None, "chan"),
        P(),
        P(),
        P(),
        P(),
        P(None, "chan"),
        P("chan"),
        P("chan"),
        P("chan", None),
        P(),
        P(),
        P(),
        P(None, "chan"),
        P("chan"),
        P("chan", None),
        P(),
    )
    chan = mesh.shape["chan"]

    def step(*arrays):
        sequences, seq_length = arrays[0].shape[:2]
        whole_sequences = sequences == mesh.shape["seq"] and chan == 4 and seq_length % (64 * sequences) == 0
        body = sequence_device if whole_sequences else spectral_device
        return jax.shard_map(
            body, mesh=mesh, in_specs=in_specs, out_specs=out_specs, check_vma=False
        )(*arrays)

    return step
```

```python
from functools import partial
import math

import jax
import jax.numpy as jnp
import ml_dtypes
import numpy as np
from jax import lax
from jax.experimental import pallas as pl
from jax.experimental.pallas import tpu as pltpu
from jax.sharding import PartitionSpec as P

EPSILON = 1e-05
HIGH_ACCURACY = lax.Precision.HIGHEST


def shifted(block, axis, distance):
    devices = range(lax.axis_size(axis))
    route = [(i - distance, i) for i in devices if i - distance in devices]
    return lax.ppermute(block, axis, route)


def layer_norm(values, gain, offset):
    average = jnp.mean(values, -1, keepdims=True)
    centered = values - average
    variance = jnp.mean(centered * centered, -1, keepdims=True)
    return centered * lax.rsqrt(variance + EPSILON) * gain + offset


def position_features(place_values, seq_length, emb_width):
    band_count = (emb_width - 1) // 2
    frequency = jnp.linspace(0.0001, band_count - 1, band_count).astype(jnp.float32)
    phases = 2.0 * math.pi * place_values[:, None] * frequency[None, :] / seq_length
    return jnp.concatenate(
        [(place_values / (seq_length - 1))[:, None], jnp.cos(phases), -jnp.sin(phases)], 1
    )


def implicit_filter(features, place_values, filt_w1, filt_b1, filt_w2, filt_b2, filt_w3, decay):
    first_layer = jnp.sin(jnp.dot(features, filt_w1, precision=HIGH_ACCURACY) + filt_b1)
    second_layer = jnp.sin(jnp.dot(first_layer, filt_w2, precision=HIGH_ACCURACY) + filt_b2)
    raw_kernel = jnp.dot(second_layer, filt_w3, precision=HIGH_ACCURACY)
    return raw_kernel * jnp.exp(-decay[None, :] * place_values[:, None])


def exact_gelu(values):
    return jax.nn.gelu(values, approximate=False)


def tables(count_rows, count_cols):
    turns = (
        jnp.arange(count_rows, dtype=jnp.int32)[:, None]
        * jnp.arange(count_cols, dtype=jnp.int32)[None, :]
        % count_rows
    )
    phases = turns.astype(jnp.float32) * (2.0 * math.pi / count_rows)
    return (jnp.cos(phases), jnp.sin(phases))


def rotate(cos_tab, sin_tab, real, imag, sign, form):
    first_part = jnp.einsum(form, cos_tab, real, precision=HIGH_ACCURACY)
    second_part = jnp.einsum(form, sin_tab, imag, precision=HIGH_ACCURACY)
    third_part = jnp.einsum(form, cos_tab, imag, precision=HIGH_ACCURACY)
    fourth_part = jnp.einsum(form, sin_tab, real, precision=HIGH_ACCURACY)
    return (first_part - sign * second_part, third_part + sign * fourth_part)


def to_spectrum(cos_tab, sin_tab, signal):
    real = jnp.einsum("wp,spc->swc", cos_tab, signal, precision=HIGH_ACCURACY)
    imag = -jnp.einsum("wp,spc->swc", sin_tab, signal, precision=HIGH_ACCURACY)
    return (real, imag)


def time_domain(cos_tab, sin_tab, real, imag):
    return jnp.einsum("wp,swc->spc", cos_tab, real, precision=HIGH_ACCURACY) - jnp.einsum(
        "wp,swc->spc", sin_tab, imag, precision=HIGH_ACCURACY
    )


def earlier_block(values):
    return jnp.pad(values, ((0, 0), (1, 0), (0, 0), (0, 0)))[:, :-1]


def later_block(values):
    return jnp.pad(values, ((0, 0), (0, 1), (0, 0), (0, 0)))[:, 1:]


def spectral_device(
    block_input,
    lengths,
    ln1_gain,
    ln1_bias,
    input_weight,
    input_bias,
    conv_w,
    conv_b,
    filt_w1,
    filt_b1,
    filt_w2,
    filt_b2,
    filt_w3,
    decay,
    skip,
    output_weight,
    output_bias,
    ln2_gain,
    ln2_bias,
    up_weight,
    up_bias,
    down_weight,
    down_bias,
    cotangent,
):
    block = block_input.shape[1]
    blocks = lax.axis_size("seq")
    share = 2 * block // blocks
    seq_index = lax.axis_index("seq")
    places = seq_index * block + jnp.arange(block, dtype=jnp.int32)
    place_values = places.astype(jnp.float32)
    mask = (places[None, :] < lengths[:, None]).astype(jnp.float32)[:, :, None]
    first_normed, norm1_pull = jax.vjp(layer_norm, block_input, ln1_gain, ln1_bias)
    input_projected = (
        jnp.einsum("spd,dkc->spkc", first_normed, input_weight, precision=HIGH_ACCURACY)
        + input_bias
    )
    rims = shifted(input_projected[:, block - 2 :], "seq", 1)
    extended = jnp.concatenate([rims, input_projected], 1)
    short = (
        conv_w[0] * extended[:, :block]
        + conv_w[1] * extended[:, 1 : block + 1]
        + conv_w[2] * extended[:, 2:]
        + conv_b
    )
    gate_out = short[:, :, 0]
    gate_in = short[:, :, 1]
    values = short[:, :, 2]
    signal = values * gate_in * mask
    cos_tab, sin_tab = tables(2 * block, block)
    block_cos, block_sin = tables(2 * blocks, blocks)
    own_freq = seq_index * share + jnp.arange(share, dtype=jnp.int32)
    parity = (1 - 2 * (own_freq % 2)).astype(jnp.float32)[:, None]
    features = position_features(place_values, blocks * block, filt_w1.shape[0])
    kernel, filter_pull = jax.vjp(
        partial(implicit_filter, features, place_values),
        filt_w1,
        filt_b1,
        filt_w2,
        filt_b2,
        filt_w3,
        decay,
    )
    signal_re, signal_im = to_spectrum(cos_tab, sin_tab, signal)
    kernel_re, kernel_im = to_spectrum(cos_tab, sin_tab, kernel[None])
    signal_re, signal_im, kernel_re, kernel_im = (
        lax.all_to_all(signal_re[:, None], "seq", split_axis=2, concat_axis=1, tiled=True),
        lax.all_to_all(signal_im[:, None], "seq", split_axis=2, concat_axis=1, tiled=True),
        lax.all_to_all(kernel_re[:, None], "seq", split_axis=2, concat_axis=1, tiled=True),
        lax.all_to_all(kernel_im[:, None], "seq", split_axis=2, concat_axis=1, tiled=True),
    )
    zq_re, zq_im = rotate(block_cos, block_sin, signal_re, signal_im, -1.0, "qk,skfc->sqfc")
    hq_re, hq_im = rotate(block_cos, block_sin, kernel_re, kernel_im, -1.0, "qk,skfc->sqfc")
    prod_re = zq_re * hq_re - zq_im * hq_im
    prod_im = zq_re * hq_im + zq_im * hq_re
    joined_re, joined_im = rotate(block_cos, block_sin, prod_re, prod_im, 1.0, "qj,sqfc->sjfc")
    joined_re = joined_re / (2 * blocks)
    joined_im = joined_im / (2 * blocks)
    folded_re = joined_re + parity * earlier_block(joined_re)
    folded_im = joined_im + parity * earlier_block(joined_im)
    folded_re, folded_im = (
        lax.all_to_all(folded_re, "seq", split_axis=1, concat_axis=2, tiled=True),
        lax.all_to_all(folded_im, "seq", split_axis=1, concat_axis=2, tiled=True),
    )
    convolved = time_domain(cos_tab, sin_tab, folded_re[:, 0], folded_im[:, 0]) / (2 * block)
    conv_sum = convolved + skip * signal
    mixer_output = conv_sum * gate_out
    partial_mix = jnp.einsum("spc,cd->spd", mixer_output, output_weight, precision=HIGH_ACCURACY)
    hidden_state = block_input + lax.psum(partial_mix, "chan") + output_bias
    second_normed2 = layer_norm(hidden_state, ln2_gain, ln2_bias)
    before = jnp.einsum("spd,df->spf", second_normed2, up_weight, precision=HIGH_ACCURACY) + up_bias
    active_units, gelu_pull = jax.vjp(exact_gelu, before)
    feed = lax.psum(
        jnp.einsum("spf,fd->spd", active_units, down_weight, precision=HIGH_ACCURACY), "chan"
    )
    output = hidden_state + feed + down_bias
    grad_b_fc2 = jnp.sum(cotangent, (0, 1))
    grad_w_fc2 = jnp.einsum("spf,spd->fd", active_units, cotangent, precision=HIGH_ACCURACY)
    grad_active = jnp.einsum("spd,fd->spf", cotangent, down_weight, precision=HIGH_ACCURACY)
    grad_before = gelu_pull(grad_active)[0]
    grad_w_fc1 = jnp.einsum("spd,spf->df", second_normed2, grad_before, precision=HIGH_ACCURACY)
    grad_b_fc1 = jnp.sum(grad_before, (0, 1))
    grad_normed2 = lax.psum(
        jnp.einsum("spf,df->spd", grad_before, up_weight, precision=HIGH_ACCURACY), "chan"
    )
    norm2_pull = jax.vjp(layer_norm, hidden_state, ln2_gain, ln2_bias)[1]
    grad_hidden_norm, grad_ln2_gain, grad_ln2_bias = norm2_pull(grad_normed2)
    grad_hidden = cotangent + grad_hidden_norm
    grad_b_out = jnp.sum(grad_hidden, (0, 1))
    grad_w_out = jnp.einsum("spc,spd->cd", mixer_output, grad_hidden, precision=HIGH_ACCURACY)
    grad_mixed = jnp.einsum("spd,cd->spc", grad_hidden, output_weight, precision=HIGH_ACCURACY)
    grad_conv = grad_mixed * gate_out
    grad_gate_out = grad_mixed * conv_sum
    grad_skip = jnp.sum(grad_conv * signal, (0, 1))
    back_re, back_im = to_spectrum(cos_tab, sin_tab, grad_conv)
    back_re = back_re / (2 * block)
    back_im = back_im / (2 * block)
    back_re, back_im = (
        lax.all_to_all(back_re[:, None], "seq", split_axis=2, concat_axis=1, tiled=True),
        lax.all_to_all(back_im[:, None], "seq", split_axis=2, concat_axis=1, tiled=True),
    )
    unfold_re = back_re + parity * later_block(back_re)
    unfold_im = back_im + parity * later_block(back_im)
    dprod_re, dprod_im = rotate(block_cos, block_sin, unfold_re, unfold_im, -1.0, "qj,sjfc->sqfc")
    dprod_re = dprod_re / (2 * blocks)
    dprod_im = dprod_im / (2 * blocks)
    dzq_re = hq_re * dprod_re + hq_im * dprod_im
    dzq_im = hq_re * dprod_im - hq_im * dprod_re
    dhq_re = jnp.sum(zq_re * dprod_re + zq_im * dprod_im, 0, keepdims=True)
    dhq_im = jnp.sum(zq_re * dprod_im - zq_im * dprod_re, 0, keepdims=True)
    dsig_re, dsig_im = rotate(block_cos, block_sin, dzq_re, dzq_im, 1.0, "qk,sqfc->skfc")
    dker_re, dker_im = rotate(block_cos, block_sin, dhq_re, dhq_im, 1.0, "qk,sqfc->skfc")
    dsig_re, dsig_im, dker_re, dker_im = (
        lax.all_to_all(dsig_re, "seq", split_axis=1, concat_axis=2, tiled=True),
        lax.all_to_all(dsig_im, "seq", split_axis=1, concat_axis=2, tiled=True),
        lax.all_to_all(dker_re, "seq", split_axis=1, concat_axis=2, tiled=True),
        lax.all_to_all(dker_im, "seq", split_axis=1, concat_axis=2, tiled=True),
    )
    grad_signal = time_domain(cos_tab, sin_tab, dsig_re[:, 0], dsig_im[:, 0]) + grad_conv * skip
    grad_kernel = time_domain(cos_tab, sin_tab, dker_re[:, 0], dker_im[:, 0])[0]
    grad_fw1, grad_fb1, grad_fw2, grad_fb2, grad_fw3, grad_decay = filter_pull(grad_kernel)
    grad_short = jnp.stack(
        [grad_gate_out, grad_signal * values * mask, grad_signal * gate_in * mask], 2
    )
    grad_conv_b = jnp.sum(grad_short, (0, 1))
    grad_conv_w = jnp.stack(
        [jnp.sum(grad_short * extended[:, offset : offset + block], (0, 1)) for offset in range(3)]
    )
    grad_extended = (
        jnp.pad(conv_w[0] * grad_short, ((0, 0), (0, 2), (0, 0), (0, 0)))
        + jnp.pad(conv_w[1] * grad_short, ((0, 0), (1, 1), (0, 0), (0, 0)))
        + jnp.pad(conv_w[2] * grad_short, ((0, 0), (2, 0), (0, 0), (0, 0)))
    )
    returned = shifted(grad_extended[:, :2], "seq", -1)
    grad_proj = grad_extended[:, 2:] + jnp.pad(returned, ((0, 0), (block - 2, 0), (0, 0), (0, 0)))
    grad_b_in = jnp.sum(grad_proj, (0, 1))
    grad_w_in = jnp.einsum("spd,spkc->dkc", first_normed, grad_proj, precision=HIGH_ACCURACY)
    grad_normed = lax.psum(
        jnp.einsum("spkc,dkc->spd", grad_proj, input_weight, precision=HIGH_ACCURACY), "chan"
    )
    grad_x_norm, grad_ln1_gain, grad_ln1_bias = norm1_pull(grad_normed)
    grad_x = grad_hidden + grad_x_norm
    (
        grad_ln1_gain,
        grad_ln1_bias,
        grad_w_in,
        grad_b_in,
        grad_conv_w,
        grad_conv_b,
        grad_fw3,
        grad_decay,
        grad_skip,
        grad_w_out,
        grad_b_out,
        grad_ln2_gain,
        grad_ln2_bias,
        grad_w_fc1,
        grad_b_fc1,
        grad_w_fc2,
        grad_b_fc2,
    ) = lax.psum(
        (
            grad_ln1_gain,
            grad_ln1_bias,
            grad_w_in,
            grad_b_in,
            grad_conv_w,
            grad_conv_b,
            grad_fw3,
            grad_decay,
            grad_skip,
            grad_w_out,
            grad_b_out,
            grad_ln2_gain,
            grad_ln2_bias,
            grad_w_fc1,
            grad_b_fc1,
            grad_w_fc2,
            grad_b_fc2,
        ),
        "seq",
    )
    grad_fw1, grad_fb1, grad_fw2, grad_fb2 = lax.psum(
        (grad_fw1, grad_fb1, grad_fw2, grad_fb2), ("seq", "chan")
    )
    return (
        output,
        grad_x,
        grad_ln1_gain,
        grad_ln1_bias,
        grad_w_in,
        grad_b_in,
        grad_conv_w,
        grad_conv_b,
        grad_fw1,
        grad_fb1,
        grad_fw2,
        grad_fb2,
        grad_fw3,
        grad_decay,
        grad_skip,
        grad_w_out,
        grad_b_out,
        grad_ln2_gain,
        grad_ln2_bias,
        grad_w_fc1,
        grad_b_fc1,
        grad_w_fc2,
        grad_b_fc2,
    )


F32 = jnp.float32
BF16 = jnp.bfloat16
NN = (((1,), (0,)), ((), ()))
NT = (((1,), (1,)), ((), ()))
TN = (((0,), (0,)), ((), ()))
VMEM_BYTES = 56 * 2**20


def parts_of(values):
    high = values.astype(BF16)
    return high, (values - high.astype(F32)).astype(BF16)


def dot_parts(left, right, dims):
    def one(a, b):
        return lax.dot_general(a, b, dims, preferred_element_type=F32)

    return one(left[0], right[0]) + (one(left[0], right[1]) + one(left[1], right[0]))


def normalise(values):
    average = jnp.mean(values, -1, keepdims=True)
    centered = values - average
    variance = jnp.mean(centered * centered, -1, keepdims=True)
    scale = lax.rsqrt(variance + EPSILON)
    return centered * scale, scale


def norm_back(unit, scale, gain, grad):
    lifted = grad * gain
    mean_one = jnp.mean(lifted, -1, keepdims=True)
    mean_two = jnp.mean(lifted * unit, -1, keepdims=True)
    return scale * (lifted - mean_one - unit * mean_two)


def fold(rows):
    half = rows.shape[0] // 2
    return jnp.concatenate([rows[:half], rows[half:]], 1)


def unfold(folded):
    width = folded.shape[1] // 2
    return jnp.concatenate([folded[:, :width], folded[:, width:]], 0)


def column_sum(values):
    return jnp.sum(values, 0, keepdims=True)


def whole(array):
    return pl.BlockSpec(array.shape, lambda *_: (0,) * len(array.shape))


def scalar_spec():
    return pl.BlockSpec(memory_space=pltpu.SMEM)


def struct(shape, kind=F32):
    return jax.ShapeDtypeStruct(tuple(shape), kind)


def run_kernel(body, name, grid, in_specs, out_specs, out_shape, scratch, args, micros):
    return pl.pallas_call(
        body,
        name=name,
        grid=grid,
        in_specs=in_specs,
        out_specs=out_specs,
        out_shape=out_shape,
        scratch_shapes=scratch,
        compiler_params=pltpu.CompilerParams(
            dimension_semantics=("arbitrary",) * len(grid), vmem_limit_bytes=VMEM_BYTES
        ),
        cost_estimate=pl.CostEstimate(
            flops=int(micros * 1.15e9), bytes_accessed=int(micros * 3.6e6), transcendentals=0
        ),
    )(*args)


def wave_tables(block):
    angles = np.pi * np.outer(2 * np.arange(block) + 1, np.arange(block)) / (2 * block)
    table = np.concatenate([np.cos(angles), -np.sin(angles)], 0)

    def both(values):
        high = values.astype(ml_dtypes.bfloat16)
        low = (values - high.astype(np.float64)).astype(ml_dtypes.bfloat16)
        return jnp.asarray(high), jnp.asarray(low)

    return both(table) + both(table.T / block)


def parity_of(rows):
    odd = lax.broadcasted_iota(jnp.int32, (rows, 1), 0) % 2
    return (1 - 2 * odd).astype(F32)


def filter_spectrum(kernel, tables):
    blocks, block, width = kernel.shape
    table_high, table_low = tables[:2]

    def body(kernel_ref, high_ref, low_ref, out_ref, before_ref):
        @pl.when(pl.program_id(0) == 0)
        def _():
            before_ref[...] = jnp.zeros_like(before_ref)

        spectrum = dot_parts((high_ref[...], low_ref[...]), parts_of(kernel_ref[0]), NN)
        sign = parity_of(block)
        out_ref[0, :block] = spectrum[:block] - sign * before_ref[block:]
        out_ref[0, block:] = spectrum[block:] + sign * before_ref[:block]
        before_ref[...] = spectrum

    return run_kernel(
        body,
        "filter_spectrum",
        (blocks,),
        [pl.BlockSpec((1, block, width), lambda b: (b, 0, 0)), whole(table_high), whole(table_low)],
        [pl.BlockSpec((1, 2 * block, width), lambda b: (b, 0, 0))],
        [struct((blocks, 2 * block, width))],
        [pltpu.VMEM((2 * block, width), F32)],
        [kernel, table_high, table_low],
        8,
    )[0]


def mixer_forward(own, length, x_parts, gain, offset, weight, bias, conv_w, conv_b, skip, spectrum, tables):
    blocks, quarter, model = x_parts[0].shape
    count = len(x_parts)
    block = quarter * count
    width = weight.shape[2]
    tile = min(32, block)
    pair = 2 - blocks % 2
    span = pair * block

    def body(*refs):
        own_ref, length_ref = refs[:2]
        x_refs = refs[2 : 2 + count]
        refs = refs[2 + count :]
        gain_ref, offset_ref, weight_ref, bias_ref, conv_w_ref, conv_b_ref, skip_ref, k_ref = refs[:8]
        th_ref, tl_ref, ih_ref, il_ref = refs[8:12]
        nh_ref, nl_ref, proj_ref, conv_ref, s_ref = refs[12:17]
        m_refs = refs[17 : 17 + count]
        wh_ref, wl_ref, ext_ref, o_ref, mixed_ref = refs[17 + count :]
        step = pl.program_id(0)
        me = own_ref[0]

        @pl.when(step == 0)
        def _():
            for k in range(3):
                wh_ref[k], wl_ref[k] = parts_of(weight_ref[k])
            ext_ref[:, :8] = jnp.zeros((3, 8, width), F32)

        for u in range(pair):
            for k in range(count):
                normed = normalise(x_refs[k][u])[0] * gain_ref[...] + offset_ref[...]
                start = pl.multiple_of(u * block + (me ^ k) * quarter, quarter)
                high, low = parts_of(normed)
                nh_ref[0, pl.ds(start, quarter), :] = high
                nl_ref[0, pl.ds(start, quarter), :] = low
        normed = (nh_ref[0], nl_ref[0])
        short = []
        for k in range(3):
            proj = dot_parts(normed, (wh_ref[k], wl_ref[k]), NN) + bias_ref[k : k + 1, :]
            proj_ref[0, k] = proj
            ext_ref[k, 8:] = proj
            short.append(
                conv_w_ref[0, k : k + 1, :] * ext_ref[k, 6 : 6 + span]
                + conv_w_ref[1, k : k + 1, :] * ext_ref[k, 7 : 7 + span]
                + conv_w_ref[2, k : k + 1, :] * proj
                + conv_b_ref[k : k + 1, :]
            )
            ext_ref[k, :8] = ext_ref[k, span:]
        places = step * span + lax.broadcasted_iota(jnp.int32, (span, 1), 0)
        mask = (places < length_ref[0]).astype(F32)
        signal = short[2] * short[1] * mask
        for u in range(pair):
            part = signal[u * block : (u + 1) * block]
            s_ref[step * pair + u] = dot_parts((th_ref[...], tl_ref[...]), parts_of(part), NN)
        for u in range(pair):
            b = step * pair + u
            for r in range(0, block, tile):
                lo = slice(r, r + tile)
                hi = slice(block + r, block + r + tile)

                def product(i, total, b=b, lo=lo, hi=hi):
                    s_re, s_im = s_ref[i, lo], s_ref[i, hi]
                    k_re, k_im = k_ref[b - i, lo], k_ref[b - i, hi]
                    return total[0] + s_re * k_re - s_im * k_im, total[1] + s_re * k_im + s_im * k_re

                zero = jnp.zeros((tile, width), F32)
                o_ref[u, lo], o_ref[u, hi] = lax.fori_loop(0, b + 1, product, (zero, zero))
        inverse = (ih_ref[...], il_ref[...])
        conv = jnp.concatenate([dot_parts(inverse, parts_of(o_ref[u]), NN) for u in range(pair)], 0)
        conv = conv + skip_ref[...] * signal
        conv_ref[0] = conv
        mixed_ref[...] = conv * short[0]
        for u in range(pair):
            for k in range(count):
                start = pl.multiple_of(u * block + (me ^ k) * quarter, quarter)
                m_refs[k][u] = fold(mixed_ref[pl.ds(start, quarter), :])

    by_block = lambda *shape: pl.BlockSpec((1,) + shape, lambda b: (b,) + (0,) * len(shape))
    args = [own, length, *x_parts, gain, offset, weight, bias, conv_w, conv_b, skip, spectrum, *tables]
    by_pair = lambda n: pl.BlockSpec((pair, quarter, n), lambda b: (b, 0, 0))
    in_specs = [scalar_spec(), scalar_spec()] + [by_pair(model)] * count
    in_specs += [whole(a) for a in args[2 + count :]]
    folded = pl.BlockSpec((pair, quarter // 2, 2 * width), lambda b: (b, 0, 0))
    s_shape = struct((blocks, 2 * block, width))
    outs = run_kernel(
        body,
        "mixer_forward",
        (blocks // pair,),
        in_specs,
        [by_block(span, model)] * 2
        + [by_block(3, span, width), by_block(span, width), whole(s_shape)]
        + [folded] * count,
        [struct((blocks // pair, span, model), BF16)] * 2
        + [struct((blocks // pair, 3, span, width)), struct((blocks // pair, span, width)), s_shape]
        + [struct((blocks, quarter // 2, 2 * width))] * count,
        [
            pltpu.VMEM((3, model, width), BF16),
            pltpu.VMEM((3, model, width), BF16),
            pltpu.VMEM((3, span + 8, width), F32),
            pltpu.VMEM((pair, 2 * block, width), F32),
            pltpu.VMEM((span, width), F32),
        ],
        args,
        36,
    )
    return outs[:5], list(outs[5:])


def hidden_forward(m_parts, weights, x_own, cotangent, bias, gain, offset):
    blocks, half, width = m_parts[0].shape
    rows, model = x_own.shape
    width = width // 2
    count = len(m_parts)
    group = math.gcd(blocks, max(128 // half, 1))
    step = 2 * half * group

    def body(*refs):
        m_refs, w_refs = refs[:count], refs[count : 2 * count]
        x_ref, c_ref, bias_ref, gain_ref, offset_ref = refs[2 * count : 2 * count + 5]
        h_ref, nh_ref, nl_ref, th_ref, tl_ref, ch_ref, cl_ref = refs[2 * count + 5 : 2 * count + 12]
        wh_ref, wl_ref = refs[2 * count + 12 :]

        @pl.when(pl.program_id(0) == 0)
        def _():
            for k in range(count):
                wh_ref[k], wl_ref[k] = parts_of(w_refs[k][...])

        hidden = x_ref[...] + bias_ref[...]
        for k in range(count):
            mixed = jnp.concatenate([unfold(m_refs[k][u]) for u in range(group)], 0)
            hidden = hidden + dot_parts(parts_of(mixed), (wh_ref[k], wl_ref[k]), NN)
        h_ref[...] = hidden
        normed = normalise(hidden)[0] * gain_ref[...] + offset_ref[...]
        nh_ref[...], nl_ref[...] = parts_of(normed)
        th_ref[...], tl_ref[...] = parts_of(normed.T)
        ch_ref[...], cl_ref[...] = parts_of(c_ref[...])

    row_spec = lambda n: pl.BlockSpec((step, n), lambda r: (r, 0))
    turned = pl.BlockSpec((model, step), lambda r: (0, r))
    args = [*m_parts, *weights, x_own, cotangent, bias, gain, offset]
    return run_kernel(
        body,
        "hidden_forward",
        (rows // step,),
        [pl.BlockSpec((group, half, 2 * width), lambda r: (r, 0, 0))] * count
        + [whole(w) for w in weights]
        + [row_spec(model)] * 2
        + [whole(bias), whole(gain), whole(offset)],
        [row_spec(model)] * 3 + [turned] * 2 + [row_spec(model)] * 2,
        [struct((rows, model))]
        + [struct((rows, model), BF16)] * 2
        + [struct((model, rows), BF16)] * 2
        + [struct((rows, model), BF16)] * 2,
        [pltpu.VMEM((count, width, model), BF16)] * 2,
        args,
        9,
    )


def feed_forward(side, normed, turned, cotangent, up, up_bias, down, sums):
    rows, model = normed[0].shape
    units = up_bias.shape[1]
    step = min(256, units)
    first = sums is None
    pieces = len(up)

    def body(side_ref, *refs):
        nh_ref, nl_ref, th_ref, tl_ref, ch_ref, cl_ref, bias_ref = refs[:7]
        up_refs, down_refs = refs[7 : 7 + pieces], refs[7 + pieces : 7 + 2 * pieces]
        refs = refs[7 + 2 * pieces :]
        feed_in, grad_in = (None, None) if first else refs[:2]
        feed_ref, grad_ref, gup_ref, gdown_ref, gbias_ref = refs[0 if first else 2 :]

        @pl.when(pl.program_id(0) == 0)
        def _():
            if first:
                feed_ref[...] = jnp.zeros_like(feed_ref)
                grad_ref[...] = jnp.zeros_like(grad_ref)
            else:
                feed_ref[...] = feed_in[...]
                grad_ref[...] = grad_in[...]

        def in_order(halves, axis):
            if pieces == 1:
                return halves[0][...]
            mine, other = halves[0][...], halves[1][...]
            low = side_ref[0] == 0
            return jnp.concatenate([jnp.where(low, mine, other), jnp.where(low, other, mine)], axis)

        own_normed = (nh_ref[...], nl_ref[...])
        own_cotangent = (ch_ref[...], cl_ref[...])
        up_parts = parts_of(in_order(up_refs, 0))
        down_parts = parts_of(in_order(down_refs, 1))
        before = dot_parts(own_normed, up_parts, NN) + bias_ref[...]
        grad_active = dot_parts(own_cotangent, down_parts, NT)
        below = 0.5 + 0.5 * lax.erf(before * math.sqrt(0.5))
        slope = below + before * (jnp.exp(-0.5 * before * before) * (1.0 / math.sqrt(2.0 * math.pi)))
        active = before * below
        grad_before = grad_active * slope
        gbias_ref[...] = column_sum(grad_before)
        active_parts = parts_of(active)
        grad_parts = parts_of(grad_before)
        feed_ref[...] += dot_parts(active_parts, down_parts, NN)
        grad_ref[...] += dot_parts(grad_parts, up_parts, NT)
        gup_ref[...] = dot_parts((th_ref[...], tl_ref[...]), grad_parts, NN)
        gdown_ref[...] = dot_parts(active_parts, own_cotangent, TN)

    total = struct((rows, model))
    args = [side, *normed, *turned, *cotangent, up_bias, *up, *down] + ([] if first else list(sums))
    columns = lambda n: pl.BlockSpec((n, step), lambda t: (0, t))
    some_rows = lambda n: pl.BlockSpec((step, n), lambda t: (t, 0))
    outs = run_kernel(
        body,
        "feed_forward",
        (units // step,),
        [scalar_spec()]
        + [whole(a) for a in args[1:7]]
        + [columns(1)]
        + [columns(model // pieces)] * pieces
        + [some_rows(model // pieces)] * pieces
        + [whole(a) for a in args[8 + 2 * pieces :]],
        [whole(total), whole(total), columns(model), some_rows(model), columns(1)],
        [total, total, struct((model, units)), struct((units, model)), struct(up_bias.shape)],
        [],
        args,
        18,
    )
    return outs[:2], outs[2:]


def feed_forward_pair(normed, turned, cotangent, ups, biases, downs, sums):
    rows, model = normed[0].shape
    units = biases[0].shape[1]
    step = min(256, units)
    tiles = units // step

    def body(*refs):
        nh_ref, nl_ref, th_ref, tl_ref, ch_ref, cl_ref, bias_ref = refs[:7]
        up_refs, down_refs, (feed_in, grad_in) = refs[7:9], refs[9:11], refs[11:13]
        feed_ref, grad_ref, gbias_ref = refs[13:16]
        gup_refs, gdown_refs = refs[16:18], refs[18:20]
        uh_ref, ul_ref, dh_ref, dl_ref = refs[20:]
        t = pl.program_id(0)

        @pl.when(t == 0)
        def _():
            feed_ref[...] = feed_in[...]
            grad_ref[...] = grad_in[...]

        for j in range(2):

            @pl.when(t // tiles == j)
            def _(j=j):
                uh_ref[...], ul_ref[...] = parts_of(up_refs[j][...])
                dh_ref[...], dl_ref[...] = parts_of(down_refs[j][...])

        own_normed = (nh_ref[...], nl_ref[...])
        own_cotangent = (ch_ref[...], cl_ref[...])
        up_parts, down_parts = (uh_ref[...], ul_ref[...]), (dh_ref[...], dl_ref[...])
        before = dot_parts(own_normed, up_parts, NN) + bias_ref[...]
        grad_active = dot_parts(own_cotangent, down_parts, NT)
        below = 0.5 + 0.5 * lax.erf(before * math.sqrt(0.5))
        slope = below + before * (jnp.exp(-0.5 * before * before) * (1.0 / math.sqrt(2.0 * math.pi)))
        active = before * below
        grad_before = grad_active * slope
        gbias_ref[...] = column_sum(grad_before)
        active_parts = parts_of(active)
        grad_parts = parts_of(grad_before)
        feed_ref[...] += dot_parts(active_parts, down_parts, NN)
        grad_ref[...] += dot_parts(grad_parts, up_parts, NT)
        grad_up = dot_parts((th_ref[...], tl_ref[...]), grad_parts, NN)
        grad_down = dot_parts(active_parts, own_cotangent, TN)
        for j in range(2):

            @pl.when(t // tiles == j)
            def _(j=j):
                gup_refs[j][...] = grad_up
                gdown_refs[j][...] = grad_down

    total = struct((rows, model))
    bias = jnp.concatenate(biases, 1)
    args = [*normed, *turned, *cotangent, bias, *ups, *downs, *sums]
    place = lambda t, j: jnp.minimum(t, tiles - 1) if j == 0 else jnp.maximum(t - tiles, 0)
    columns = [pl.BlockSpec((model, step), lambda t, j=j: (0, place(t, j))) for j in range(2)]
    some_rows = [pl.BlockSpec((step, model), lambda t, j=j: (place(t, j), 0)) for j in range(2)]
    one_row = pl.BlockSpec((1, step), lambda t: (0, t))
    outs = run_kernel(
        body,
        "feed_forward_pair",
        (2 * tiles,),
        [whole(a) for a in args[:6]] + [one_row] + columns + some_rows + [whole(total)] * 2,
        [whole(total)] * 2 + [one_row] + columns + some_rows,
        [total, total, struct(bias.shape)] + [struct((model, units))] * 2 + [struct((units, model))] * 2,
        [pltpu.VMEM((model, step), BF16)] * 2 + [pltpu.VMEM((step, model), BF16)] * 2,
        args,
        31,
    )
    return outs[:2], outs[2], outs[3:5], outs[5:7]


def hidden_backward(hidden, feed, grad_normed, cotangent, m_parts, weights, gain, bias):
    rows, model = hidden.shape
    blocks, half, width = m_parts[0].shape
    width = width // 2
    count = len(m_parts)
    group = math.gcd(blocks, max(128 // half, 1))
    step = 2 * half * group

    def body(*refs):
        h_ref, f_ref, g_ref, c_ref = refs[:4]
        m_refs, w_refs = refs[4 : 4 + count], refs[4 + count : 4 + 2 * count]
        gain_ref, bias_ref, out_ref, gh_ref, sum_ref = refs[4 + 2 * count : 9 + 2 * count]
        gm_refs, refs = refs[9 + 2 * count : 9 + 3 * count], refs[9 + 3 * count :]
        gw_refs, (wh_ref, wl_ref) = refs[:2], refs[2:]

        @pl.when(pl.program_id(0) == 0)
        def _():
            sum_ref[...] = jnp.zeros_like(sum_ref)
            for k in range(count):
                wh_ref[k], wl_ref[k] = parts_of(w_refs[k][...])
            for k in range(2):
                gw_refs[k][...] = jnp.zeros_like(gw_refs[k])

        hidden_rows, grad, above = h_ref[...], g_ref[...], c_ref[...]
        out_ref[...] = hidden_rows + f_ref[...] + bias_ref[...]
        unit, scale = normalise(hidden_rows)
        grad_hidden = above + norm_back(unit, scale, gain_ref[...], grad)
        gh_ref[...] = grad_hidden
        sum_ref[0:1] += column_sum(grad * unit)
        sum_ref[1:2] += column_sum(grad)
        sum_ref[2:3] += column_sum(grad_hidden)
        sum_ref[3:4] += column_sum(above)
        parts = parts_of(grad_hidden)
        for k in range(count):
            grad_mixed = dot_parts(parts, (wh_ref[k], wl_ref[k]), NT)
            for u in range(group):
                gm_refs[k][u] = fold(grad_mixed[u * 2 * half : (u + 1) * 2 * half])
            mixed = jnp.concatenate([unfold(m_refs[k][u]) for u in range(group)], 0)
            gw_refs[k // 2][k % 2] += dot_parts(parts_of(mixed), parts, TN)

    folded = pl.BlockSpec((group, half, 2 * width), lambda r: (r, 0, 0))
    row_spec = lambda n: pl.BlockSpec((step, n), lambda r: (r, 0))
    args = [hidden, feed, grad_normed, cotangent, *m_parts, *weights, gain, bias]
    sums, pair = struct((8, model)), struct((2, width, model))
    outs = run_kernel(
        body,
        "hidden_backward",
        (rows // step,),
        [row_spec(model)] * 4 + [folded] * count + [whole(w) for w in weights] + [whole(gain), whole(bias)],
        [row_spec(model)] * 2
        + [whole(sums)]
        + [folded] * count
        + [whole(pair)] * 2,
        [struct((rows, model))] * 2 + [sums] + [struct((blocks, half, 2 * width))] * count + [pair] * 2,
        [pltpu.VMEM((count, width, model), BF16)] * 2,
        args,
        15,
    )
    return outs[:3], list(outs[3 : 3 + count]), outs[3 + count :]


def mixer_backward(own, length, gm_parts, proj, conv, s_spec, k_spec, conv_w, conv_b, skip, weight, tables):
    blocks, quarter, width = gm_parts[0].shape
    quarter, width = 2 * quarter, width // 2
    count = len(gm_parts)
    block = quarter * count
    model = weight.shape[1]
    tile = min(32, block)
    pair = 2 - blocks % 2
    span = pair * block

    def body(*refs):
        own_ref, length_ref = refs[:2]
        gm_refs = refs[2 : 2 + count]
        refs = refs[2 + count :]
        proj_ref, rim_ref, conv_ref, k_ref, conv_w_ref, conv_b_ref, skip_ref, weight_ref = refs[:8]
        th_ref, tl_ref, ih_ref, il_ref = refs[8:12]
        g_ref, gp_ref, sum_ref = refs[12:15]
        gn_refs = refs[15 : 15 + count]
        wh_ref, wl_ref, ext_ref, gs_ref, o_ref, rows_ref, gn_ref = refs[15 + count :]
        step = pl.program_id(0)
        slot = blocks // pair - 1 - step
        me = own_ref[0]

        @pl.when(step == 0)
        def _():
            for k in range(3):
                wh_ref[k], wl_ref[k] = parts_of(weight_ref[k])
            gs_ref[:, span:] = jnp.zeros((3, 8, width), F32)
            sum_ref[...] = jnp.zeros_like(sum_ref)

        for u in range(pair):
            for k in range(count):
                start = pl.multiple_of(u * block + (me ^ k) * quarter, quarter)
                rows_ref[pl.ds(start, quarter), :] = unfold(gm_refs[k][u])
        inside = (slot > 0).astype(F32)
        short = []
        for k in range(3):
            ext_ref[k, :8] = rim_ref[0, k] * inside
            ext_ref[k, 8:] = proj_ref[0, k]
            short.append(
                conv_w_ref[0, k : k + 1, :] * ext_ref[k, 6 : 6 + span]
                + conv_w_ref[1, k : k + 1, :] * ext_ref[k, 7 : 7 + span]
                + conv_w_ref[2, k : k + 1, :] * proj_ref[0, k]
                + conv_b_ref[k : k + 1, :]
            )
        places = slot * span + lax.broadcasted_iota(jnp.int32, (span, 1), 0)
        mask = (places < length_ref[0]).astype(F32)
        gate_in, values = short[1] * mask, short[2] * mask
        grad_mixed = rows_ref[...]
        grad_conv = grad_mixed * short[0]
        gs_ref[0, :span] = grad_mixed * conv_ref[0]
        for u in range(pair):
            part = grad_conv[u * block : (u + 1) * block]
            g_ref[slot * pair + u] = dot_parts((th_ref[...], tl_ref[...]), parts_of(part), NN)
        for u in range(pair):
            b = slot * pair + u
            for r in range(0, block, tile):
                lo = slice(r, r + tile)
                hi = slice(block + r, block + r + tile)

                def product(j, total, b=b, lo=lo, hi=hi):
                    g_re, g_im = g_ref[j, lo], g_ref[j, hi]
                    k_re, k_im = k_ref[j - b, lo], k_ref[j - b, hi]
                    return total[0] + g_re * k_re + g_im * k_im, total[1] + g_im * k_re - g_re * k_im

                zero = jnp.zeros((tile, width), F32)
                o_ref[u, lo], o_ref[u, hi] = lax.fori_loop(b, blocks, product, (zero, zero))
        inverse = (ih_ref[...], il_ref[...])
        grad_signal = jnp.concatenate([dot_parts(inverse, parts_of(o_ref[u]), NN) for u in range(pair)], 0)
        grad_signal = grad_signal + skip_ref[...] * grad_conv
        gs_ref[1, :span] = grad_signal * values
        gs_ref[2, :span] = grad_signal * gate_in
        sum_ref[0:1] += column_sum(grad_conv * short[2] * gate_in)
        normed_grad = jnp.zeros((span, model), F32)
        for k in range(3):
            grad_short = gs_ref[k, :span]
            sum_ref[1 + k : 2 + k] += column_sum(grad_short)
            for t in range(3):
                row = 4 + 3 * t + k
                sum_ref[row : row + 1] += column_sum(grad_short * ext_ref[k, 6 + t : 6 + t + span])
            grad_proj = (
                conv_w_ref[2, k : k + 1, :] * grad_short
                + conv_w_ref[1, k : k + 1, :] * gs_ref[k, 1 : 1 + span]
                + conv_w_ref[0, k : k + 1, :] * gs_ref[k, 2 : 2 + span]
            )
            sum_ref[13 + k : 14 + k] += column_sum(grad_proj)
            gp_ref[0, k] = grad_proj
            normed_grad = normed_grad + dot_parts(parts_of(grad_proj), (wh_ref[k], wl_ref[k]), NT)
            gs_ref[k, span:] = gs_ref[k, :8]
        gn_ref[...] = normed_grad
        for u in range(pair):
            for k in range(count):
                start = pl.multiple_of(u * block + (me ^ k) * quarter, quarter)
                gn_refs[k][u] = gn_ref[pl.ds(start, quarter), :]

    last = blocks // pair - 1
    by_block = lambda *shape: pl.BlockSpec((1,) + shape, lambda s: (last - s,) + (0,) * len(shape))
    rim = pl.BlockSpec((1, 3, 8, width), lambda s: (jnp.maximum(last - s - 1, 0), 0, span // 8 - 1, 0))
    by_pair = lambda n: pl.BlockSpec((pair, quarter, n), lambda s: (last - s, 0, 0))
    fixed = [k_spec, conv_w, conv_b, skip, weight, *tables]
    spectra = struct((blocks, 2 * block, width))
    sums = struct((16, width))
    outs = run_kernel(
        body,
        "mixer_backward",
        (blocks // pair,),
        [scalar_spec(), scalar_spec()]
        + [pl.BlockSpec((pair, quarter // 2, 2 * width), lambda s: (last - s, 0, 0))] * count
        + [by_block(3, span, width), rim, by_block(span, width)]
        + [whole(a) for a in fixed],
        [whole(spectra), by_block(3, span, width), whole(sums)] + [by_pair(model)] * count,
        [spectra, struct((blocks // pair, 3, span, width)), sums] + [struct((blocks, quarter, model))] * count,
        [
            pltpu.VMEM((3, model, width), BF16),
            pltpu.VMEM((3, model, width), BF16),
            pltpu.VMEM((3, span + 8, width), F32),
            pltpu.VMEM((3, span + 8, width), F32),
            pltpu.VMEM((pair, 2 * block, width), F32),
            pltpu.VMEM((span, width), F32),
            pltpu.VMEM((span, model), F32),
        ],
        [own, length, *gm_parts, proj, proj, conv, *fixed],
        35,
    )
    return outs[:3], list(outs[3:])


def filter_backward(s_spec, g_spec, tables):
    blocks, double, width = s_spec.shape
    block = double // 2
    tile = min(32, block)
    inverse = tables[2:]

    def body(s_ref, g_ref, ih_ref, il_ref, out_ref, after_ref, o_ref):
        m = blocks - 1 - pl.program_id(0)

        @pl.when(m == blocks - 1)
        def _():
            after_ref[...] = jnp.zeros_like(after_ref)

        sign = parity_of(tile)
        for r in range(0, block, tile):
            lo = slice(r, r + tile)
            hi = slice(block + r, block + r + tile)

            def product(j, total, lo=lo, hi=hi):
                g_re, g_im = g_ref[j, lo], g_ref[j, hi]
                s_re, s_im = s_ref[j - m, lo], s_ref[j - m, hi]
                return total[0] + g_re * s_re + g_im * s_im, total[1] + g_im * s_re - g_re * s_im

            zero = jnp.zeros((tile, width), F32)
            re, im = lax.fori_loop(m, blocks, product, (zero, zero))
            o_ref[lo] = re + sign * after_ref[hi]
            o_ref[hi] = im - sign * after_ref[lo]
            after_ref[lo], after_ref[hi] = re, im
        out_ref[0] = dot_parts((ih_ref[...], il_ref[...]), parts_of(o_ref[...]), NN)

    return run_kernel(
        body,
        "filter_backward",
        (blocks,),
        [whole(s_spec), whole(g_spec), whole(inverse[0]), whole(inverse[1])],
        [pl.BlockSpec((1, block, width), lambda s: (blocks - 1 - s, 0, 0))],
        [struct((blocks, block, width))],
        [pltpu.VMEM((double, width), F32)] * 2,
        [s_spec, g_spec, *inverse],
        13,
    )[0]


def input_weight_grad(normed_high, normed_low, grad_proj):
    blocks, block, model = normed_high.shape
    width = grad_proj.shape[3]

    def body(nh_ref, nl_ref, gp_ref, out_ref):
        @pl.when(pl.program_id(0) == 0)
        def _():
            out_ref[...] = jnp.zeros_like(out_ref)

        normed = (nh_ref[0], nl_ref[0])
        for k in range(3):
            out_ref[k] += dot_parts(parts_of(gp_ref[0, k]), normed, TN)

    by_block = lambda *shape: pl.BlockSpec((1,) + shape, lambda b: (b,) + (0,) * len(shape))
    out = struct((3, width, model))
    return run_kernel(
        body,
        "input_weight_grad",
        (blocks,),
        [by_block(block, model)] * 2 + [by_block(3, block, width)],
        [whole(out)],
        [out],
        [],
        [normed_high, normed_low, grad_proj],
        12,
    )[0]


def input_backward(grad_pieces, x_own, grad_hidden, gain):
    rows, model = x_own.shape
    count = len(grad_pieces)
    step = min(256, rows)

    def body(*refs):
        piece_refs = refs[:count]
        x_ref, gh_ref, gain_ref, out_ref, sum_ref = refs[count:]

        @pl.when(pl.program_id(0) == 0)
        def _():
            sum_ref[...] = jnp.zeros_like(sum_ref)

        grad = sum(r[...] for r in piece_refs)
        unit, scale = normalise(x_ref[...])
        out_ref[...] = gh_ref[...] + norm_back(unit, scale, gain_ref[...], grad)
        sum_ref[0:1] += column_sum(grad * unit)
        sum_ref[1:2] += column_sum(grad)

    row_spec = pl.BlockSpec((step, model), lambda r: (r, 0))
    sums = struct((8, model))
    return run_kernel(
        body,
        "input_backward",
        (rows // step,),
        [row_spec] * (count + 2) + [whole(gain)],
        [row_spec, whole(sums)],
        [struct((rows, model)), sums],
        [],
        [*grad_pieces, x_own, grad_hidden, gain],
        5,
    )


def put_together(own, pieces):
    groups, quarter, model = pieces[0].shape
    count = len(pieces)
    pair = 2 - groups % 2

    def body(own_ref, *refs):
        for u in range(pair):
            for k in range(count):
                start = pl.multiple_of((own_ref[0] ^ k) * quarter, quarter)
                refs[count][u, pl.ds(start, quarter), :] = refs[k][u]

    by_group = lambda n: pl.BlockSpec((pair, n, model), lambda s: (s, 0, 0))
    return run_kernel(
        body,
        "put_together",
        (groups // pair,),
        [scalar_spec()] + [by_group(quarter)] * count,
        [by_group(quarter * count)],
        [struct((groups, quarter * count, model))],
        [],
        [own, *pieces],
        8,
    )[0]


def swap(values, axis, bit):
    size = lax.axis_size(axis)
    return lax.ppermute(values, axis, [(i, i ^ bit) for i in range(size)])


def total_over(values, axis):
    bit = 1
    while bit < lax.axis_size(axis):
        values = values + swap(values, axis, bit)
        bit *= 2
    return values


def meet(*values):
    return lax.optimization_barrier(values)


def split_rows(values, axis, bit):
    mine = (lax.axis_index(axis) // bit) % 2
    half = values.shape[0] // 2
    leaving = lax.dynamic_slice_in_dim(values, (1 - mine) * half, half, 0)
    staying = lax.dynamic_slice_in_dim(values, mine * half, half, 0)
    return leaving, staying


def join_rows(values, other, axis, bit):
    first = (lax.axis_index(axis) // bit) % 2 == 0
    return jnp.concatenate([jnp.where(first, values, other), jnp.where(first, other, values)], 0)


def transpose_blocks(values):
    return lax.all_to_all(values, "seq", split_axis=0, concat_axis=0, tiled=True)


def spread(values):
    far = swap(values, "chan", 2)
    return [values, swap(values, "chan", 1), far, swap(far, "chan", 1)]


def collect(pieces):
    far = pieces[2] + swap(pieces[3], "chan", 1)
    return [pieces[0], swap(pieces[1], "chan", 1), swap(far, "chan", 2)]


def pack(arrays):
    flat = jnp.concatenate([a.reshape(-1) for a in arrays])
    return jnp.pad(flat, (0, -flat.shape[0] % 1024))


def unpack(flat, arrays):
    out = []
    start = 0
    for a in arrays:
        size = math.prod(a.shape)
        out.append(flat[start : start + size].reshape(a.shape))
        start += size
    return out


def sequence_device(
    block_input,
    lengths,
    ln1_gain,
    ln1_bias,
    input_weight,
    input_bias,
    conv_w,
    conv_b,
    filt_w1,
    filt_b1,
    filt_w2,
    filt_b2,
    filt_w3,
    decay,
    skip,
    output_weight,
    output_bias,
    ln2_gain,
    ln2_bias,
    up_weight,
    up_bias,
    down_weight,
    down_bias,
    cotangent,
):
    blocks, block, model = block_input.shape
    count = lax.axis_size("chan")
    quarter = block // count
    rows = blocks * quarter
    width = decay.shape[0]
    seq_length = blocks * block
    seq_index = lax.axis_index("seq")
    chan_index = lax.axis_index("chan")
    own = chan_index.astype(jnp.int32).reshape(1)
    length = lax.dynamic_slice(lengths, (seq_index,), (1,))
    tables = wave_tables(block)
    row = lambda v: v.reshape(1, -1)

    def own_rows(values):
        part = lax.dynamic_slice_in_dim(values, chan_index * quarter, quarter, 1)
        return transpose_blocks(part)

    place_values = jnp.arange(seq_length, dtype=jnp.int32).astype(F32)
    features = position_features(place_values, seq_length, filt_w1.shape[0])
    kernel, filter_pull = jax.vjp(
        partial(implicit_filter, features, place_values), filt_w1, filt_b1, filt_w2, filt_b2, filt_w3, decay
    )
    k_spec = filter_spectrum(kernel.reshape(blocks, block, width), tables)
    weight = jnp.transpose(input_weight, (1, 0, 2))

    x_own = own_rows(block_input)
    side = (seq_index % 2).astype(jnp.int32)

    def half_of(values, axis):
        half = values.shape[axis] // 2
        return lax.dynamic_slice_in_dim(values, side * half, half, axis)

    up_far = swap(half_of(up_weight, 0), "chan", 2)
    up_bias_parts = [swap(up_bias, "chan", k) if k else up_bias for k in range(count)]
    x_own, k_spec, weight, up_far, up_bias_parts, cotangent_home = meet(
        x_own, k_spec, weight, up_far, up_bias_parts, cotangent
    )
    x_far = swap(x_own, "chan", 2)
    x_parts = [x_own, swap(x_own, "chan", 1), x_far, swap(x_far, "chan", 1)]
    cot_own = own_rows(cotangent_home)
    x_rows = x_own.reshape(rows, model)
    x_parts[2], out_home, down_home, up_far = meet(x_parts[2], output_weight, down_weight, up_far)
    out_far = swap(out_home, "chan", 2)
    down_far = swap(half_of(down_home, 1), "chan", 2)
    up_other = swap(up_far, "seq", 1)
    x_parts[0], cot_own = meet(x_parts[0], cot_own)
    cot_own = cot_own.reshape(rows, model)

    (normed_high, normed_low, proj, conv, s_spec), mixed = mixer_forward(
        own, length, x_parts, row(ln1_gain), row(ln1_bias), weight, input_bias, conv_w, conv_b, row(skip), k_spec, tables
    )
    *mixed, down_far, out_far, up_other = meet(*mixed, down_far, out_far, up_other)
    mixed = [m if k == 0 else swap(m, "chan", k) for k, m in enumerate(mixed)]
    down_other = swap(down_far, "seq", 1)
    out_3 = swap(out_far, "chan", 1)
    *mixed, out_3 = meet(*mixed, out_3)
    out_parts = [output_weight, swap(output_weight, "chan", 1), out_far, out_3]
    up_parts = [[up_weight], [swap(up_weight, "chan", 1)], [up_far, up_other]]
    up_parts.append([swap(u, "chan", 1) for u in up_parts[2]])
    down_side = swap(down_far, "chan", 1)

    hidden, *rest = hidden_forward(
        mixed, out_parts, x_rows, cot_own, row(output_bias), row(ln2_gain), row(ln2_bias)
    )
    rest, down_other, down_side = meet(rest, down_other, down_side)
    normed2, turned, cot_parts = rest[0:2], rest[2:4], rest[4:6]
    down_parts = [[down_weight], [swap(down_weight, "chan", 1)], [down_far, down_other]]
    down_parts.append([down_side, swap(down_other, "chan", 1)])

    def units(k, sums):
        return feed_forward(
            side.reshape(1), normed2, turned, cot_parts, up_parts[k], row(up_bias_parts[k]), down_parts[k], sums
        )

    bias_grads = [None] * count
    sums, (up_3, down_3, bias_grads[3]) = units(3, None)
    up_3, down_3 = swap(up_3, "chan", 1), swap(down_3, "chan", 1)
    sums, (up_2, down_2, bias_grads[2]) = units(2, sums)
    *sums, up_2, up_3, down_2, down_3 = meet(*sums, up_2, up_3, down_2, down_3)

    third = model // 3
    far_up = lambda i: up_2[i * third : (i + 1) * third] + up_3[i * third : (i + 1) * third]
    leaving_2, staying_2 = split_rows(down_2, "seq", 1)
    leaving_3, staying_3 = split_rows(down_3, "seq", 1)
    far_ups = [swap(up_2[: 2 * third] + up_3[: 2 * third], "chan", 2)]
    came = swap(leaving_2 + leaving_3, "seq", 1)
    sums, near_bias, (up_1, up_0), (down_1, down_0) = feed_forward_pair(
        normed2, turned, cot_parts, [up_parts[1][0], up_parts[0][0]], [row(up_bias_parts[1]), row(up_bias_parts[0])],
        [down_parts[1][0], down_parts[0][0]], sums,
    )
    bias_grads[1], bias_grads[0] = jnp.split(near_bias, 2, 1)
    *sums, far_ups[0], came, up_1, down_1 = meet(*sums, far_ups[0], came, up_1, down_1)
    down_1, up_1 = swap(down_1, "chan", 1), swap(up_1, "chan", 1)
    far_ups.append(swap(up_2[2 * third :] + up_3[2 * third :], "chan", 2))
    leaving, far_staying = split_rows(staying_2 + staying_3 + came, "seq", 2)
    far_came = swap(leaving, "seq", 2)
    leaving_0, staying_0 = split_rows(down_0, "seq", 1)
    leaving_1, staying_1 = split_rows(down_1, "seq", 1)
    near_leaving = leaving_0 + leaving_1
    near_leaving, *sums = meet(near_leaving, *sums)
    near_came = swap(near_leaving, "seq", 1)
    (out_rows, grad_hidden, sums2), grad_mixed, (out_near, out_far) = hidden_backward(
        hidden, sums[0], sums[1], cot_own, mixed, out_parts, row(ln2_gain), row(down_bias)
    )
    grad_hidden, far_ups[1], far_came, grad_mixed, out_rows, up_1 = meet(
        grad_hidden, far_ups[1], far_came, grad_mixed, out_rows, up_1
    )

    grad_mixed = [g if k == 0 else swap(g, "chan", k) for k, g in enumerate(grad_mixed)]
    leaving, far_staying = split_rows(far_staying + far_came, "seq", 4)
    far_came = swap(leaving, "seq", 4)
    out_blocks = transpose_blocks(out_rows.reshape(blocks, quarter, model))
    grad_up = up_0 + up_1 + jnp.concatenate(far_ups, 0)
    up_leaving, up_staying = split_rows(grad_up, "seq", 1)
    grad_mixed, up_leaving, up_staying, out_far, near_came = meet(
        grad_mixed, up_leaving, up_staying, out_far, near_came
    )

    up_came = swap(up_leaving, "seq", 1)
    leaving, near_staying = split_rows(staying_0 + staying_1 + near_came, "seq", 2)
    near_came = swap(leaving, "seq", 2)
    out_far = swap(out_far, "chan", 2)
    (g_spec, grad_proj, mixer_sums), grad_normed = mixer_backward(
        own, length, grad_mixed, proj, conv, s_spec, k_spec, conv_w, conv_b, row(skip), weight, tables
    )
    grad_normed, grad_proj, out_far, near_came, up_came, out_blocks, far_came = meet(
        grad_normed, grad_proj, out_far, near_came, up_came, out_blocks, far_came
    )

    grad_normed[3], grad_normed[1] = swap(grad_normed[3], "chan", 1), swap(grad_normed[1], "chan", 1)
    far_down = swap(far_staying + far_came, "chan", 2)
    leaving, near_staying = split_rows(near_staying + near_came, "seq", 4)
    up_leaving, up_staying = split_rows(up_staying + up_came, "seq", 2)
    far_normed, grad_proj, leaving, up_leaving = meet(
        grad_normed[2] + grad_normed[3], grad_proj, leaving, up_leaving
    )
    far_normed = swap(far_normed, "chan", 2)
    near_came, up_came = swap(leaving, "seq", 4), swap(up_leaving, "seq", 2)
    grad_in = input_weight_grad(normed_high, normed_low, grad_proj)
    grad_out = out_near[0] + out_far[0] + swap(out_near[1] + out_far[1], "chan", 1)
    g_spec, grad_in, grad_out, near_came, far_down, up_came = meet(
        g_spec, grad_in, grad_out, near_came, far_down, up_came
    )

    grad_down = near_staying + near_came + far_down
    down_came = swap(grad_down, "seq", 4)
    up_leaving, up_staying = split_rows(up_staying + up_came, "seq", 4)
    up_came = swap(up_leaving, "seq", 4)
    mixer_leaving, mixer_staying = split_rows(
        jnp.concatenate([grad_in.reshape(-1, model), grad_out], 0), "seq", 1
    )
    mixer_came = swap(mixer_leaving, "seq", 1)
    grad_kernel = filter_backward(s_spec, g_spec, tables).reshape(seq_length, width)
    far_normed, grad_kernel, down_came, up_came = meet(far_normed, grad_kernel, down_came, up_came)

    pieces = [p.reshape(rows, model) for p in (grad_normed[0], grad_normed[1], far_normed)]
    grad_x_rows, sums1 = input_backward(pieces, x_rows, grad_hidden, row(ln1_gain))
    grad_x_rows, grad_kernel, out_blocks, mixer_came, down_came, up_came, sums1 = meet(
        grad_x_rows, grad_kernel, out_blocks, mixer_came, down_came, up_came, sums1
    )

    grad_x_blocks = transpose_blocks(grad_x_rows.reshape(blocks, quarter, model))
    leaving, staying = split_rows(mixer_staying + mixer_came, "seq", 2)
    came = swap(leaving, "seq", 2)
    grad_up, grad_down = up_staying + up_came, join_rows(grad_down, down_came, "seq", 4)
    down_came, up_came = swap(grad_down, "seq", 2), swap(grad_up, "seq", 4)
    out_far = swap(out_blocks, "chan", 2)
    grad_fw1, grad_fb1, grad_fw2, grad_fb2, grad_fw3, grad_decay = filter_pull(grad_kernel)
    up_bias_grads = jnp.take(
        jnp.concatenate(bias_grads, 0), jnp.arange(count, dtype=jnp.int32) ^ chan_index, axis=0
    )
    shared = [sums1[0], sums1[1], *[sums2[i] for i in range(4)], up_bias_grads, grad_fw1, grad_fb1, grad_fw2, grad_fb2]
    split = [mixer_sums, grad_fw3, grad_decay]
    shared_flat, split_flat = pack(shared), pack(split)
    shared_flat = shared_flat + swap(shared_flat, "chan", 1)
    side_flat = swap(shared_flat, "chan", 2)
    grad_x_blocks, came, up_came, down_came, side_flat, out_far, out_blocks = meet(
        grad_x_blocks, came, up_came, down_came, side_flat, out_far, out_blocks
    )

    grad_x_far = swap(grad_x_blocks, "chan", 2)
    grad_up, grad_down = join_rows(grad_up, up_came, "seq", 4), join_rows(grad_down, down_came, "seq", 2)
    down_came, up_came = swap(grad_down, "seq", 1), swap(grad_up, "seq", 2)
    leaving, staying = split_rows(staying + came, "seq", 4)
    came = swap(leaving, "seq", 4)
    came, up_came, grad_x_blocks, out_far, out_blocks = meet(came, up_came, grad_x_blocks, out_far, out_blocks)

    mixer_grads = staying + came
    came = swap(mixer_grads, "seq", 4)
    grad_up = join_rows(grad_up, up_came, "seq", 2)
    up_came = swap(grad_up, "seq", 1)
    flat = jnp.concatenate([shared_flat + side_flat, split_flat])
    side_flat = swap(flat, "seq", 2)
    came, grad_x_far, side_flat, grad_x_blocks, out_far, out_blocks, down_came = meet(
        came, grad_x_far, side_flat, grad_x_blocks, out_far, out_blocks, down_came
    )

    mixer_grads = join_rows(mixer_grads, came, "seq", 4)
    came = swap(mixer_grads, "seq", 2)
    grad_x_near, grad_x_side = swap(grad_x_blocks, "chan", 1), swap(grad_x_far, "chan", 1)
    flat = flat + side_flat
    side_flat = swap(flat, "seq", 4)
    grad_down = join_rows(grad_down, down_came, "seq", 1)
    came, side_flat, grad_x_near, grad_x_side, out_far, out_blocks = meet(
        came, side_flat, grad_x_near, grad_x_side, out_far, out_blocks
    )
    flat = flat + side_flat
    side_flat = swap(flat, "seq", 1)
    mixer_grads = join_rows(mixer_grads, came, "seq", 2)
    came = swap(mixer_grads, "seq", 1)
    out_near, out_side = swap(out_blocks, "chan", 1), swap(out_far, "chan", 1)
    grad_x = put_together(own, [grad_x_blocks, grad_x_near, grad_x_far, grad_x_side])
    up_came, side_flat, out_near, out_side, grad_x = meet(up_came, side_flat, out_near, out_side, grad_x)
    flat = flat + side_flat
    grad_up = join_rows(grad_up, up_came, "seq", 1)
    output = put_together(own, [out_blocks, out_near, out_far, out_side])
    cut = shared_flat.shape[0]
    grad_ln1_gain, grad_ln1_bias, grad_ln2_gain, grad_ln2_bias, grad_b_out, grad_b_fc2, up_bias_grads, *filt = unpack(
        flat[:cut], shared
    )
    mixer_sums, grad_fw3, grad_decay = unpack(flat[cut:], split)
    grad_b_fc1 = lax.dynamic_slice_in_dim(up_bias_grads, chan_index, 1, 0)[0]
    grad_skip = mixer_sums[0]
    grad_conv_b = mixer_sums[1:4]
    grad_conv_w = mixer_sums[4:13].reshape(3, 3, width)
    grad_b_in = mixer_sums[13:16]
    small = (
        [grad_ln1_gain, grad_ln1_bias, grad_ln2_gain, grad_ln2_bias, grad_b_out, grad_b_fc2, grad_b_fc1]
        + [*filt, grad_fw3, grad_decay, grad_skip, grad_conv_b, grad_conv_w, grad_b_in]
    )
    output, grad_up, came, small = meet(output, grad_up, came, small)
    grad_ln1_gain, grad_ln1_bias, grad_ln2_gain, grad_ln2_bias, grad_b_out, grad_b_fc2, grad_b_fc1 = small[:7]
    *filt, grad_fw3, grad_decay, grad_skip, grad_conv_b, grad_conv_w, grad_b_in = small[7:]
    mixer_grads = join_rows(mixer_grads, came, "seq", 1)
    grad_in = jnp.transpose(mixer_grads[: 3 * width].reshape(3, width, model), (2, 0, 1))
    grad_out = mixer_grads[3 * width :]
    return (
        output,
        grad_x,
        grad_ln1_gain,
        grad_ln1_bias,
        grad_in,
        grad_b_in,
        grad_conv_w,
        grad_conv_b,
        *filt,
        grad_fw3,
        grad_decay,
        grad_skip,
        grad_out,
        grad_b_out,
        grad_ln2_gain,
        grad_ln2_bias,
        grad_up,
        grad_b_fc1,
        grad_down,
        grad_b_fc2,
    )


def solution(mesh):
    in_specs = (
        P(None, "seq", None),
        P(),
        P(),
        P(),
        P(None, None, "chan"),
        P(None, "chan"),
        P(None, None, "chan"),
        P(None, "chan"),
        P(),
        P(),
        P(),
        P(),
        P(None, "chan"),
        P("chan"),
        P("chan"),
        P("chan", None),
        P(),
        P(),
        P(),
        P(None, "chan"),
        P("chan"),
        P("chan", None),
        P(),
        P(None, "seq", None),
    )
    out_specs = (
        P(None, "seq", None),
        P(None, "seq", None),
        P(),
        P(),
        P(None, None, "chan"),
        P(None, "chan"),
        P(None, None, "chan"),
        P(None, "chan"),
        P(),
        P(),
        P(),
        P(),
        P(None, "chan"),
        P("chan"),
        P("chan"),
        P("chan", None),
        P(),
        P(),
        P(),
        P(None, "chan"),
        P("chan"),
        P("chan", None),
        P(),
    )
    chan = mesh.shape["chan"]

    def step(*arrays):
        sequences, seq_length = arrays[0].shape[:2]
        whole_sequences = sequences == mesh.shape["seq"] and chan == 4 and seq_length % (64 * sequences) == 0
        body = sequence_device if whole_sequences else spectral_device
        return jax.shard_map(
            body, mesh=mesh, in_specs=in_specs, out_specs=out_specs, check_vma=False
        )(*arrays)

    return step
```

```python
from functools import partial
import math

import jax
import jax.numpy as jnp
import ml_dtypes
import numpy as np
from jax import lax
from jax.experimental import pallas as pl
from jax.experimental.pallas import tpu as pltpu
from jax.sharding import PartitionSpec as P

EPSILON = 1e-05
HIGH_ACCURACY = lax.Precision.HIGHEST


def shifted(block, axis, distance):
    devices = range(lax.axis_size(axis))
    route = [(i - distance, i) for i in devices if i - distance in devices]
    return lax.ppermute(block, axis, route)


def layer_norm(values, gain, offset):
    average = jnp.mean(values, -1, keepdims=True)
    centered = values - average
    variance = jnp.mean(centered * centered, -1, keepdims=True)
    return centered * lax.rsqrt(variance + EPSILON) * gain + offset


def position_features(place_values, seq_length, emb_width):
    band_count = (emb_width - 1) // 2
    frequency = jnp.linspace(0.0001, band_count - 1, band_count).astype(jnp.float32)
    phases = 2.0 * math.pi * place_values[:, None] * frequency[None, :] / seq_length
    return jnp.concatenate(
        [(place_values / (seq_length - 1))[:, None], jnp.cos(phases), -jnp.sin(phases)], 1
    )


def implicit_filter(features, place_values, filt_w1, filt_b1, filt_w2, filt_b2, filt_w3, decay):
    first_layer = jnp.sin(jnp.dot(features, filt_w1, precision=HIGH_ACCURACY) + filt_b1)
    second_layer = jnp.sin(jnp.dot(first_layer, filt_w2, precision=HIGH_ACCURACY) + filt_b2)
    raw_kernel = jnp.dot(second_layer, filt_w3, precision=HIGH_ACCURACY)
    return raw_kernel * jnp.exp(-decay[None, :] * place_values[:, None])


def exact_gelu(values):
    return jax.nn.gelu(values, approximate=False)


def tables(count_rows, count_cols):
    turns = (
        jnp.arange(count_rows, dtype=jnp.int32)[:, None]
        * jnp.arange(count_cols, dtype=jnp.int32)[None, :]
        % count_rows
    )
    phases = turns.astype(jnp.float32) * (2.0 * math.pi / count_rows)
    return (jnp.cos(phases), jnp.sin(phases))


def rotate(cos_tab, sin_tab, real, imag, sign, form):
    first_part = jnp.einsum(form, cos_tab, real, precision=HIGH_ACCURACY)
    second_part = jnp.einsum(form, sin_tab, imag, precision=HIGH_ACCURACY)
    third_part = jnp.einsum(form, cos_tab, imag, precision=HIGH_ACCURACY)
    fourth_part = jnp.einsum(form, sin_tab, real, precision=HIGH_ACCURACY)
    return (first_part - sign * second_part, third_part + sign * fourth_part)


def to_spectrum(cos_tab, sin_tab, signal):
    real = jnp.einsum("wp,spc->swc", cos_tab, signal, precision=HIGH_ACCURACY)
    imag = -jnp.einsum("wp,spc->swc", sin_tab, signal, precision=HIGH_ACCURACY)
    return (real, imag)


def time_domain(cos_tab, sin_tab, real, imag):
    return jnp.einsum("wp,swc->spc", cos_tab, real, precision=HIGH_ACCURACY) - jnp.einsum(
        "wp,swc->spc", sin_tab, imag, precision=HIGH_ACCURACY
    )


def earlier_block(values):
    return jnp.pad(values, ((0, 0), (1, 0), (0, 0), (0, 0)))[:, :-1]


def later_block(values):
    return jnp.pad(values, ((0, 0), (0, 1), (0, 0), (0, 0)))[:, 1:]


def spectral_device(
    block_input,
    lengths,
    ln1_gain,
    ln1_bias,
    input_weight,
    input_bias,
    conv_w,
    conv_b,
    filt_w1,
    filt_b1,
    filt_w2,
    filt_b2,
    filt_w3,
    decay,
    skip,
    output_weight,
    output_bias,
    ln2_gain,
    ln2_bias,
    up_weight,
    up_bias,
    down_weight,
    down_bias,
    cotangent,
):
    block = block_input.shape[1]
    blocks = lax.axis_size("seq")
    share = 2 * block // blocks
    seq_index = lax.axis_index("seq")
    places = seq_index * block + jnp.arange(block, dtype=jnp.int32)
    place_values = places.astype(jnp.float32)
    mask = (places[None, :] < lengths[:, None]).astype(jnp.float32)[:, :, None]
    first_normed, norm1_pull = jax.vjp(layer_norm, block_input, ln1_gain, ln1_bias)
    input_projected = (
        jnp.einsum("spd,dkc->spkc", first_normed, input_weight, precision=HIGH_ACCURACY)
        + input_bias
    )
    rims = shifted(input_projected[:, block - 2 :], "seq", 1)
    extended = jnp.concatenate([rims, input_projected], 1)
    short = (
        conv_w[0] * extended[:, :block]
        + conv_w[1] * extended[:, 1 : block + 1]
        + conv_w[2] * extended[:, 2:]
        + conv_b
    )
    gate_out = short[:, :, 0]
    gate_in = short[:, :, 1]
    values = short[:, :, 2]
    signal = values * gate_in * mask
    cos_tab, sin_tab = tables(2 * block, block)
    block_cos, block_sin = tables(2 * blocks, blocks)
    own_freq = seq_index * share + jnp.arange(share, dtype=jnp.int32)
    parity = (1 - 2 * (own_freq % 2)).astype(jnp.float32)[:, None]
    features = position_features(place_values, blocks * block, filt_w1.shape[0])
    kernel, filter_pull = jax.vjp(
        partial(implicit_filter, features, place_values),
        filt_w1,
        filt_b1,
        filt_w2,
        filt_b2,
        filt_w3,
        decay,
    )
    signal_re, signal_im = to_spectrum(cos_tab, sin_tab, signal)
    kernel_re, kernel_im = to_spectrum(cos_tab, sin_tab, kernel[None])
    signal_re, signal_im, kernel_re, kernel_im = (
        lax.all_to_all(signal_re[:, None], "seq", split_axis=2, concat_axis=1, tiled=True),
        lax.all_to_all(signal_im[:, None], "seq", split_axis=2, concat_axis=1, tiled=True),
        lax.all_to_all(kernel_re[:, None], "seq", split_axis=2, concat_axis=1, tiled=True),
        lax.all_to_all(kernel_im[:, None], "seq", split_axis=2, concat_axis=1, tiled=True),
    )
    zq_re, zq_im = rotate(block_cos, block_sin, signal_re, signal_im, -1.0, "qk,skfc->sqfc")
    hq_re, hq_im = rotate(block_cos, block_sin, kernel_re, kernel_im, -1.0, "qk,skfc->sqfc")
    prod_re = zq_re * hq_re - zq_im * hq_im
    prod_im = zq_re * hq_im + zq_im * hq_re
    joined_re, joined_im = rotate(block_cos, block_sin, prod_re, prod_im, 1.0, "qj,sqfc->sjfc")
    joined_re = joined_re / (2 * blocks)
    joined_im = joined_im / (2 * blocks)
    folded_re = joined_re + parity * earlier_block(joined_re)
    folded_im = joined_im + parity * earlier_block(joined_im)
    folded_re, folded_im = (
        lax.all_to_all(folded_re, "seq", split_axis=1, concat_axis=2, tiled=True),
        lax.all_to_all(folded_im, "seq", split_axis=1, concat_axis=2, tiled=True),
    )
    convolved = time_domain(cos_tab, sin_tab, folded_re[:, 0], folded_im[:, 0]) / (2 * block)
    conv_sum = convolved + skip * signal
    mixer_output = conv_sum * gate_out
    partial_mix = jnp.einsum("spc,cd->spd", mixer_output, output_weight, precision=HIGH_ACCURACY)
    hidden_state = block_input + lax.psum(partial_mix, "chan") + output_bias
    second_normed2 = layer_norm(hidden_state, ln2_gain, ln2_bias)
    before = jnp.einsum("spd,df->spf", second_normed2, up_weight, precision=HIGH_ACCURACY) + up_bias
    active_units, gelu_pull = jax.vjp(exact_gelu, before)
    feed = lax.psum(
        jnp.einsum("spf,fd->spd", active_units, down_weight, precision=HIGH_ACCURACY), "chan"
    )
    output = hidden_state + feed + down_bias
    grad_b_fc2 = jnp.sum(cotangent, (0, 1))
    grad_w_fc2 = jnp.einsum("spf,spd->fd", active_units, cotangent, precision=HIGH_ACCURACY)
    grad_active = jnp.einsum("spd,fd->spf", cotangent, down_weight, precision=HIGH_ACCURACY)
    grad_before = gelu_pull(grad_active)[0]
    grad_w_fc1 = jnp.einsum("spd,spf->df", second_normed2, grad_before, precision=HIGH_ACCURACY)
    grad_b_fc1 = jnp.sum(grad_before, (0, 1))
    grad_normed2 = lax.psum(
        jnp.einsum("spf,df->spd", grad_before, up_weight, precision=HIGH_ACCURACY), "chan"
    )
    norm2_pull = jax.vjp(layer_norm, hidden_state, ln2_gain, ln2_bias)[1]
    grad_hidden_norm, grad_ln2_gain, grad_ln2_bias = norm2_pull(grad_normed2)
    grad_hidden = cotangent + grad_hidden_norm
    grad_b_out = jnp.sum(grad_hidden, (0, 1))
    grad_w_out = jnp.einsum("spc,spd->cd", mixer_output, grad_hidden, precision=HIGH_ACCURACY)
    grad_mixed = jnp.einsum("spd,cd->spc", grad_hidden, output_weight, precision=HIGH_ACCURACY)
    grad_conv = grad_mixed * gate_out
    grad_gate_out = grad_mixed * conv_sum
    grad_skip = jnp.sum(grad_conv * signal, (0, 1))
    back_re, back_im = to_spectrum(cos_tab, sin_tab, grad_conv)
    back_re = back_re / (2 * block)
    back_im = back_im / (2 * block)
    back_re, back_im = (
        lax.all_to_all(back_re[:, None], "seq", split_axis=2, concat_axis=1, tiled=True),
        lax.all_to_all(back_im[:, None], "seq", split_axis=2, concat_axis=1, tiled=True),
    )
    unfold_re = back_re + parity * later_block(back_re)
    unfold_im = back_im + parity * later_block(back_im)
    dprod_re, dprod_im = rotate(block_cos, block_sin, unfold_re, unfold_im, -1.0, "qj,sjfc->sqfc")
    dprod_re = dprod_re / (2 * blocks)
    dprod_im = dprod_im / (2 * blocks)
    dzq_re = hq_re * dprod_re + hq_im * dprod_im
    dzq_im = hq_re * dprod_im - hq_im * dprod_re
    dhq_re = jnp.sum(zq_re * dprod_re + zq_im * dprod_im, 0, keepdims=True)
    dhq_im = jnp.sum(zq_re * dprod_im - zq_im * dprod_re, 0, keepdims=True)
    dsig_re, dsig_im = rotate(block_cos, block_sin, dzq_re, dzq_im, 1.0, "qk,sqfc->skfc")
    dker_re, dker_im = rotate(block_cos, block_sin, dhq_re, dhq_im, 1.0, "qk,sqfc->skfc")
    dsig_re, dsig_im, dker_re, dker_im = (
        lax.all_to_all(dsig_re, "seq", split_axis=1, concat_axis=2, tiled=True),
        lax.all_to_all(dsig_im, "seq", split_axis=1, concat_axis=2, tiled=True),
        lax.all_to_all(dker_re, "seq", split_axis=1, concat_axis=2, tiled=True),
        lax.all_to_all(dker_im, "seq", split_axis=1, concat_axis=2, tiled=True),
    )
    grad_signal = time_domain(cos_tab, sin_tab, dsig_re[:, 0], dsig_im[:, 0]) + grad_conv * skip
    grad_kernel = time_domain(cos_tab, sin_tab, dker_re[:, 0], dker_im[:, 0])[0]
    grad_fw1, grad_fb1, grad_fw2, grad_fb2, grad_fw3, grad_decay = filter_pull(grad_kernel)
    grad_short = jnp.stack(
        [grad_gate_out, grad_signal * values * mask, grad_signal * gate_in * mask], 2
    )
    grad_conv_b = jnp.sum(grad_short, (0, 1))
    grad_conv_w = jnp.stack(
        [jnp.sum(grad_short * extended[:, offset : offset + block], (0, 1)) for offset in range(3)]
    )
    grad_extended = (
        jnp.pad(conv_w[0] * grad_short, ((0, 0), (0, 2), (0, 0), (0, 0)))
        + jnp.pad(conv_w[1] * grad_short, ((0, 0), (1, 1), (0, 0), (0, 0)))
        + jnp.pad(conv_w[2] * grad_short, ((0, 0), (2, 0), (0, 0), (0, 0)))
    )
    returned = shifted(grad_extended[:, :2], "seq", -1)
    grad_proj = grad_extended[:, 2:] + jnp.pad(returned, ((0, 0), (block - 2, 0), (0, 0), (0, 0)))
    grad_b_in = jnp.sum(grad_proj, (0, 1))
    grad_w_in = jnp.einsum("spd,spkc->dkc", first_normed, grad_proj, precision=HIGH_ACCURACY)
    grad_normed = lax.psum(
        jnp.einsum("spkc,dkc->spd", grad_proj, input_weight, precision=HIGH_ACCURACY), "chan"
    )
    grad_x_norm, grad_ln1_gain, grad_ln1_bias = norm1_pull(grad_normed)
    grad_x = grad_hidden + grad_x_norm
    (
        grad_ln1_gain,
        grad_ln1_bias,
        grad_w_in,
        grad_b_in,
        grad_conv_w,
        grad_conv_b,
        grad_fw3,
        grad_decay,
        grad_skip,
        grad_w_out,
        grad_b_out,
        grad_ln2_gain,
        grad_ln2_bias,
        grad_w_fc1,
        grad_b_fc1,
        grad_w_fc2,
        grad_b_fc2,
    ) = lax.psum(
        (
            grad_ln1_gain,
            grad_ln1_bias,
            grad_w_in,
            grad_b_in,
            grad_conv_w,
            grad_conv_b,
            grad_fw3,
            grad_decay,
            grad_skip,
            grad_w_out,
            grad_b_out,
            grad_ln2_gain,
            grad_ln2_bias,
            grad_w_fc1,
            grad_b_fc1,
            grad_w_fc2,
            grad_b_fc2,
        ),
        "seq",
    )
    grad_fw1, grad_fb1, grad_fw2, grad_fb2 = lax.psum(
        (grad_fw1, grad_fb1, grad_fw2, grad_fb2), ("seq", "chan")
    )
    return (
        output,
        grad_x,
        grad_ln1_gain,
        grad_ln1_bias,
        grad_w_in,
        grad_b_in,
        grad_conv_w,
        grad_conv_b,
        grad_fw1,
        grad_fb1,
        grad_fw2,
        grad_fb2,
        grad_fw3,
        grad_decay,
        grad_skip,
        grad_w_out,
        grad_b_out,
        grad_ln2_gain,
        grad_ln2_bias,
        grad_w_fc1,
        grad_b_fc1,
        grad_w_fc2,
        grad_b_fc2,
    )


F32 = jnp.float32
BF16 = jnp.bfloat16
NN = (((1,), (0,)), ((), ()))
NT = (((1,), (1,)), ((), ()))
TN = (((0,), (0,)), ((), ()))
VMEM_BYTES = 56 * 2**20


def parts_of(values):
    high = values.astype(BF16)
    return high, (values - high.astype(F32)).astype(BF16)


def dot_parts(left, right, dims):
    def one(a, b):
        return lax.dot_general(a, b, dims, preferred_element_type=F32)

    return one(left[0], right[0]) + (one(left[0], right[1]) + one(left[1], right[0]))


def normalise(values):
    average = jnp.mean(values, -1, keepdims=True)
    centered = values - average
    variance = jnp.mean(centered * centered, -1, keepdims=True)
    scale = lax.rsqrt(variance + EPSILON)
    return centered * scale, scale


def norm_back(unit, scale, gain, grad):
    lifted = grad * gain
    mean_one = jnp.mean(lifted, -1, keepdims=True)
    mean_two = jnp.mean(lifted * unit, -1, keepdims=True)
    return scale * (lifted - mean_one - unit * mean_two)


def fold(rows):
    half = rows.shape[0] // 2
    return jnp.concatenate([rows[:half], rows[half:]], 1)


def unfold(folded):
    width = folded.shape[1] // 2
    return jnp.concatenate([folded[:, :width], folded[:, width:]], 0)


def column_sum(values):
    return jnp.sum(values, 0, keepdims=True)


def whole(array):
    return pl.BlockSpec(array.shape, lambda *_: (0,) * len(array.shape))


def scalar_spec():
    return pl.BlockSpec(memory_space=pltpu.SMEM)


def struct(shape, kind=F32):
    return jax.ShapeDtypeStruct(tuple(shape), kind)


def run_kernel(body, name, grid, in_specs, out_specs, out_shape, scratch, args, micros):
    return pl.pallas_call(
        body,
        name=name,
        grid=grid,
        in_specs=in_specs,
        out_specs=out_specs,
        out_shape=out_shape,
        scratch_shapes=scratch,
        compiler_params=pltpu.CompilerParams(
            dimension_semantics=("arbitrary",) * len(grid), vmem_limit_bytes=VMEM_BYTES
        ),
        cost_estimate=pl.CostEstimate(
            flops=int(micros * 1.15e9), bytes_accessed=int(micros * 3.6e6), transcendentals=0
        ),
    )(*args)


def wave_tables(block):
    angles = np.pi * np.outer(2 * np.arange(block) + 1, np.arange(block)) / (2 * block)
    table = np.concatenate([np.cos(angles), -np.sin(angles)], 0)

    def both(values):
        high = values.astype(ml_dtypes.bfloat16)
        low = (values - high.astype(np.float64)).astype(ml_dtypes.bfloat16)
        return jnp.asarray(high), jnp.asarray(low)

    return both(table) + both(table.T / block)


def parity_of(rows):
    odd = lax.broadcasted_iota(jnp.int32, (rows, 1), 0) % 2
    return (1 - 2 * odd).astype(F32)


def filter_spectrum(kernel, tables):
    blocks, block, width = kernel.shape
    table_high, table_low = tables[:2]

    def body(kernel_ref, high_ref, low_ref, out_ref, before_ref):
        @pl.when(pl.program_id(0) == 0)
        def _():
            before_ref[...] = jnp.zeros_like(before_ref)

        spectrum = dot_parts((high_ref[...], low_ref[...]), parts_of(kernel_ref[0]), NN)
        sign = parity_of(block)
        out_ref[0, :block] = spectrum[:block] - sign * before_ref[block:]
        out_ref[0, block:] = spectrum[block:] + sign * before_ref[:block]
        before_ref[...] = spectrum

    return run_kernel(
        body,
        "filter_spectrum",
        (blocks,),
        [pl.BlockSpec((1, block, width), lambda b: (b, 0, 0)), whole(table_high), whole(table_low)],
        [pl.BlockSpec((1, 2 * block, width), lambda b: (b, 0, 0))],
        [struct((blocks, 2 * block, width))],
        [pltpu.VMEM((2 * block, width), F32)],
        [kernel, table_high, table_low],
        8,
    )[0]


def mixer_forward(own, length, x_parts, gain, offset, weight, bias, conv_w, conv_b, skip, spectrum, tables):
    blocks, quarter, model = x_parts[0].shape
    count = len(x_parts)
    block = quarter * count
    width = weight.shape[2]
    tile = min(32, block)
    pair = 2 - blocks % 2
    span = pair * block

    def body(*refs):
        own_ref, length_ref = refs[:2]
        x_refs = refs[2 : 2 + count]
        refs = refs[2 + count :]
        gain_ref, offset_ref, weight_ref, bias_ref, conv_w_ref, conv_b_ref, skip_ref, k_ref = refs[:8]
        th_ref, tl_ref, ih_ref, il_ref = refs[8:12]
        nh_ref, nl_ref, proj_ref, conv_ref, s_ref = refs[12:17]
        m_refs = refs[17 : 17 + count]
        wh_ref, wl_ref, ext_ref, o_ref, mixed_ref = refs[17 + count :]
        step = pl.program_id(0)
        me = own_ref[0]

        @pl.when(step == 0)
        def _():
            for k in range(3):
                wh_ref[k], wl_ref[k] = parts_of(weight_ref[k])
            ext_ref[:, :8] = jnp.zeros((3, 8, width), F32)

        for u in range(pair):
            for k in range(count):
                normed = normalise(x_refs[k][u])[0] * gain_ref[...] + offset_ref[...]
                start = pl.multiple_of(u * block + (me ^ k) * quarter, quarter)
                high, low = parts_of(normed)
                nh_ref[0, pl.ds(start, quarter), :] = high
                nl_ref[0, pl.ds(start, quarter), :] = low
        normed = (nh_ref[0], nl_ref[0])
        short = []
        for k in range(3):
            proj = dot_parts(normed, (wh_ref[k], wl_ref[k]), NN) + bias_ref[k : k + 1, :]
            proj_ref[0, k] = proj
            ext_ref[k, 8:] = proj
            short.append(
                conv_w_ref[0, k : k + 1, :] * ext_ref[k, 6 : 6 + span]
                + conv_w_ref[1, k : k + 1, :] * ext_ref[k, 7 : 7 + span]
                + conv_w_ref[2, k : k + 1, :] * proj
                + conv_b_ref[k : k + 1, :]
            )
            ext_ref[k, :8] = ext_ref[k, span:]
        places = step * span + lax.broadcasted_iota(jnp.int32, (span, 1), 0)
        mask = (places < length_ref[0]).astype(F32)
        signal = short[2] * short[1] * mask
        for u in range(pair):
            part = signal[u * block : (u + 1) * block]
            s_ref[step * pair + u] = dot_parts((th_ref[...], tl_ref[...]), parts_of(part), NN)
        for u in range(pair):
            b = step * pair + u
            for r in range(0, block, tile):
                lo = slice(r, r + tile)
                hi = slice(block + r, block + r + tile)

                def product(i, total, b=b, lo=lo, hi=hi):
                    s_re, s_im = s_ref[i, lo], s_ref[i, hi]
                    k_re, k_im = k_ref[b - i, lo], k_ref[b - i, hi]
                    return total[0] + s_re * k_re - s_im * k_im, total[1] + s_re * k_im + s_im * k_re

                zero = jnp.zeros((tile, width), F32)
                o_ref[u, lo], o_ref[u, hi] = lax.fori_loop(0, b + 1, product, (zero, zero))
        inverse = (ih_ref[...], il_ref[...])
        conv = jnp.concatenate([dot_parts(inverse, parts_of(o_ref[u]), NN) for u in range(pair)], 0)
        conv = conv + skip_ref[...] * signal
        conv_ref[0] = conv
        mixed_ref[...] = conv * short[0]
        for u in range(pair):
            for k in range(count):
                start = pl.multiple_of(u * block + (me ^ k) * quarter, quarter)
                m_refs[k][u] = fold(mixed_ref[pl.ds(start, quarter), :])

    by_block = lambda *shape: pl.BlockSpec((1,) + shape, lambda b: (b,) + (0,) * len(shape))
    args = [own, length, *x_parts, gain, offset, weight, bias, conv_w, conv_b, skip, spectrum, *tables]
    by_pair = lambda n: pl.BlockSpec((pair, quarter, n), lambda b: (b, 0, 0))
    in_specs = [scalar_spec(), scalar_spec()] + [by_pair(model)] * count
    in_specs += [whole(a) for a in args[2 + count :]]
    folded = pl.BlockSpec((pair, quarter // 2, 2 * width), lambda b: (b, 0, 0))
    s_shape = struct((blocks, 2 * block, width))
    outs = run_kernel(
        body,
        "mixer_forward",
        (blocks // pair,),
        in_specs,
        [by_block(span, model)] * 2
        + [by_block(3, span, width), by_block(span, width), whole(s_shape)]
        + [folded] * count,
        [struct((blocks // pair, span, model), BF16)] * 2
        + [struct((blocks // pair, 3, span, width)), struct((blocks // pair, span, width)), s_shape]
        + [struct((blocks, quarter // 2, 2 * width))] * count,
        [
            pltpu.VMEM((3, model, width), BF16),
            pltpu.VMEM((3, model, width), BF16),
            pltpu.VMEM((3, span + 8, width), F32),
            pltpu.VMEM((pair, 2 * block, width), F32),
            pltpu.VMEM((span, width), F32),
        ],
        args,
        36,
    )
    return outs[:5], list(outs[5:])


def hidden_forward(m_parts, weights, x_own, cotangent, bias, gain, offset):
    blocks, half, width = m_parts[0].shape
    rows, model = x_own.shape
    width = width // 2
    count = len(m_parts)
    group = math.gcd(blocks, max(128 // half, 1))
    step = 2 * half * group

    def body(*refs):
        m_refs, w_refs = refs[:count], refs[count : 2 * count]
        x_ref, c_ref, bias_ref, gain_ref, offset_ref = refs[2 * count : 2 * count + 5]
        h_ref, nh_ref, nl_ref, th_ref, tl_ref, ch_ref, cl_ref = refs[2 * count + 5 : 2 * count + 12]
        wh_ref, wl_ref = refs[2 * count + 12 :]

        @pl.when(pl.program_id(0) == 0)
        def _():
            for k in range(count):
                wh_ref[k], wl_ref[k] = parts_of(w_refs[k][...])

        hidden = x_ref[...] + bias_ref[...]
        for k in range(count):
            mixed = jnp.concatenate([unfold(m_refs[k][u]) for u in range(group)], 0)
            hidden = hidden + dot_parts(parts_of(mixed), (wh_ref[k], wl_ref[k]), NN)
        h_ref[...] = hidden
        normed = normalise(hidden)[0] * gain_ref[...] + offset_ref[...]
        nh_ref[...], nl_ref[...] = parts_of(normed)
        th_ref[...], tl_ref[...] = parts_of(normed.T)
        ch_ref[...], cl_ref[...] = parts_of(c_ref[...])

    row_spec = lambda n: pl.BlockSpec((step, n), lambda r: (r, 0))
    turned = pl.BlockSpec((model, step), lambda r: (0, r))
    args = [*m_parts, *weights, x_own, cotangent, bias, gain, offset]
    return run_kernel(
        body,
        "hidden_forward",
        (rows // step,),
        [pl.BlockSpec((group, half, 2 * width), lambda r: (r, 0, 0))] * count
        + [whole(w) for w in weights]
        + [row_spec(model)] * 2
        + [whole(bias), whole(gain), whole(offset)],
        [row_spec(model)] * 3 + [turned] * 2 + [row_spec(model)] * 2,
        [struct((rows, model))]
        + [struct((rows, model), BF16)] * 2
        + [struct((model, rows), BF16)] * 2
        + [struct((rows, model), BF16)] * 2,
        [pltpu.VMEM((count, width, model), BF16)] * 2,
        args,
        9,
    )


def feed_forward(side, normed, turned, cotangent, up, up_bias, down, sums):
    rows, model = normed[0].shape
    units = up_bias.shape[1]
    step = min(256, units)
    first = sums is None
    pieces = len(up)

    def body(side_ref, *refs):
        nh_ref, nl_ref, th_ref, tl_ref, ch_ref, cl_ref, bias_ref = refs[:7]
        up_refs, down_refs = refs[7 : 7 + pieces], refs[7 + pieces : 7 + 2 * pieces]
        refs = refs[7 + 2 * pieces :]
        feed_in, grad_in = (None, None) if first else refs[:2]
        feed_ref, grad_ref, gup_ref, gdown_ref, gbias_ref = refs[0 if first else 2 :]

        @pl.when(pl.program_id(0) == 0)
        def _():
            if first:
                feed_ref[...] = jnp.zeros_like(feed_ref)
                grad_ref[...] = jnp.zeros_like(grad_ref)
            else:
                feed_ref[...] = feed_in[...]
                grad_ref[...] = grad_in[...]

        def in_order(halves, axis):
            if pieces == 1:
                return halves[0][...]
            mine, other = halves[0][...], halves[1][...]
            low = side_ref[0] == 0
            return jnp.concatenate([jnp.where(low, mine, other), jnp.where(low, other, mine)], axis)

        own_normed = (nh_ref[...], nl_ref[...])
        own_cotangent = (ch_ref[...], cl_ref[...])
        up_parts = parts_of(in_order(up_refs, 0))
        down_parts = parts_of(in_order(down_refs, 1))
        before = dot_parts(own_normed, up_parts, NN) + bias_ref[...]
        grad_active = dot_parts(own_cotangent, down_parts, NT)
        below = 0.5 + 0.5 * lax.erf(before * math.sqrt(0.5))
        slope = below + before * (jnp.exp(-0.5 * before * before) * (1.0 / math.sqrt(2.0 * math.pi)))
        active = before * below
        grad_before = grad_active * slope
        gbias_ref[...] = column_sum(grad_before)
        active_parts = parts_of(active)
        grad_parts = parts_of(grad_before)
        feed_ref[...] += dot_parts(active_parts, down_parts, NN)
        grad_ref[...] += dot_parts(grad_parts, up_parts, NT)
        gup_ref[...] = dot_parts((th_ref[...], tl_ref[...]), grad_parts, NN)
        gdown_ref[...] = dot_parts(active_parts, own_cotangent, TN)

    total = struct((rows, model))
    args = [side, *normed, *turned, *cotangent, up_bias, *up, *down] + ([] if first else list(sums))
    columns = lambda n: pl.BlockSpec((n, step), lambda t: (0, t))
    some_rows = lambda n: pl.BlockSpec((step, n), lambda t: (t, 0))
    outs = run_kernel(
        body,
        "feed_forward",
        (units // step,),
        [scalar_spec()]
        + [whole(a) for a in args[1:7]]
        + [columns(1)]
        + [columns(model // pieces)] * pieces
        + [some_rows(model // pieces)] * pieces
        + [whole(a) for a in args[8 + 2 * pieces :]],
        [whole(total), whole(total), columns(model), some_rows(model), columns(1)],
        [total, total, struct((model, units)), struct((units, model)), struct(up_bias.shape)],
        [],
        args,
        18,
    )
    return outs[:2], outs[2:]


def feed_forward_pair(normed, turned, cotangent, ups, biases, downs, sums):
    rows, model = normed[0].shape
    units = biases[0].shape[1]
    step = min(256, units)
    tiles = units // step

    def body(*refs):
        nh_ref, nl_ref, th_ref, tl_ref, ch_ref, cl_ref, bias_ref = refs[:7]
        up_refs, down_refs, (feed_in, grad_in) = refs[7:9], refs[9:11], refs[11:13]
        feed_ref, grad_ref, gbias_ref = refs[13:16]
        gup_refs, gdown_refs = refs[16:18], refs[18:20]
        uh_ref, ul_ref, dh_ref, dl_ref = refs[20:]
        t = pl.program_id(0)

        @pl.when(t == 0)
        def _():
            feed_ref[...] = feed_in[...]
            grad_ref[...] = grad_in[...]

        for j in range(2):

            @pl.when(t // tiles == j)
            def _(j=j):
                uh_ref[...], ul_ref[...] = parts_of(up_refs[j][...])
                dh_ref[...], dl_ref[...] = parts_of(down_refs[j][...])

        own_normed = (nh_ref[...], nl_ref[...])
        own_cotangent = (ch_ref[...], cl_ref[...])
        up_parts, down_parts = (uh_ref[...], ul_ref[...]), (dh_ref[...], dl_ref[...])
        before = dot_parts(own_normed, up_parts, NN) + bias_ref[...]
        grad_active = dot_parts(own_cotangent, down_parts, NT)
        below = 0.5 + 0.5 * lax.erf(before * math.sqrt(0.5))
        slope = below + before * (jnp.exp(-0.5 * before * before) * (1.0 / math.sqrt(2.0 * math.pi)))
        active = before * below
        grad_before = grad_active * slope
        gbias_ref[...] = column_sum(grad_before)
        active_parts = parts_of(active)
        grad_parts = parts_of(grad_before)
        feed_ref[...] += dot_parts(active_parts, down_parts, NN)
        grad_ref[...] += dot_parts(grad_parts, up_parts, NT)
        grad_up = dot_parts((th_ref[...], tl_ref[...]), grad_parts, NN)
        grad_down = dot_parts(active_parts, own_cotangent, TN)
        for j in range(2):

            @pl.when(t // tiles == j)
            def _(j=j):
                gup_refs[j][...] = grad_up
                gdown_refs[j][...] = grad_down

    total = struct((rows, model))
    bias = jnp.concatenate(biases, 1)
    args = [*normed, *turned, *cotangent, bias, *ups, *downs, *sums]
    place = lambda t, j: jnp.minimum(t, tiles - 1) if j == 0 else jnp.maximum(t - tiles, 0)
    columns = [pl.BlockSpec((model, step), lambda t, j=j: (0, place(t, j))) for j in range(2)]
    some_rows = [pl.BlockSpec((step, model), lambda t, j=j: (place(t, j), 0)) for j in range(2)]
    one_row = pl.BlockSpec((1, step), lambda t: (0, t))
    outs = run_kernel(
        body,
        "feed_forward_pair",
        (2 * tiles,),
        [whole(a) for a in args[:6]] + [one_row] + columns + some_rows + [whole(total)] * 2,
        [whole(total)] * 2 + [one_row] + columns + some_rows,
        [total, total, struct(bias.shape)] + [struct((model, units))] * 2 + [struct((units, model))] * 2,
        [pltpu.VMEM((model, step), BF16)] * 2 + [pltpu.VMEM((step, model), BF16)] * 2,
        args,
        31,
    )
    return outs[:2], outs[2], outs[3:5], outs[5:7]


def hidden_backward(hidden, feed, grad_normed, cotangent, m_parts, weights, gain, bias):
    rows, model = hidden.shape
    blocks, half, width = m_parts[0].shape
    width = width // 2
    count = len(m_parts)
    group = math.gcd(blocks, max(128 // half, 1))
    step = 2 * half * group

    def body(*refs):
        h_ref, f_ref, g_ref, c_ref = refs[:4]
        m_refs, w_refs = refs[4 : 4 + count], refs[4 + count : 4 + 2 * count]
        gain_ref, bias_ref, out_ref, gh_ref, sum_ref = refs[4 + 2 * count : 9 + 2 * count]
        gm_refs, refs = refs[9 + 2 * count : 9 + 3 * count], refs[9 + 3 * count :]
        gw_refs, (wh_ref, wl_ref) = refs[:2], refs[2:]

        @pl.when(pl.program_id(0) == 0)
        def _():
            sum_ref[...] = jnp.zeros_like(sum_ref)
            for k in range(count):
                wh_ref[k], wl_ref[k] = parts_of(w_refs[k][...])
            for k in range(2):
                gw_refs[k][...] = jnp.zeros_like(gw_refs[k])

        hidden_rows, grad, above = h_ref[...], g_ref[...], c_ref[...]
        out_ref[...] = hidden_rows + f_ref[...] + bias_ref[...]
        unit, scale = normalise(hidden_rows)
        grad_hidden = above + norm_back(unit, scale, gain_ref[...], grad)
        gh_ref[...] = grad_hidden
        sum_ref[0:1] += column_sum(grad * unit)
        sum_ref[1:2] += column_sum(grad)
        sum_ref[2:3] += column_sum(grad_hidden)
        sum_ref[3:4] += column_sum(above)
        parts = parts_of(grad_hidden)
        for k in range(count):
            grad_mixed = dot_parts(parts, (wh_ref[k], wl_ref[k]), NT)
            for u in range(group):
                gm_refs[k][u] = fold(grad_mixed[u * 2 * half : (u + 1) * 2 * half])
            mixed = jnp.concatenate([unfold(m_refs[k][u]) for u in range(group)], 0)
            gw_refs[k // 2][k % 2] += dot_parts(parts_of(mixed), parts, TN)

    folded = pl.BlockSpec((group, half, 2 * width), lambda r: (r, 0, 0))
    row_spec = lambda n: pl.BlockSpec((step, n), lambda r: (r, 0))
    args = [hidden, feed, grad_normed, cotangent, *m_parts, *weights, gain, bias]
    sums, pair = struct((8, model)), struct((2, width, model))
    outs = run_kernel(
        body,
        "hidden_backward",
        (rows // step,),
        [row_spec(model)] * 4 + [folded] * count + [whole(w) for w in weights] + [whole(gain), whole(bias)],
        [row_spec(model)] * 2
        + [whole(sums)]
        + [folded] * count
        + [whole(pair)] * 2,
        [struct((rows, model))] * 2 + [sums] + [struct((blocks, half, 2 * width))] * count + [pair] * 2,
        [pltpu.VMEM((count, width, model), BF16)] * 2,
        args,
        15,
    )
    return outs[:3], list(outs[3 : 3 + count]), outs[3 + count :]


def mixer_backward(own, length, gm_parts, proj, conv, s_spec, k_spec, conv_w, conv_b, skip, weight, tables):
    blocks, quarter, width = gm_parts[0].shape
    quarter, width = 2 * quarter, width // 2
    count = len(gm_parts)
    block = quarter * count
    model = weight.shape[1]
    tile = min(32, block)
    pair = 2 - blocks % 2
    span = pair * block

    def body(*refs):
        own_ref, length_ref = refs[:2]
        gm_refs = refs[2 : 2 + count]
        refs = refs[2 + count :]
        proj_ref, rim_ref, conv_ref, k_ref, conv_w_ref, conv_b_ref, skip_ref, weight_ref = refs[:8]
        th_ref, tl_ref, ih_ref, il_ref = refs[8:12]
        g_ref, gp_ref, sum_ref = refs[12:15]
        gn_refs = refs[15 : 15 + count]
        wh_ref, wl_ref, ext_ref, gs_ref, o_ref, rows_ref, gn_ref = refs[15 + count :]
        step = pl.program_id(0)
        slot = blocks // pair - 1 - step
        me = own_ref[0]

        @pl.when(step == 0)
        def _():
            for k in range(3):
                wh_ref[k], wl_ref[k] = parts_of(weight_ref[k])
            gs_ref[:, span:] = jnp.zeros((3, 8, width), F32)
            sum_ref[...] = jnp.zeros_like(sum_ref)

        for u in range(pair):
            for k in range(count):
                start = pl.multiple_of(u * block + (me ^ k) * quarter, quarter)
                rows_ref[pl.ds(start, quarter), :] = unfold(gm_refs[k][u])
        inside = (slot > 0).astype(F32)
        short = []
        for k in range(3):
            ext_ref[k, :8] = rim_ref[0, k] * inside
            ext_ref[k, 8:] = proj_ref[0, k]
            short.append(
                conv_w_ref[0, k : k + 1, :] * ext_ref[k, 6 : 6 + span]
                + conv_w_ref[1, k : k + 1, :] * ext_ref[k, 7 : 7 + span]
                + conv_w_ref[2, k : k + 1, :] * proj_ref[0, k]
                + conv_b_ref[k : k + 1, :]
            )
        places = slot * span + lax.broadcasted_iota(jnp.int32, (span, 1), 0)
        mask = (places < length_ref[0]).astype(F32)
        gate_in, values = short[1] * mask, short[2] * mask
        grad_mixed = rows_ref[...]
        grad_conv = grad_mixed * short[0]
        gs_ref[0, :span] = grad_mixed * conv_ref[0]
        for u in range(pair):
            part = grad_conv[u * block : (u + 1) * block]
            g_ref[slot * pair + u] = dot_parts((th_ref[...], tl_ref[...]), parts_of(part), NN)
        for u in range(pair):
            b = slot * pair + u
            for r in range(0, block, tile):
                lo = slice(r, r + tile)
                hi = slice(block + r, block + r + tile)

                def product(j, total, b=b, lo=lo, hi=hi):
                    g_re, g_im = g_ref[j, lo], g_ref[j, hi]
                    k_re, k_im = k_ref[j - b, lo], k_ref[j - b, hi]
                    return total[0] + g_re * k_re + g_im * k_im, total[1] + g_im * k_re - g_re * k_im

                zero = jnp.zeros((tile, width), F32)
                o_ref[u, lo], o_ref[u, hi] = lax.fori_loop(b, blocks, product, (zero, zero))
        inverse = (ih_ref[...], il_ref[...])
        grad_signal = jnp.concatenate([dot_parts(inverse, parts_of(o_ref[u]), NN) for u in range(pair)], 0)
        grad_signal = grad_signal + skip_ref[...] * grad_conv
        gs_ref[1, :span] = grad_signal * values
        gs_ref[2, :span] = grad_signal * gate_in
        sum_ref[0:1] += column_sum(grad_conv * short[2] * gate_in)
        normed_grad = jnp.zeros((span, model), F32)
        for k in range(3):
            grad_short = gs_ref[k, :span]
            sum_ref[1 + k : 2 + k] += column_sum(grad_short)
            for t in range(3):
                row = 4 + 3 * t + k
                sum_ref[row : row + 1] += column_sum(grad_short * ext_ref[k, 6 + t : 6 + t + span])
            grad_proj = (
                conv_w_ref[2, k : k + 1, :] * grad_short
                + conv_w_ref[1, k : k + 1, :] * gs_ref[k, 1 : 1 + span]
                + conv_w_ref[0, k : k + 1, :] * gs_ref[k, 2 : 2 + span]
            )
            sum_ref[13 + k : 14 + k] += column_sum(grad_proj)
            gp_ref[0, k] = grad_proj
            normed_grad = normed_grad + dot_parts(parts_of(grad_proj), (wh_ref[k], wl_ref[k]), NT)
            gs_ref[k, span:] = gs_ref[k, :8]
        gn_ref[...] = normed_grad
        for u in range(pair):
            for k in range(count):
                start = pl.multiple_of(u * block + (me ^ k) * quarter, quarter)
                gn_refs[k][u] = gn_ref[pl.ds(start, quarter), :]

    last = blocks // pair - 1
    by_block = lambda *shape: pl.BlockSpec((1,) + shape, lambda s: (last - s,) + (0,) * len(shape))
    rim = pl.BlockSpec((1, 3, 8, width), lambda s: (jnp.maximum(last - s - 1, 0), 0, span // 8 - 1, 0))
    by_pair = lambda n: pl.BlockSpec((pair, quarter, n), lambda s: (last - s, 0, 0))
    fixed = [k_spec, conv_w, conv_b, skip, weight, *tables]
    spectra = struct((blocks, 2 * block, width))
    sums = struct((16, width))
    outs = run_kernel(
        body,
        "mixer_backward",
        (blocks // pair,),
        [scalar_spec(), scalar_spec()]
        + [pl.BlockSpec((pair, quarter // 2, 2 * width), lambda s: (last - s, 0, 0))] * count
        + [by_block(3, span, width), rim, by_block(span, width)]
        + [whole(a) for a in fixed],
        [whole(spectra), by_block(3, span, width), whole(sums)] + [by_pair(model)] * count,
        [spectra, struct((blocks // pair, 3, span, width)), sums] + [struct((blocks, quarter, model))] * count,
        [
            pltpu.VMEM((3, model, width), BF16),
            pltpu.VMEM((3, model, width), BF16),
            pltpu.VMEM((3, span + 8, width), F32),
            pltpu.VMEM((3, span + 8, width), F32),
            pltpu.VMEM((pair, 2 * block, width), F32),
            pltpu.VMEM((span, width), F32),
            pltpu.VMEM((span, model), F32),
        ],
        [own, length, *gm_parts, proj, proj, conv, *fixed],
        35,
    )
    return outs[:3], list(outs[3:])


def filter_backward(s_spec, g_spec, tables):
    blocks, double, width = s_spec.shape
    block = double // 2
    tile = min(32, block)
    inverse = tables[2:]

    def body(s_ref, g_ref, ih_ref, il_ref, out_ref, after_ref, o_ref):
        m = blocks - 1 - pl.program_id(0)

        @pl.when(m == blocks - 1)
        def _():
            after_ref[...] = jnp.zeros_like(after_ref)

        sign = parity_of(tile)
        for r in range(0, block, tile):
            lo = slice(r, r + tile)
            hi = slice(block + r, block + r + tile)

            def product(j, total, lo=lo, hi=hi):
                g_re, g_im = g_ref[j, lo], g_ref[j, hi]
                s_re, s_im = s_ref[j - m, lo], s_ref[j - m, hi]
                return total[0] + g_re * s_re + g_im * s_im, total[1] + g_im * s_re - g_re * s_im

            zero = jnp.zeros((tile, width), F32)
            re, im = lax.fori_loop(m, blocks, product, (zero, zero))
            o_ref[lo] = re + sign * after_ref[hi]
            o_ref[hi] = im - sign * after_ref[lo]
            after_ref[lo], after_ref[hi] = re, im
        out_ref[0] = dot_parts((ih_ref[...], il_ref[...]), parts_of(o_ref[...]), NN)

    return run_kernel(
        body,
        "filter_backward",
        (blocks,),
        [whole(s_spec), whole(g_spec), whole(inverse[0]), whole(inverse[1])],
        [pl.BlockSpec((1, block, width), lambda s: (blocks - 1 - s, 0, 0))],
        [struct((blocks, block, width))],
        [pltpu.VMEM((double, width), F32)] * 2,
        [s_spec, g_spec, *inverse],
        13,
    )[0]


def input_weight_grad(normed_high, normed_low, grad_proj):
    blocks, block, model = normed_high.shape
    width = grad_proj.shape[3]

    def body(nh_ref, nl_ref, gp_ref, out_ref):
        @pl.when(pl.program_id(0) == 0)
        def _():
            out_ref[...] = jnp.zeros_like(out_ref)

        normed = (nh_ref[0], nl_ref[0])
        for k in range(3):
            out_ref[k] += dot_parts(parts_of(gp_ref[0, k]), normed, TN)

    by_block = lambda *shape: pl.BlockSpec((1,) + shape, lambda b: (b,) + (0,) * len(shape))
    out = struct((3, width, model))
    return run_kernel(
        body,
        "input_weight_grad",
        (blocks,),
        [by_block(block, model)] * 2 + [by_block(3, block, width)],
        [whole(out)],
        [out],
        [],
        [normed_high, normed_low, grad_proj],
        12,
    )[0]


def input_backward(grad_pieces, x_own, grad_hidden, gain):
    rows, model = x_own.shape
    count = len(grad_pieces)
    step = min(256, rows)

    def body(*refs):
        piece_refs = refs[:count]
        x_ref, gh_ref, gain_ref, out_ref, sum_ref = refs[count:]

        @pl.when(pl.program_id(0) == 0)
        def _():
            sum_ref[...] = jnp.zeros_like(sum_ref)

        grad = sum(r[...] for r in piece_refs)
        unit, scale = normalise(x_ref[...])
        out_ref[...] = gh_ref[...] + norm_back(unit, scale, gain_ref[...], grad)
        sum_ref[0:1] += column_sum(grad * unit)
        sum_ref[1:2] += column_sum(grad)

    row_spec = pl.BlockSpec((step, model), lambda r: (r, 0))
    sums = struct((8, model))
    return run_kernel(
        body,
        "input_backward",
        (rows // step,),
        [row_spec] * (count + 2) + [whole(gain)],
        [row_spec, whole(sums)],
        [struct((rows, model)), sums],
        [],
        [*grad_pieces, x_own, grad_hidden, gain],
        5,
    )


def put_together(own, pieces):
    groups, quarter, model = pieces[0].shape
    count = len(pieces)
    pair = 2 - groups % 2

    def body(own_ref, *refs):
        for u in range(pair):
            for k in range(count):
                start = pl.multiple_of((own_ref[0] ^ k) * quarter, quarter)
                refs[count][u, pl.ds(start, quarter), :] = refs[k][u]

    by_group = lambda n: pl.BlockSpec((pair, n, model), lambda s: (s, 0, 0))
    return run_kernel(
        body,
        "put_together",
        (groups // pair,),
        [scalar_spec()] + [by_group(quarter)] * count,
        [by_group(quarter * count)],
        [struct((groups, quarter * count, model))],
        [],
        [own, *pieces],
        8,
    )[0]


def swap(values, axis, bit):
    size = lax.axis_size(axis)
    return lax.ppermute(values, axis, [(i, i ^ bit) for i in range(size)])


def total_over(values, axis):
    bit = 1
    while bit < lax.axis_size(axis):
        values = values + swap(values, axis, bit)
        bit *= 2
    return values


def meet(*values):
    return lax.optimization_barrier(values)


def split_rows(values, axis, bit):
    mine = (lax.axis_index(axis) // bit) % 2
    half = values.shape[0] // 2
    leaving = lax.dynamic_slice_in_dim(values, (1 - mine) * half, half, 0)
    staying = lax.dynamic_slice_in_dim(values, mine * half, half, 0)
    return leaving, staying


def join_rows(values, other, axis, bit):
    first = (lax.axis_index(axis) // bit) % 2 == 0
    return jnp.concatenate([jnp.where(first, values, other), jnp.where(first, other, values)], 0)


def transpose_blocks(values):
    return lax.all_to_all(values, "seq", split_axis=0, concat_axis=0, tiled=True)


def spread(values):
    far = swap(values, "chan", 2)
    return [values, swap(values, "chan", 1), far, swap(far, "chan", 1)]


def collect(pieces):
    far = pieces[2] + swap(pieces[3], "chan", 1)
    return [pieces[0], swap(pieces[1], "chan", 1), swap(far, "chan", 2)]


def pack(arrays):
    flat = jnp.concatenate([a.reshape(-1) for a in arrays])
    return jnp.pad(flat, (0, -flat.shape[0] % 1024))


def unpack(flat, arrays):
    out = []
    start = 0
    for a in arrays:
        size = math.prod(a.shape)
        out.append(flat[start : start + size].reshape(a.shape))
        start += size
    return out


def sequence_device(
    block_input,
    lengths,
    ln1_gain,
    ln1_bias,
    input_weight,
    input_bias,
    conv_w,
    conv_b,
    filt_w1,
    filt_b1,
    filt_w2,
    filt_b2,
    filt_w3,
    decay,
    skip,
    output_weight,
    output_bias,
    ln2_gain,
    ln2_bias,
    up_weight,
    up_bias,
    down_weight,
    down_bias,
    cotangent,
):
    blocks, block, model = block_input.shape
    count = lax.axis_size("chan")
    quarter = block // count
    rows = blocks * quarter
    width = decay.shape[0]
    seq_length = blocks * block
    seq_index = lax.axis_index("seq")
    chan_index = lax.axis_index("chan")
    own = chan_index.astype(jnp.int32).reshape(1)
    length = lax.dynamic_slice(lengths, (seq_index,), (1,))
    tables = wave_tables(block)
    row = lambda v: v.reshape(1, -1)

    def own_rows(values):
        part = lax.dynamic_slice_in_dim(values, chan_index * quarter, quarter, 1)
        return transpose_blocks(part)

    place_values = jnp.arange(seq_length, dtype=jnp.int32).astype(F32)
    features = position_features(place_values, seq_length, filt_w1.shape[0])
    kernel, filter_pull = jax.vjp(
        partial(implicit_filter, features, place_values), filt_w1, filt_b1, filt_w2, filt_b2, filt_w3, decay
    )
    k_spec = filter_spectrum(kernel.reshape(blocks, block, width), tables)
    weight = jnp.transpose(input_weight, (1, 0, 2))

    x_own = own_rows(block_input)
    side = (seq_index % 2).astype(jnp.int32)

    def half_of(values, axis):
        half = values.shape[axis] // 2
        return lax.dynamic_slice_in_dim(values, side * half, half, axis)

    up_far = swap(half_of(up_weight, 0), "chan", 2)
    up_bias_parts = [swap(up_bias, "chan", k) if k else up_bias for k in range(count)]
    x_own, k_spec, weight, up_far, up_bias_parts, cotangent_home = meet(
        x_own, k_spec, weight, up_far, up_bias_parts, cotangent
    )
    x_far = swap(x_own, "chan", 2)
    x_parts = [x_own, swap(x_own, "chan", 1), x_far, swap(x_far, "chan", 1)]
    cot_own = own_rows(cotangent_home)
    x_rows = x_own.reshape(rows, model)
    x_parts[2], out_home, down_home, up_far = meet(x_parts[2], output_weight, down_weight, up_far)
    out_far = swap(out_home, "chan", 2)
    down_far = swap(half_of(down_home, 1), "chan", 2)
    up_other = swap(up_far, "seq", 1)
    x_parts[0], cot_own = meet(x_parts[0], cot_own)
    cot_own = cot_own.reshape(rows, model)

    (normed_high, normed_low, proj, conv, s_spec), mixed = mixer_forward(
        own, length, x_parts, row(ln1_gain), row(ln1_bias), weight, input_bias, conv_w, conv_b, row(skip), k_spec, tables
    )
    *mixed, down_far, out_far, up_other = meet(*mixed, down_far, out_far, up_other)
    mixed = [m if k == 0 else swap(m, "chan", k) for k, m in enumerate(mixed)]
    down_other = swap(down_far, "seq", 1)
    out_3 = swap(out_far, "chan", 1)
    *mixed, out_3 = meet(*mixed, out_3)
    out_parts = [output_weight, swap(output_weight, "chan", 1), out_far, out_3]
    up_parts = [[up_weight], [swap(up_weight, "chan", 1)], [up_far, up_other]]
    up_parts.append([swap(u, "chan", 1) for u in up_parts[2]])
    down_side = swap(down_far, "chan", 1)

    hidden, *rest = hidden_forward(
        mixed, out_parts, x_rows, cot_own, row(output_bias), row(ln2_gain), row(ln2_bias)
    )
    rest, down_other, down_side = meet(rest, down_other, down_side)
    normed2, turned, cot_parts = rest[0:2], rest[2:4], rest[4:6]
    down_parts = [[down_weight], [swap(down_weight, "chan", 1)], [down_far, down_other]]
    down_parts.append([down_side, swap(down_other, "chan", 1)])

    def units(k, sums):
        return feed_forward(
            side.reshape(1), normed2, turned, cot_parts, up_parts[k], row(up_bias_parts[k]), down_parts[k], sums
        )

    bias_grads = [None] * count
    sums, (up_3, down_3, bias_grads[3]) = units(3, None)
    up_3, down_3 = swap(up_3, "chan", 1), swap(down_3, "chan", 1)
    sums, (up_2, down_2, bias_grads[2]) = units(2, sums)
    *sums, up_2, up_3, down_2, down_3 = meet(*sums, up_2, up_3, down_2, down_3)

    third = model // 3
    far_up = lambda i: up_2[i * third : (i + 1) * third] + up_3[i * third : (i + 1) * third]
    leaving_2, staying_2 = split_rows(down_2, "seq", 1)
    leaving_3, staying_3 = split_rows(down_3, "seq", 1)
    far_ups = [swap(up_2[: 2 * third] + up_3[: 2 * third], "chan", 2)]
    came = swap(leaving_2 + leaving_3, "seq", 1)
    sums, near_bias, (up_1, up_0), (down_1, down_0) = feed_forward_pair(
        normed2, turned, cot_parts, [up_parts[1][0], up_parts[0][0]], [row(up_bias_parts[1]), row(up_bias_parts[0])],
        [down_parts[1][0], down_parts[0][0]], sums,
    )
    bias_grads[1], bias_grads[0] = jnp.split(near_bias, 2, 1)
    *sums, far_ups[0], came, up_1, down_1 = meet(*sums, far_ups[0], came, up_1, down_1)
    down_1, up_1 = swap(down_1, "chan", 1), swap(up_1, "chan", 1)
    far_ups.append(swap(up_2[2 * third :] + up_3[2 * third :], "chan", 2))
    leaving, far_staying = split_rows(staying_2 + staying_3 + came, "seq", 2)
    far_came = swap(leaving, "seq", 2)
    leaving_0, staying_0 = split_rows(down_0, "seq", 1)
    leaving_1, staying_1 = split_rows(down_1, "seq", 1)
    near_leaving = leaving_0 + leaving_1
    near_leaving, *sums = meet(near_leaving, *sums)
    near_came = swap(near_leaving, "seq", 1)
    (out_rows, grad_hidden, sums2), grad_mixed, (out_near, out_far) = hidden_backward(
        hidden, sums[0], sums[1], cot_own, mixed, out_parts, row(ln2_gain), row(down_bias)
    )
    grad_hidden, far_ups[1], far_came, grad_mixed, out_rows, up_1 = meet(
        grad_hidden, far_ups[1], far_came, grad_mixed, out_rows, up_1
    )

    grad_mixed = [g if k == 0 else swap(g, "chan", k) for k, g in enumerate(grad_mixed)]
    leaving, far_staying = split_rows(far_staying + far_came, "seq", 4)
    far_came = swap(leaving, "seq", 4)
    out_blocks = transpose_blocks(out_rows.reshape(blocks, quarter, model))
    grad_up = up_0 + up_1 + jnp.concatenate(far_ups, 0)
    up_leaving, up_staying = split_rows(grad_up, "seq", 1)
    grad_mixed, up_leaving, up_staying, out_far, near_came = meet(
        grad_mixed, up_leaving, up_staying, out_far, near_came
    )

    up_came = swap(up_leaving, "seq", 1)
    leaving, near_staying = split_rows(staying_0 + staying_1 + near_came, "seq", 2)
    near_came = swap(leaving, "seq", 2)
    out_far = swap(out_far, "chan", 2)
    (g_spec, grad_proj, mixer_sums), grad_normed = mixer_backward(
        own, length, grad_mixed, proj, conv, s_spec, k_spec, conv_w, conv_b, row(skip), weight, tables
    )
    grad_normed, grad_proj, out_far, near_came, up_came, out_blocks, far_came = meet(
        grad_normed, grad_proj, out_far, near_came, up_came, out_blocks, far_came
    )

    grad_normed[3], grad_normed[1] = swap(grad_normed[3], "chan", 1), swap(grad_normed[1], "chan", 1)
    far_down = swap(far_staying + far_came, "chan", 2)
    leaving, near_staying = split_rows(near_staying + near_came, "seq", 4)
    up_leaving, up_staying = split_rows(up_staying + up_came, "seq", 2)
    far_normed, grad_proj, leaving, up_leaving = meet(
        grad_normed[2] + grad_normed[3], grad_proj, leaving, up_leaving
    )
    far_normed = swap(far_normed, "chan", 2)
    near_came, up_came = swap(leaving, "seq", 4), swap(up_leaving, "seq", 2)
    grad_in = input_weight_grad(normed_high, normed_low, grad_proj)
    grad_out = out_near[0] + out_far[0] + swap(out_near[1] + out_far[1], "chan", 1)
    g_spec, grad_in, grad_out, near_came, far_down, up_came = meet(
        g_spec, grad_in, grad_out, near_came, far_down, up_came
    )

    grad_down = near_staying + near_came + far_down
    down_came = swap(grad_down, "seq", 4)
    up_leaving, up_staying = split_rows(up_staying + up_came, "seq", 4)
    up_came = swap(up_leaving, "seq", 4)
    mixer_leaving, mixer_staying = split_rows(
        jnp.concatenate([grad_in.reshape(-1, model), grad_out], 0), "seq", 1
    )
    mixer_came = swap(mixer_leaving, "seq", 1)
    grad_kernel = filter_backward(s_spec, g_spec, tables).reshape(seq_length, width)
    grad_kernel, down_came = meet(grad_kernel, down_came)
    grad_down = join_rows(grad_down, down_came, "seq", 4)
    far_normed, up_came, grad_down = meet(far_normed, up_came, grad_down)
    down_came = swap(grad_down, "seq", 2)

    pieces = [p.reshape(rows, model) for p in (grad_normed[0], grad_normed[1], far_normed)]
    grad_x_rows, sums1 = input_backward(pieces, x_rows, grad_hidden, row(ln1_gain))
    grad_x_rows, grad_kernel, out_blocks, mixer_came, up_came, sums1 = meet(
        grad_x_rows, grad_kernel, out_blocks, mixer_came, up_came, sums1
    )

    grad_x_blocks = transpose_blocks(grad_x_rows.reshape(blocks, quarter, model))
    leaving, staying = split_rows(mixer_staying + mixer_came, "seq", 2)
    came = swap(leaving, "seq", 2)
    grad_up = up_staying + up_came
    grad_down = join_rows(grad_down, down_came, "seq", 2)
    up_came, down_came = swap(grad_up, "seq", 4), swap(grad_down, "seq", 1)
    out_far = swap(out_blocks, "chan", 2)
    grad_fw1, grad_fb1, grad_fw2, grad_fb2, grad_fw3, grad_decay = filter_pull(grad_kernel)
    up_bias_grads = jnp.take(
        jnp.concatenate(bias_grads, 0), jnp.arange(count, dtype=jnp.int32) ^ chan_index, axis=0
    )
    shared = [sums1[0], sums1[1], *[sums2[i] for i in range(4)], up_bias_grads, grad_fw1, grad_fb1, grad_fw2, grad_fb2]
    split = [mixer_sums, grad_fw3, grad_decay]
    shared_flat, split_flat = pack(shared), pack(split)
    shared_flat = shared_flat + swap(shared_flat, "chan", 1)
    side_flat = swap(shared_flat, "chan", 2)
    grad_x_blocks, came, up_came, down_came, out_far, out_blocks = meet(
        grad_x_blocks, came, up_came, down_came, out_far, out_blocks
    )

    grad_x_far = swap(grad_x_blocks, "chan", 2)
    grad_up, grad_down = join_rows(grad_up, up_came, "seq", 4), join_rows(grad_down, down_came, "seq", 1)
    up_came, up_low = swap(grad_up, "seq", 2), swap(grad_up, "seq", 1)
    leaving, staying = split_rows(staying + came, "seq", 4)
    came = swap(leaving, "seq", 4)
    came, up_came, up_low, grad_x_blocks, out_far, out_blocks, side_flat = meet(
        came, up_came, up_low, grad_x_blocks, out_far, out_blocks, side_flat
    )

    mixer_grads = staying + came
    came = swap(mixer_grads, "seq", 4)
    up_high = swap(up_came, "seq", 1)
    flat = jnp.concatenate([shared_flat + side_flat, split_flat])
    side_flat = swap(flat, "seq", 2)
    came, grad_x_far, side_flat, grad_x_blocks, out_far, out_blocks, grad_down, up_high = meet(
        came, grad_x_far, side_flat, grad_x_blocks, out_far, out_blocks, grad_down, up_high
    )

    mixer_grads = join_rows(mixer_grads, came, "seq", 4)
    came, low = swap(mixer_grads, "seq", 2), swap(mixer_grads, "seq", 1)
    grad_x_near, grad_x_side = swap(grad_x_blocks, "chan", 1), swap(grad_x_far, "chan", 1)
    flat = flat + side_flat
    side_flat = swap(flat, "seq", 4)
    came, low, side_flat, grad_x_near, grad_x_side, out_far, out_blocks = meet(
        came, low, side_flat, grad_x_near, grad_x_side, out_far, out_blocks
    )
    flat = flat + side_flat
    side_flat = swap(flat, "seq", 1)
    mixer_grads, came = join_rows(mixer_grads, came, "seq", 2), swap(came, "seq", 1)
    out_near, out_side = swap(out_blocks, "chan", 1), swap(out_far, "chan", 1)
    grad_x = put_together(own, [grad_x_blocks, grad_x_near, grad_x_far, grad_x_side])
    side_flat, out_near, out_side, grad_x = meet(side_flat, out_near, out_side, grad_x)
    flat = flat + side_flat
    grad_up = join_rows(join_rows(grad_up, up_came, "seq", 2), join_rows(up_low, up_high, "seq", 2), "seq", 1)
    output = put_together(own, [out_blocks, out_near, out_far, out_side])
    cut = shared_flat.shape[0]
    grad_ln1_gain, grad_ln1_bias, grad_ln2_gain, grad_ln2_bias, grad_b_out, grad_b_fc2, up_bias_grads, *filt = unpack(
        flat[:cut], shared
    )
    mixer_sums, grad_fw3, grad_decay = unpack(flat[cut:], split)
    grad_b_fc1 = lax.dynamic_slice_in_dim(up_bias_grads, chan_index, 1, 0)[0]
    grad_skip = mixer_sums[0]
    grad_conv_b = mixer_sums[1:4]
    grad_conv_w = mixer_sums[4:13].reshape(3, 3, width)
    grad_b_in = mixer_sums[13:16]
    small = (
        [grad_ln1_gain, grad_ln1_bias, grad_ln2_gain, grad_ln2_bias, grad_b_out, grad_b_fc2, grad_b_fc1]
        + [*filt, grad_fw3, grad_decay, grad_skip, grad_conv_b, grad_conv_w, grad_b_in]
    )
    output, grad_up, came, small = meet(output, grad_up, came, small)
    grad_ln1_gain, grad_ln1_bias, grad_ln2_gain, grad_ln2_bias, grad_b_out, grad_b_fc2, grad_b_fc1 = small[:7]
    *filt, grad_fw3, grad_decay, grad_skip, grad_conv_b, grad_conv_w, grad_b_in = small[7:]
    mixer_grads = join_rows(mixer_grads, join_rows(low, came, "seq", 2), "seq", 1)
    grad_in = jnp.transpose(mixer_grads[: 3 * width].reshape(3, width, model), (2, 0, 1))
    grad_out = mixer_grads[3 * width :]
    return (
        output,
        grad_x,
        grad_ln1_gain,
        grad_ln1_bias,
        grad_in,
        grad_b_in,
        grad_conv_w,
        grad_conv_b,
        *filt,
        grad_fw3,
        grad_decay,
        grad_skip,
        grad_out,
        grad_b_out,
        grad_ln2_gain,
        grad_ln2_bias,
        grad_up,
        grad_b_fc1,
        grad_down,
        grad_b_fc2,
    )


def solution(mesh):
    in_specs = (
        P(None, "seq", None),
        P(),
        P(),
        P(),
        P(None, None, "chan"),
        P(None, "chan"),
        P(None, None, "chan"),
        P(None, "chan"),
        P(),
        P(),
        P(),
        P(),
        P(None, "chan"),
        P("chan"),
        P("chan"),
        P("chan", None),
        P(),
        P(),
        P(),
        P(None, "chan"),
        P("chan"),
        P("chan", None),
        P(),
        P(None, "seq", None),
    )
    out_specs = (
        P(None, "seq", None),
        P(None, "seq", None),
        P(),
        P(),
        P(None, None, "chan"),
        P(None, "chan"),
        P(None, None, "chan"),
        P(None, "chan"),
        P(),
        P(),
        P(),
        P(),
        P(None, "chan"),
        P("chan"),
        P("chan"),
        P("chan", None),
        P(),
        P(),
        P(),
        P(None, "chan"),
        P("chan"),
        P("chan", None),
        P(),
    )
    chan = mesh.shape["chan"]

    def step(*arrays):
        sequences, seq_length = arrays[0].shape[:2]
        whole_sequences = sequences == mesh.shape["seq"] and chan == 4 and seq_length % (64 * sequences) == 0
        body = sequence_device if whole_sequences else spectral_device
        return jax.shard_map(
            body, mesh=mesh, in_specs=in_specs, out_specs=out_specs, check_vma=False
        )(*arrays)

    return step
```

```python
from functools import partial
import math

import jax
import jax.numpy as jnp
import ml_dtypes
import numpy as np
from jax import lax
from jax.experimental import pallas as pl
from jax.experimental.pallas import tpu as pltpu
from jax.sharding import PartitionSpec as P

EPSILON = 1e-05
HIGH_ACCURACY = lax.Precision.HIGHEST


def shifted(block, axis, distance):
    devices = range(lax.axis_size(axis))
    route = [(i - distance, i) for i in devices if i - distance in devices]
    return lax.ppermute(block, axis, route)


def layer_norm(values, gain, offset):
    average = jnp.mean(values, -1, keepdims=True)
    centered = values - average
    variance = jnp.mean(centered * centered, -1, keepdims=True)
    return centered * lax.rsqrt(variance + EPSILON) * gain + offset


def position_features(place_values, seq_length, emb_width):
    band_count = (emb_width - 1) // 2
    frequency = jnp.linspace(0.0001, band_count - 1, band_count).astype(jnp.float32)
    phases = 2.0 * math.pi * place_values[:, None] * frequency[None, :] / seq_length
    return jnp.concatenate(
        [(place_values / (seq_length - 1))[:, None], jnp.cos(phases), -jnp.sin(phases)], 1
    )


def implicit_filter(features, place_values, filt_w1, filt_b1, filt_w2, filt_b2, filt_w3, decay):
    first_layer = jnp.sin(jnp.dot(features, filt_w1, precision=HIGH_ACCURACY) + filt_b1)
    second_layer = jnp.sin(jnp.dot(first_layer, filt_w2, precision=HIGH_ACCURACY) + filt_b2)
    raw_kernel = jnp.dot(second_layer, filt_w3, precision=HIGH_ACCURACY)
    return raw_kernel * jnp.exp(-decay[None, :] * place_values[:, None])


def exact_gelu(values):
    return jax.nn.gelu(values, approximate=False)


def tables(count_rows, count_cols):
    turns = (
        jnp.arange(count_rows, dtype=jnp.int32)[:, None]
        * jnp.arange(count_cols, dtype=jnp.int32)[None, :]
        % count_rows
    )
    phases = turns.astype(jnp.float32) * (2.0 * math.pi / count_rows)
    return (jnp.cos(phases), jnp.sin(phases))


def rotate(cos_tab, sin_tab, real, imag, sign, form):
    first_part = jnp.einsum(form, cos_tab, real, precision=HIGH_ACCURACY)
    second_part = jnp.einsum(form, sin_tab, imag, precision=HIGH_ACCURACY)
    third_part = jnp.einsum(form, cos_tab, imag, precision=HIGH_ACCURACY)
    fourth_part = jnp.einsum(form, sin_tab, real, precision=HIGH_ACCURACY)
    return (first_part - sign * second_part, third_part + sign * fourth_part)


def to_spectrum(cos_tab, sin_tab, signal):
    real = jnp.einsum("wp,spc->swc", cos_tab, signal, precision=HIGH_ACCURACY)
    imag = -jnp.einsum("wp,spc->swc", sin_tab, signal, precision=HIGH_ACCURACY)
    return (real, imag)


def time_domain(cos_tab, sin_tab, real, imag):
    return jnp.einsum("wp,swc->spc", cos_tab, real, precision=HIGH_ACCURACY) - jnp.einsum(
        "wp,swc->spc", sin_tab, imag, precision=HIGH_ACCURACY
    )


def earlier_block(values):
    return jnp.pad(values, ((0, 0), (1, 0), (0, 0), (0, 0)))[:, :-1]


def later_block(values):
    return jnp.pad(values, ((0, 0), (0, 1), (0, 0), (0, 0)))[:, 1:]


def spectral_device(
    block_input,
    lengths,
    ln1_gain,
    ln1_bias,
    input_weight,
    input_bias,
    conv_w,
    conv_b,
    filt_w1,
    filt_b1,
    filt_w2,
    filt_b2,
    filt_w3,
    decay,
    skip,
    output_weight,
    output_bias,
    ln2_gain,
    ln2_bias,
    up_weight,
    up_bias,
    down_weight,
    down_bias,
    cotangent,
):
    block = block_input.shape[1]
    blocks = lax.axis_size("seq")
    share = 2 * block // blocks
    seq_index = lax.axis_index("seq")
    places = seq_index * block + jnp.arange(block, dtype=jnp.int32)
    place_values = places.astype(jnp.float32)
    mask = (places[None, :] < lengths[:, None]).astype(jnp.float32)[:, :, None]
    first_normed, norm1_pull = jax.vjp(layer_norm, block_input, ln1_gain, ln1_bias)
    input_projected = (
        jnp.einsum("spd,dkc->spkc", first_normed, input_weight, precision=HIGH_ACCURACY)
        + input_bias
    )
    rims = shifted(input_projected[:, block - 2 :], "seq", 1)
    extended = jnp.concatenate([rims, input_projected], 1)
    short = (
        conv_w[0] * extended[:, :block]
        + conv_w[1] * extended[:, 1 : block + 1]
        + conv_w[2] * extended[:, 2:]
        + conv_b
    )
    gate_out = short[:, :, 0]
    gate_in = short[:, :, 1]
    values = short[:, :, 2]
    signal = values * gate_in * mask
    cos_tab, sin_tab = tables(2 * block, block)
    block_cos, block_sin = tables(2 * blocks, blocks)
    own_freq = seq_index * share + jnp.arange(share, dtype=jnp.int32)
    parity = (1 - 2 * (own_freq % 2)).astype(jnp.float32)[:, None]
    features = position_features(place_values, blocks * block, filt_w1.shape[0])
    kernel, filter_pull = jax.vjp(
        partial(implicit_filter, features, place_values),
        filt_w1,
        filt_b1,
        filt_w2,
        filt_b2,
        filt_w3,
        decay,
    )
    signal_re, signal_im = to_spectrum(cos_tab, sin_tab, signal)
    kernel_re, kernel_im = to_spectrum(cos_tab, sin_tab, kernel[None])
    signal_re, signal_im, kernel_re, kernel_im = (
        lax.all_to_all(signal_re[:, None], "seq", split_axis=2, concat_axis=1, tiled=True),
        lax.all_to_all(signal_im[:, None], "seq", split_axis=2, concat_axis=1, tiled=True),
        lax.all_to_all(kernel_re[:, None], "seq", split_axis=2, concat_axis=1, tiled=True),
        lax.all_to_all(kernel_im[:, None], "seq", split_axis=2, concat_axis=1, tiled=True),
    )
    zq_re, zq_im = rotate(block_cos, block_sin, signal_re, signal_im, -1.0, "qk,skfc->sqfc")
    hq_re, hq_im = rotate(block_cos, block_sin, kernel_re, kernel_im, -1.0, "qk,skfc->sqfc")
    prod_re = zq_re * hq_re - zq_im * hq_im
    prod_im = zq_re * hq_im + zq_im * hq_re
    joined_re, joined_im = rotate(block_cos, block_sin, prod_re, prod_im, 1.0, "qj,sqfc->sjfc")
    joined_re = joined_re / (2 * blocks)
    joined_im = joined_im / (2 * blocks)
    folded_re = joined_re + parity * earlier_block(joined_re)
    folded_im = joined_im + parity * earlier_block(joined_im)
    folded_re, folded_im = (
        lax.all_to_all(folded_re, "seq", split_axis=1, concat_axis=2, tiled=True),
        lax.all_to_all(folded_im, "seq", split_axis=1, concat_axis=2, tiled=True),
    )
    convolved = time_domain(cos_tab, sin_tab, folded_re[:, 0], folded_im[:, 0]) / (2 * block)
    conv_sum = convolved + skip * signal
    mixer_output = conv_sum * gate_out
    partial_mix = jnp.einsum("spc,cd->spd", mixer_output, output_weight, precision=HIGH_ACCURACY)
    hidden_state = block_input + lax.psum(partial_mix, "chan") + output_bias
    second_normed2 = layer_norm(hidden_state, ln2_gain, ln2_bias)
    before = jnp.einsum("spd,df->spf", second_normed2, up_weight, precision=HIGH_ACCURACY) + up_bias
    active_units, gelu_pull = jax.vjp(exact_gelu, before)
    feed = lax.psum(
        jnp.einsum("spf,fd->spd", active_units, down_weight, precision=HIGH_ACCURACY), "chan"
    )
    output = hidden_state + feed + down_bias
    grad_b_fc2 = jnp.sum(cotangent, (0, 1))
    grad_w_fc2 = jnp.einsum("spf,spd->fd", active_units, cotangent, precision=HIGH_ACCURACY)
    grad_active = jnp.einsum("spd,fd->spf", cotangent, down_weight, precision=HIGH_ACCURACY)
    grad_before = gelu_pull(grad_active)[0]
    grad_w_fc1 = jnp.einsum("spd,spf->df", second_normed2, grad_before, precision=HIGH_ACCURACY)
    grad_b_fc1 = jnp.sum(grad_before, (0, 1))
    grad_normed2 = lax.psum(
        jnp.einsum("spf,df->spd", grad_before, up_weight, precision=HIGH_ACCURACY), "chan"
    )
    norm2_pull = jax.vjp(layer_norm, hidden_state, ln2_gain, ln2_bias)[1]
    grad_hidden_norm, grad_ln2_gain, grad_ln2_bias = norm2_pull(grad_normed2)
    grad_hidden = cotangent + grad_hidden_norm
    grad_b_out = jnp.sum(grad_hidden, (0, 1))
    grad_w_out = jnp.einsum("spc,spd->cd", mixer_output, grad_hidden, precision=HIGH_ACCURACY)
    grad_mixed = jnp.einsum("spd,cd->spc", grad_hidden, output_weight, precision=HIGH_ACCURACY)
    grad_conv = grad_mixed * gate_out
    grad_gate_out = grad_mixed * conv_sum
    grad_skip = jnp.sum(grad_conv * signal, (0, 1))
    back_re, back_im = to_spectrum(cos_tab, sin_tab, grad_conv)
    back_re = back_re / (2 * block)
    back_im = back_im / (2 * block)
    back_re, back_im = (
        lax.all_to_all(back_re[:, None], "seq", split_axis=2, concat_axis=1, tiled=True),
        lax.all_to_all(back_im[:, None], "seq", split_axis=2, concat_axis=1, tiled=True),
    )
    unfold_re = back_re + parity * later_block(back_re)
    unfold_im = back_im + parity * later_block(back_im)
    dprod_re, dprod_im = rotate(block_cos, block_sin, unfold_re, unfold_im, -1.0, "qj,sjfc->sqfc")
    dprod_re = dprod_re / (2 * blocks)
    dprod_im = dprod_im / (2 * blocks)
    dzq_re = hq_re * dprod_re + hq_im * dprod_im
    dzq_im = hq_re * dprod_im - hq_im * dprod_re
    dhq_re = jnp.sum(zq_re * dprod_re + zq_im * dprod_im, 0, keepdims=True)
    dhq_im = jnp.sum(zq_re * dprod_im - zq_im * dprod_re, 0, keepdims=True)
    dsig_re, dsig_im = rotate(block_cos, block_sin, dzq_re, dzq_im, 1.0, "qk,sqfc->skfc")
    dker_re, dker_im = rotate(block_cos, block_sin, dhq_re, dhq_im, 1.0, "qk,sqfc->skfc")
    dsig_re, dsig_im, dker_re, dker_im = (
        lax.all_to_all(dsig_re, "seq", split_axis=1, concat_axis=2, tiled=True),
        lax.all_to_all(dsig_im, "seq", split_axis=1, concat_axis=2, tiled=True),
        lax.all_to_all(dker_re, "seq", split_axis=1, concat_axis=2, tiled=True),
        lax.all_to_all(dker_im, "seq", split_axis=1, concat_axis=2, tiled=True),
    )
    grad_signal = time_domain(cos_tab, sin_tab, dsig_re[:, 0], dsig_im[:, 0]) + grad_conv * skip
    grad_kernel = time_domain(cos_tab, sin_tab, dker_re[:, 0], dker_im[:, 0])[0]
    grad_fw1, grad_fb1, grad_fw2, grad_fb2, grad_fw3, grad_decay = filter_pull(grad_kernel)
    grad_short = jnp.stack(
        [grad_gate_out, grad_signal * values * mask, grad_signal * gate_in * mask], 2
    )
    grad_conv_b = jnp.sum(grad_short, (0, 1))
    grad_conv_w = jnp.stack(
        [jnp.sum(grad_short * extended[:, offset : offset + block], (0, 1)) for offset in range(3)]
    )
    grad_extended = (
        jnp.pad(conv_w[0] * grad_short, ((0, 0), (0, 2), (0, 0), (0, 0)))
        + jnp.pad(conv_w[1] * grad_short, ((0, 0), (1, 1), (0, 0), (0, 0)))
        + jnp.pad(conv_w[2] * grad_short, ((0, 0), (2, 0), (0, 0), (0, 0)))
    )
    returned = shifted(grad_extended[:, :2], "seq", -1)
    grad_proj = grad_extended[:, 2:] + jnp.pad(returned, ((0, 0), (block - 2, 0), (0, 0), (0, 0)))
    grad_b_in = jnp.sum(grad_proj, (0, 1))
    grad_w_in = jnp.einsum("spd,spkc->dkc", first_normed, grad_proj, precision=HIGH_ACCURACY)
    grad_normed = lax.psum(
        jnp.einsum("spkc,dkc->spd", grad_proj, input_weight, precision=HIGH_ACCURACY), "chan"
    )
    grad_x_norm, grad_ln1_gain, grad_ln1_bias = norm1_pull(grad_normed)
    grad_x = grad_hidden + grad_x_norm
    (
        grad_ln1_gain,
        grad_ln1_bias,
        grad_w_in,
        grad_b_in,
        grad_conv_w,
        grad_conv_b,
        grad_fw3,
        grad_decay,
        grad_skip,
        grad_w_out,
        grad_b_out,
        grad_ln2_gain,
        grad_ln2_bias,
        grad_w_fc1,
        grad_b_fc1,
        grad_w_fc2,
        grad_b_fc2,
    ) = lax.psum(
        (
            grad_ln1_gain,
            grad_ln1_bias,
            grad_w_in,
            grad_b_in,
            grad_conv_w,
            grad_conv_b,
            grad_fw3,
            grad_decay,
            grad_skip,
            grad_w_out,
            grad_b_out,
            grad_ln2_gain,
            grad_ln2_bias,
            grad_w_fc1,
            grad_b_fc1,
            grad_w_fc2,
            grad_b_fc2,
        ),
        "seq",
    )
    grad_fw1, grad_fb1, grad_fw2, grad_fb2 = lax.psum(
        (grad_fw1, grad_fb1, grad_fw2, grad_fb2), ("seq", "chan")
    )
    return (
        output,
        grad_x,
        grad_ln1_gain,
        grad_ln1_bias,
        grad_w_in,
        grad_b_in,
        grad_conv_w,
        grad_conv_b,
        grad_fw1,
        grad_fb1,
        grad_fw2,
        grad_fb2,
        grad_fw3,
        grad_decay,
        grad_skip,
        grad_w_out,
        grad_b_out,
        grad_ln2_gain,
        grad_ln2_bias,
        grad_w_fc1,
        grad_b_fc1,
        grad_w_fc2,
        grad_b_fc2,
    )


F32 = jnp.float32
BF16 = jnp.bfloat16
NN = (((1,), (0,)), ((), ()))
NT = (((1,), (1,)), ((), ()))
TN = (((0,), (0,)), ((), ()))
VMEM_BYTES = 56 * 2**20


def parts_of(values):
    high = values.astype(BF16)
    return high, (values - high.astype(F32)).astype(BF16)


def dot_parts(left, right, dims):
    def one(a, b):
        return lax.dot_general(a, b, dims, preferred_element_type=F32)

    return one(left[0], right[0]) + (one(left[0], right[1]) + one(left[1], right[0]))


def normalise(values):
    average = jnp.mean(values, -1, keepdims=True)
    centered = values - average
    variance = jnp.mean(centered * centered, -1, keepdims=True)
    scale = lax.rsqrt(variance + EPSILON)
    return centered * scale, scale


def norm_back(unit, scale, gain, grad):
    lifted = grad * gain
    mean_one = jnp.mean(lifted, -1, keepdims=True)
    mean_two = jnp.mean(lifted * unit, -1, keepdims=True)
    return scale * (lifted - mean_one - unit * mean_two)


def fold(rows):
    half = rows.shape[0] // 2
    return jnp.concatenate([rows[:half], rows[half:]], 1)


def unfold(folded):
    width = folded.shape[1] // 2
    return jnp.concatenate([folded[:, :width], folded[:, width:]], 0)


def column_sum(values):
    return jnp.sum(values, 0, keepdims=True)


def whole(array):
    return pl.BlockSpec(array.shape, lambda *_: (0,) * len(array.shape))


def scalar_spec():
    return pl.BlockSpec(memory_space=pltpu.SMEM)


def struct(shape, kind=F32):
    return jax.ShapeDtypeStruct(tuple(shape), kind)


def run_kernel(body, name, grid, in_specs, out_specs, out_shape, scratch, args, micros):
    return pl.pallas_call(
        body,
        name=name,
        grid=grid,
        in_specs=in_specs,
        out_specs=out_specs,
        out_shape=out_shape,
        scratch_shapes=scratch,
        compiler_params=pltpu.CompilerParams(
            dimension_semantics=("arbitrary",) * len(grid), vmem_limit_bytes=VMEM_BYTES
        ),
        cost_estimate=pl.CostEstimate(
            flops=int(micros * 1.15e9), bytes_accessed=int(micros * 3.6e6), transcendentals=0
        ),
    )(*args)


def wave_tables(block):
    angles = np.pi * np.outer(2 * np.arange(block) + 1, np.arange(block)) / (2 * block)
    table = np.concatenate([np.cos(angles), -np.sin(angles)], 0)

    def both(values):
        high = values.astype(ml_dtypes.bfloat16)
        low = (values - high.astype(np.float64)).astype(ml_dtypes.bfloat16)
        return jnp.asarray(high), jnp.asarray(low)

    return both(table) + both(table.T / block)


def parity_of(rows):
    odd = lax.broadcasted_iota(jnp.int32, (rows, 1), 0) % 2
    return (1 - 2 * odd).astype(F32)


def filter_spectrum(kernel, tables):
    blocks, block, width = kernel.shape
    table_high, table_low = tables[:2]

    def body(kernel_ref, high_ref, low_ref, out_ref, before_ref):
        @pl.when(pl.program_id(0) == 0)
        def _():
            before_ref[...] = jnp.zeros_like(before_ref)

        spectrum = dot_parts((high_ref[...], low_ref[...]), parts_of(kernel_ref[0]), NN)
        sign = parity_of(block)
        out_ref[0, :block] = spectrum[:block] - sign * before_ref[block:]
        out_ref[0, block:] = spectrum[block:] + sign * before_ref[:block]
        before_ref[...] = spectrum

    return run_kernel(
        body,
        "filter_spectrum",
        (blocks,),
        [pl.BlockSpec((1, block, width), lambda b: (b, 0, 0)), whole(table_high), whole(table_low)],
        [pl.BlockSpec((1, 2 * block, width), lambda b: (b, 0, 0))],
        [struct((blocks, 2 * block, width))],
        [pltpu.VMEM((2 * block, width), F32)],
        [kernel, table_high, table_low],
        8,
    )[0]


def mixer_forward(own, length, x_parts, gain, offset, weight, bias, conv_w, conv_b, skip, spectrum, tables):
    blocks, quarter, model = x_parts[0].shape
    count = len(x_parts)
    block = quarter * count
    width = weight.shape[2]
    tile = min(32, block)
    pair = math.gcd(blocks, 4)
    span = pair * block

    def body(*refs):
        own_ref, length_ref = refs[:2]
        x_refs = refs[2 : 2 + count]
        refs = refs[2 + count :]
        gain_ref, offset_ref, weight_ref, bias_ref, conv_w_ref, conv_b_ref, skip_ref, k_ref = refs[:8]
        th_ref, tl_ref, ih_ref, il_ref = refs[8:12]
        nh_ref, nl_ref, proj_ref, conv_ref, s_ref = refs[12:17]
        m_refs = refs[17 : 17 + count]
        wh_ref, wl_ref, ext_ref, o_ref, mixed_ref = refs[17 + count :]
        step = pl.program_id(0)
        me = own_ref[0]

        @pl.when(step == 0)
        def _():
            for k in range(3):
                wh_ref[k], wl_ref[k] = parts_of(weight_ref[k])
            ext_ref[:, :8] = jnp.zeros((3, 8, width), F32)

        for u in range(pair):
            for k in range(count):
                normed = normalise(x_refs[k][u])[0] * gain_ref[...] + offset_ref[...]
                start = pl.multiple_of(u * block + (me ^ k) * quarter, quarter)
                high, low = parts_of(normed)
                nh_ref[0, pl.ds(start, quarter), :] = high
                nl_ref[0, pl.ds(start, quarter), :] = low
        normed = (nh_ref[0], nl_ref[0])
        short = []
        for k in range(3):
            proj = dot_parts(normed, (wh_ref[k], wl_ref[k]), NN) + bias_ref[k : k + 1, :]
            proj_ref[0, k] = proj
            ext_ref[k, 8:] = proj
            short.append(
                conv_w_ref[0, k : k + 1, :] * ext_ref[k, 6 : 6 + span]
                + conv_w_ref[1, k : k + 1, :] * ext_ref[k, 7 : 7 + span]
                + conv_w_ref[2, k : k + 1, :] * proj
                + conv_b_ref[k : k + 1, :]
            )
            ext_ref[k, :8] = ext_ref[k, span:]
        places = step * span + lax.broadcasted_iota(jnp.int32, (span, 1), 0)
        mask = (places < length_ref[0]).astype(F32)
        signal = short[2] * short[1] * mask
        for u in range(pair):
            part = signal[u * block : (u + 1) * block]
            s_ref[step * pair + u] = dot_parts((th_ref[...], tl_ref[...]), parts_of(part), NN)
        for u in range(pair):
            b = step * pair + u
            for r in range(0, block, tile):
                lo = slice(r, r + tile)
                hi = slice(block + r, block + r + tile)

                def product(i, total, b=b, lo=lo, hi=hi):
                    s_re, s_im = s_ref[i, lo], s_ref[i, hi]
                    k_re, k_im = k_ref[b - i, lo], k_ref[b - i, hi]
                    return total[0] + s_re * k_re - s_im * k_im, total[1] + s_re * k_im + s_im * k_re

                zero = jnp.zeros((tile, width), F32)
                o_ref[u, lo], o_ref[u, hi] = lax.fori_loop(0, b + 1, product, (zero, zero))
        inverse = (ih_ref[...], il_ref[...])
        conv = jnp.concatenate([dot_parts(inverse, parts_of(o_ref[u]), NN) for u in range(pair)], 0)
        conv = conv + skip_ref[...] * signal
        conv_ref[0] = conv
        mixed_ref[...] = conv * short[0]
        for u in range(pair):
            for k in range(count):
                start = pl.multiple_of(u * block + (me ^ k) * quarter, quarter)
                m_refs[k][u] = fold(mixed_ref[pl.ds(start, quarter), :])

    by_block = lambda *shape: pl.BlockSpec((1,) + shape, lambda b: (b,) + (0,) * len(shape))
    args = [own, length, *x_parts, gain, offset, weight, bias, conv_w, conv_b, skip, spectrum, *tables]
    by_pair = lambda n: pl.BlockSpec((pair, quarter, n), lambda b: (b, 0, 0))
    in_specs = [scalar_spec(), scalar_spec()] + [by_pair(model)] * count
    in_specs += [whole(a) for a in args[2 + count :]]
    folded = pl.BlockSpec((pair, quarter // 2, 2 * width), lambda b: (b, 0, 0))
    s_shape = struct((blocks, 2 * block, width))
    outs = run_kernel(
        body,
        "mixer_forward",
        (blocks // pair,),
        in_specs,
        [by_block(span, model)] * 2
        + [by_block(3, span, width), by_block(span, width), whole(s_shape)]
        + [folded] * count,
        [struct((blocks // pair, span, model), BF16)] * 2
        + [struct((blocks // pair, 3, span, width)), struct((blocks // pair, span, width)), s_shape]
        + [struct((blocks, quarter // 2, 2 * width))] * count,
        [
            pltpu.VMEM((3, model, width), BF16),
            pltpu.VMEM((3, model, width), BF16),
            pltpu.VMEM((3, span + 8, width), F32),
            pltpu.VMEM((pair, 2 * block, width), F32),
            pltpu.VMEM((span, width), F32),
        ],
        args,
        36,
    )
    return outs[:5], list(outs[5:])


def hidden_forward(m_parts, weights, x_own, cotangent, bias, gain, offset):
    blocks, half, width = m_parts[0].shape
    rows, model = x_own.shape
    width = width // 2
    count = len(m_parts)
    group = math.gcd(blocks, max(128 // half, 1))
    step = 2 * half * group

    def body(*refs):
        m_refs, w_refs = refs[:count], refs[count : 2 * count]
        x_ref, c_ref, bias_ref, gain_ref, offset_ref = refs[2 * count : 2 * count + 5]
        h_ref, nh_ref, nl_ref, th_ref, tl_ref, ch_ref, cl_ref = refs[2 * count + 5 : 2 * count + 12]
        wh_ref, wl_ref = refs[2 * count + 12 :]

        @pl.when(pl.program_id(0) == 0)
        def _():
            for k in range(count):
                wh_ref[k], wl_ref[k] = parts_of(w_refs[k][...])

        hidden = x_ref[...] + bias_ref[...]
        for k in range(count):
            mixed = jnp.concatenate([unfold(m_refs[k][u]) for u in range(group)], 0)
            hidden = hidden + dot_parts(parts_of(mixed), (wh_ref[k], wl_ref[k]), NN)
        h_ref[...] = hidden
        normed = normalise(hidden)[0] * gain_ref[...] + offset_ref[...]
        nh_ref[...], nl_ref[...] = parts_of(normed)
        th_ref[...], tl_ref[...] = parts_of(normed.T)
        ch_ref[...], cl_ref[...] = parts_of(c_ref[...])

    row_spec = lambda n: pl.BlockSpec((step, n), lambda r: (r, 0))
    turned = pl.BlockSpec((model, step), lambda r: (0, r))
    args = [*m_parts, *weights, x_own, cotangent, bias, gain, offset]
    return run_kernel(
        body,
        "hidden_forward",
        (rows // step,),
        [pl.BlockSpec((group, half, 2 * width), lambda r: (r, 0, 0))] * count
        + [whole(w) for w in weights]
        + [row_spec(model)] * 2
        + [whole(bias), whole(gain), whole(offset)],
        [row_spec(model)] * 3 + [turned] * 2 + [row_spec(model)] * 2,
        [struct((rows, model))]
        + [struct((rows, model), BF16)] * 2
        + [struct((model, rows), BF16)] * 2
        + [struct((rows, model), BF16)] * 2,
        [pltpu.VMEM((count, width, model), BF16)] * 2,
        args,
        9,
    )


def feed_forward(side, normed, turned, cotangent, up, up_bias, down, sums):
    rows, model = normed[0].shape
    units = up_bias.shape[1]
    step = min(256, units)
    first = sums is None
    pieces = len(up)

    def body(side_ref, *refs):
        nh_ref, nl_ref, th_ref, tl_ref, ch_ref, cl_ref, bias_ref = refs[:7]
        up_refs, down_refs = refs[7 : 7 + pieces], refs[7 + pieces : 7 + 2 * pieces]
        refs = refs[7 + 2 * pieces :]
        feed_in, grad_in = (None, None) if first else refs[:2]
        feed_ref, grad_ref, gup_ref, gdown_ref, gbias_ref = refs[0 if first else 2 :]

        @pl.when(pl.program_id(0) == 0)
        def _():
            if first:
                feed_ref[...] = jnp.zeros_like(feed_ref)
                grad_ref[...] = jnp.zeros_like(grad_ref)
            else:
                feed_ref[...] = feed_in[...]
                grad_ref[...] = grad_in[...]

        def in_order(halves, axis):
            if pieces == 1:
                return halves[0][...]
            mine, other = halves[0][...], halves[1][...]
            low = side_ref[0] == 0
            return jnp.concatenate([jnp.where(low, mine, other), jnp.where(low, other, mine)], axis)

        own_normed = (nh_ref[...], nl_ref[...])
        own_cotangent = (ch_ref[...], cl_ref[...])
        up_parts = parts_of(in_order(up_refs, 0))
        down_parts = parts_of(in_order(down_refs, 1))
        before = dot_parts(own_normed, up_parts, NN) + bias_ref[...]
        grad_active = dot_parts(own_cotangent, down_parts, NT)
        below = 0.5 + 0.5 * lax.erf(before * math.sqrt(0.5))
        slope = below + before * (jnp.exp(-0.5 * before * before) * (1.0 / math.sqrt(2.0 * math.pi)))
        active = before * below
        grad_before = grad_active * slope
        gbias_ref[...] = column_sum(grad_before)
        active_parts = parts_of(active)
        grad_parts = parts_of(grad_before)
        feed_ref[...] += dot_parts(active_parts, down_parts, NN)
        grad_ref[...] += dot_parts(grad_parts, up_parts, NT)
        gup_ref[...] = dot_parts((th_ref[...], tl_ref[...]), grad_parts, NN)
        gdown_ref[...] = dot_parts(active_parts, own_cotangent, TN)

    total = struct((rows, model))
    args = [side, *normed, *turned, *cotangent, up_bias, *up, *down] + ([] if first else list(sums))
    columns = lambda n: pl.BlockSpec((n, step), lambda t: (0, t))
    some_rows = lambda n: pl.BlockSpec((step, n), lambda t: (t, 0))
    outs = run_kernel(
        body,
        "feed_forward",
        (units // step,),
        [scalar_spec()]
        + [whole(a) for a in args[1:7]]
        + [columns(1)]
        + [columns(model // pieces)] * pieces
        + [some_rows(model // pieces)] * pieces
        + [whole(a) for a in args[8 + 2 * pieces :]],
        [whole(total), whole(total), columns(model), some_rows(model), columns(1)],
        [total, total, struct((model, units)), struct((units, model)), struct(up_bias.shape)],
        [],
        args,
        18,
    )
    return outs[:2], outs[2:]


def feed_forward_pair(normed, turned, cotangent, ups, biases, downs, sums):
    rows, model = normed[0].shape
    units = biases[0].shape[1]
    step = min(256, units)
    tiles = units // step

    def body(*refs):
        nh_ref, nl_ref, th_ref, tl_ref, ch_ref, cl_ref, bias_ref = refs[:7]
        up_refs, down_refs, (feed_in, grad_in) = refs[7:9], refs[9:11], refs[11:13]
        feed_ref, grad_ref, gbias_ref = refs[13:16]
        gup_refs, gdown_refs = refs[16:18], refs[18:20]
        uh_ref, ul_ref, dh_ref, dl_ref = refs[20:]
        t = pl.program_id(0)

        @pl.when(t == 0)
        def _():
            feed_ref[...] = feed_in[...]
            grad_ref[...] = grad_in[...]

        for j in range(2):

            @pl.when(t // tiles == j)
            def _(j=j):
                uh_ref[...], ul_ref[...] = parts_of(up_refs[j][...])
                dh_ref[...], dl_ref[...] = parts_of(down_refs[j][...])

        own_normed = (nh_ref[...], nl_ref[...])
        own_cotangent = (ch_ref[...], cl_ref[...])
        up_parts, down_parts = (uh_ref[...], ul_ref[...]), (dh_ref[...], dl_ref[...])
        before = dot_parts(own_normed, up_parts, NN) + bias_ref[...]
        grad_active = dot_parts(own_cotangent, down_parts, NT)
        below = 0.5 + 0.5 * lax.erf(before * math.sqrt(0.5))
        slope = below + before * (jnp.exp(-0.5 * before * before) * (1.0 / math.sqrt(2.0 * math.pi)))
        active = before * below
        grad_before = grad_active * slope
        gbias_ref[...] = column_sum(grad_before)
        active_parts = parts_of(active)
        grad_parts = parts_of(grad_before)
        feed_ref[...] += dot_parts(active_parts, down_parts, NN)
        grad_ref[...] += dot_parts(grad_parts, up_parts, NT)
        grad_up = dot_parts((th_ref[...], tl_ref[...]), grad_parts, NN)
        grad_down = dot_parts(active_parts, own_cotangent, TN)
        for j in range(2):

            @pl.when(t // tiles == j)
            def _(j=j):
                gup_refs[j][...] = grad_up
                gdown_refs[j][...] = grad_down

    total = struct((rows, model))
    bias = jnp.concatenate(biases, 1)
    args = [*normed, *turned, *cotangent, bias, *ups, *downs, *sums]
    place = lambda t, j: jnp.minimum(t, tiles - 1) if j == 0 else jnp.maximum(t - tiles, 0)
    columns = [pl.BlockSpec((model, step), lambda t, j=j: (0, place(t, j))) for j in range(2)]
    some_rows = [pl.BlockSpec((step, model), lambda t, j=j: (place(t, j), 0)) for j in range(2)]
    one_row = pl.BlockSpec((1, step), lambda t: (0, t))
    outs = run_kernel(
        body,
        "feed_forward_pair",
        (2 * tiles,),
        [whole(a) for a in args[:6]] + [one_row] + columns + some_rows + [whole(total)] * 2,
        [whole(total)] * 2 + [one_row] + columns + some_rows,
        [total, total, struct(bias.shape)] + [struct((model, units))] * 2 + [struct((units, model))] * 2,
        [pltpu.VMEM((model, step), BF16)] * 2 + [pltpu.VMEM((step, model), BF16)] * 2,
        args,
        31,
    )
    return outs[:2], outs[2], outs[3:5], outs[5:7]


def hidden_backward(hidden, feed, grad_normed, cotangent, m_parts, weights, gain, bias):
    rows, model = hidden.shape
    blocks, half, width = m_parts[0].shape
    width = width // 2
    count = len(m_parts)
    group = math.gcd(blocks, max(128 // half, 1))
    step = 2 * half * group

    def body(*refs):
        h_ref, f_ref, g_ref, c_ref = refs[:4]
        m_refs, w_refs = refs[4 : 4 + count], refs[4 + count : 4 + 2 * count]
        gain_ref, bias_ref, out_ref, gh_ref, sum_ref = refs[4 + 2 * count : 9 + 2 * count]
        gm_refs, refs = refs[9 + 2 * count : 9 + 3 * count], refs[9 + 3 * count :]
        gw_refs, (wh_ref, wl_ref) = refs[:2], refs[2:]

        @pl.when(pl.program_id(0) == 0)
        def _():
            sum_ref[...] = jnp.zeros_like(sum_ref)
            for k in range(count):
                wh_ref[k], wl_ref[k] = parts_of(w_refs[k][...])
            for k in range(2):
                gw_refs[k][...] = jnp.zeros_like(gw_refs[k])

        hidden_rows, grad, above = h_ref[...], g_ref[...], c_ref[...]
        out_ref[...] = hidden_rows + f_ref[...] + bias_ref[...]
        unit, scale = normalise(hidden_rows)
        grad_hidden = above + norm_back(unit, scale, gain_ref[...], grad)
        gh_ref[...] = grad_hidden
        sum_ref[0:1] += column_sum(grad * unit)
        sum_ref[1:2] += column_sum(grad)
        sum_ref[2:3] += column_sum(grad_hidden)
        sum_ref[3:4] += column_sum(above)
        parts = parts_of(grad_hidden)
        for k in range(count):
            grad_mixed = dot_parts(parts, (wh_ref[k], wl_ref[k]), NT)
            for u in range(group):
                gm_refs[k][u] = fold(grad_mixed[u * 2 * half : (u + 1) * 2 * half])
            mixed = jnp.concatenate([unfold(m_refs[k][u]) for u in range(group)], 0)
            gw_refs[k // 2][k % 2] += dot_parts(parts_of(mixed), parts, TN)

    folded = pl.BlockSpec((group, half, 2 * width), lambda r: (r, 0, 0))
    row_spec = lambda n: pl.BlockSpec((step, n), lambda r: (r, 0))
    args = [hidden, feed, grad_normed, cotangent, *m_parts, *weights, gain, bias]
    sums, pair = struct((8, model)), struct((2, width, model))
    outs = run_kernel(
        body,
        "hidden_backward",
        (rows // step,),
        [row_spec(model)] * 4 + [folded] * count + [whole(w) for w in weights] + [whole(gain), whole(bias)],
        [row_spec(model)] * 2
        + [whole(sums)]
        + [folded] * count
        + [whole(pair)] * 2,
        [struct((rows, model))] * 2 + [sums] + [struct((blocks, half, 2 * width))] * count + [pair] * 2,
        [pltpu.VMEM((count, width, model), BF16)] * 2,
        args,
        15,
    )
    return outs[:3], list(outs[3 : 3 + count]), outs[3 + count :]


def mixer_backward(own, length, gm_parts, proj, conv, s_spec, k_spec, conv_w, conv_b, skip, weight, tables):
    blocks, quarter, width = gm_parts[0].shape
    quarter, width = 2 * quarter, width // 2
    count = len(gm_parts)
    block = quarter * count
    model = weight.shape[1]
    tile = min(32, block)
    pair = math.gcd(blocks, 4)
    span = pair * block

    def body(*refs):
        own_ref, length_ref = refs[:2]
        gm_refs = refs[2 : 2 + count]
        refs = refs[2 + count :]
        proj_ref, rim_ref, conv_ref, k_ref, conv_w_ref, conv_b_ref, skip_ref, weight_ref = refs[:8]
        th_ref, tl_ref, ih_ref, il_ref = refs[8:12]
        g_ref, gp_ref, sum_ref = refs[12:15]
        gn_refs = refs[15 : 15 + count]
        wh_ref, wl_ref, ext_ref, gs_ref, o_ref, rows_ref, gn_ref = refs[15 + count :]
        step = pl.program_id(0)
        slot = blocks // pair - 1 - step
        me = own_ref[0]

        @pl.when(step == 0)
        def _():
            for k in range(3):
                wh_ref[k], wl_ref[k] = parts_of(weight_ref[k])
            gs_ref[:, span:] = jnp.zeros((3, 8, width), F32)
            sum_ref[...] = jnp.zeros_like(sum_ref)

        for u in range(pair):
            for k in range(count):
                start = pl.multiple_of(u * block + (me ^ k) * quarter, quarter)
                rows_ref[pl.ds(start, quarter), :] = unfold(gm_refs[k][u])
        inside = (slot > 0).astype(F32)
        short = []
        for k in range(3):
            ext_ref[k, :8] = rim_ref[0, k] * inside
            ext_ref[k, 8:] = proj_ref[0, k]
            short.append(
                conv_w_ref[0, k : k + 1, :] * ext_ref[k, 6 : 6 + span]
                + conv_w_ref[1, k : k + 1, :] * ext_ref[k, 7 : 7 + span]
                + conv_w_ref[2, k : k + 1, :] * proj_ref[0, k]
                + conv_b_ref[k : k + 1, :]
            )
        places = slot * span + lax.broadcasted_iota(jnp.int32, (span, 1), 0)
        mask = (places < length_ref[0]).astype(F32)
        gate_in, values = short[1] * mask, short[2] * mask
        grad_mixed = rows_ref[...]
        grad_conv = grad_mixed * short[0]
        gs_ref[0, :span] = grad_mixed * conv_ref[0]
        for u in range(pair):
            part = grad_conv[u * block : (u + 1) * block]
            g_ref[slot * pair + u] = dot_parts((th_ref[...], tl_ref[...]), parts_of(part), NN)
        for u in range(pair):
            b = slot * pair + u
            for r in range(0, block, tile):
                lo = slice(r, r + tile)
                hi = slice(block + r, block + r + tile)

                def product(j, total, b=b, lo=lo, hi=hi):
                    g_re, g_im = g_ref[j, lo], g_ref[j, hi]
                    k_re, k_im = k_ref[j - b, lo], k_ref[j - b, hi]
                    return total[0] + g_re * k_re + g_im * k_im, total[1] + g_im * k_re - g_re * k_im

                zero = jnp.zeros((tile, width), F32)
                o_ref[u, lo], o_ref[u, hi] = lax.fori_loop(b, blocks, product, (zero, zero))
        inverse = (ih_ref[...], il_ref[...])
        grad_signal = jnp.concatenate([dot_parts(inverse, parts_of(o_ref[u]), NN) for u in range(pair)], 0)
        grad_signal = grad_signal + skip_ref[...] * grad_conv
        gs_ref[1, :span] = grad_signal * values
        gs_ref[2, :span] = grad_signal * gate_in
        sum_ref[0:1] += column_sum(grad_conv * short[2] * gate_in)
        normed_grad = jnp.zeros((span, model), F32)
        for k in range(3):
            grad_short = gs_ref[k, :span]
            sum_ref[1 + k : 2 + k] += column_sum(grad_short)
            for t in range(3):
                row = 4 + 3 * t + k
                sum_ref[row : row + 1] += column_sum(grad_short * ext_ref[k, 6 + t : 6 + t + span])
            grad_proj = (
                conv_w_ref[2, k : k + 1, :] * grad_short
                + conv_w_ref[1, k : k + 1, :] * gs_ref[k, 1 : 1 + span]
                + conv_w_ref[0, k : k + 1, :] * gs_ref[k, 2 : 2 + span]
            )
            sum_ref[13 + k : 14 + k] += column_sum(grad_proj)
            gp_ref[0, k] = grad_proj
            normed_grad = normed_grad + dot_parts(parts_of(grad_proj), (wh_ref[k], wl_ref[k]), NT)
            gs_ref[k, span:] = gs_ref[k, :8]
        gn_ref[...] = normed_grad
        for u in range(pair):
            for k in range(count):
                start = pl.multiple_of(u * block + (me ^ k) * quarter, quarter)
                gn_refs[k][u] = gn_ref[pl.ds(start, quarter), :]

    last = blocks // pair - 1
    by_block = lambda *shape: pl.BlockSpec((1,) + shape, lambda s: (last - s,) + (0,) * len(shape))
    rim = pl.BlockSpec((1, 3, 8, width), lambda s: (jnp.maximum(last - s - 1, 0), 0, span // 8 - 1, 0))
    by_pair = lambda n: pl.BlockSpec((pair, quarter, n), lambda s: (last - s, 0, 0))
    fixed = [k_spec, conv_w, conv_b, skip, weight, *tables]
    spectra = struct((blocks, 2 * block, width))
    sums = struct((16, width))
    outs = run_kernel(
        body,
        "mixer_backward",
        (blocks // pair,),
        [scalar_spec(), scalar_spec()]
        + [pl.BlockSpec((pair, quarter // 2, 2 * width), lambda s: (last - s, 0, 0))] * count
        + [by_block(3, span, width), rim, by_block(span, width)]
        + [whole(a) for a in fixed],
        [whole(spectra), by_block(3, span, width), whole(sums)] + [by_pair(model)] * count,
        [spectra, struct((blocks // pair, 3, span, width)), sums] + [struct((blocks, quarter, model))] * count,
        [
            pltpu.VMEM((3, model, width), BF16),
            pltpu.VMEM((3, model, width), BF16),
            pltpu.VMEM((3, span + 8, width), F32),
            pltpu.VMEM((3, span + 8, width), F32),
            pltpu.VMEM((pair, 2 * block, width), F32),
            pltpu.VMEM((span, width), F32),
            pltpu.VMEM((span, model), F32),
        ],
        [own, length, *gm_parts, proj, proj, conv, *fixed],
        35,
    )
    return outs[:3], list(outs[3:])


def filter_backward(s_spec, g_spec, tables):
    blocks, double, width = s_spec.shape
    block = double // 2
    tile = min(32, block)
    inverse = tables[2:]

    def body(s_ref, g_ref, ih_ref, il_ref, out_ref, after_ref, o_ref):
        m = blocks - 1 - pl.program_id(0)

        @pl.when(m == blocks - 1)
        def _():
            after_ref[...] = jnp.zeros_like(after_ref)

        sign = parity_of(tile)
        for r in range(0, block, tile):
            lo = slice(r, r + tile)
            hi = slice(block + r, block + r + tile)

            def product(j, total, lo=lo, hi=hi):
                g_re, g_im = g_ref[j, lo], g_ref[j, hi]
                s_re, s_im = s_ref[j - m, lo], s_ref[j - m, hi]
                return total[0] + g_re * s_re + g_im * s_im, total[1] + g_im * s_re - g_re * s_im

            zero = jnp.zeros((tile, width), F32)
            re, im = lax.fori_loop(m, blocks, product, (zero, zero))
            o_ref[lo] = re + sign * after_ref[hi]
            o_ref[hi] = im - sign * after_ref[lo]
            after_ref[lo], after_ref[hi] = re, im
        out_ref[0] = dot_parts((ih_ref[...], il_ref[...]), parts_of(o_ref[...]), NN)

    return run_kernel(
        body,
        "filter_backward",
        (blocks,),
        [whole(s_spec), whole(g_spec), whole(inverse[0]), whole(inverse[1])],
        [pl.BlockSpec((1, block, width), lambda s: (blocks - 1 - s, 0, 0))],
        [struct((blocks, block, width))],
        [pltpu.VMEM((double, width), F32)] * 2,
        [s_spec, g_spec, *inverse],
        13,
    )[0]


def input_weight_grad(normed_high, normed_low, grad_proj):
    blocks, block, model = normed_high.shape
    width = grad_proj.shape[3]

    def body(nh_ref, nl_ref, gp_ref, out_ref):
        @pl.when(pl.program_id(0) == 0)
        def _():
            out_ref[...] = jnp.zeros_like(out_ref)

        normed = (nh_ref[0], nl_ref[0])
        for k in range(3):
            out_ref[k] += dot_parts(parts_of(gp_ref[0, k]), normed, TN)

    by_block = lambda *shape: pl.BlockSpec((1,) + shape, lambda b: (b,) + (0,) * len(shape))
    out = struct((3, width, model))
    return run_kernel(
        body,
        "input_weight_grad",
        (blocks,),
        [by_block(block, model)] * 2 + [by_block(3, block, width)],
        [whole(out)],
        [out],
        [],
        [normed_high, normed_low, grad_proj],
        12,
    )[0]


def input_backward(grad_pieces, x_own, grad_hidden, gain):
    rows, model = x_own.shape
    count = len(grad_pieces)
    step = min(256, rows)

    def body(*refs):
        piece_refs = refs[:count]
        x_ref, gh_ref, gain_ref, out_ref, sum_ref = refs[count:]

        @pl.when(pl.program_id(0) == 0)
        def _():
            sum_ref[...] = jnp.zeros_like(sum_ref)

        grad = sum(r[...] for r in piece_refs)
        unit, scale = normalise(x_ref[...])
        out_ref[...] = gh_ref[...] + norm_back(unit, scale, gain_ref[...], grad)
        sum_ref[0:1] += column_sum(grad * unit)
        sum_ref[1:2] += column_sum(grad)

    row_spec = pl.BlockSpec((step, model), lambda r: (r, 0))
    sums = struct((8, model))
    return run_kernel(
        body,
        "input_backward",
        (rows // step,),
        [row_spec] * (count + 2) + [whole(gain)],
        [row_spec, whole(sums)],
        [struct((rows, model)), sums],
        [],
        [*grad_pieces, x_own, grad_hidden, gain],
        5,
    )


def put_together(own, pieces):
    groups, quarter, model = pieces[0].shape
    count = len(pieces)
    pair = 2 - groups % 2

    def body(own_ref, *refs):
        for u in range(pair):
            for k in range(count):
                start = pl.multiple_of((own_ref[0] ^ k) * quarter, quarter)
                refs[count][u, pl.ds(start, quarter), :] = refs[k][u]

    by_group = lambda n: pl.BlockSpec((pair, n, model), lambda s: (s, 0, 0))
    return run_kernel(
        body,
        "put_together",
        (groups // pair,),
        [scalar_spec()] + [by_group(quarter)] * count,
        [by_group(quarter * count)],
        [struct((groups, quarter * count, model))],
        [],
        [own, *pieces],
        8,
    )[0]


def swap(values, axis, bit):
    size = lax.axis_size(axis)
    return lax.ppermute(values, axis, [(i, i ^ bit) for i in range(size)])


def total_over(values, axis):
    bit = 1
    while bit < lax.axis_size(axis):
        values = values + swap(values, axis, bit)
        bit *= 2
    return values


def meet(*values):
    return lax.optimization_barrier(values)


def split_rows(values, axis, bit):
    mine = (lax.axis_index(axis) // bit) % 2
    half = values.shape[0] // 2
    leaving = lax.dynamic_slice_in_dim(values, (1 - mine) * half, half, 0)
    staying = lax.dynamic_slice_in_dim(values, mine * half, half, 0)
    return leaving, staying


def join_rows(values, other, axis, bit):
    first = (lax.axis_index(axis) // bit) % 2 == 0
    return jnp.concatenate([jnp.where(first, values, other), jnp.where(first, other, values)], 0)


def transpose_blocks(values):
    return lax.all_to_all(values, "seq", split_axis=0, concat_axis=0, tiled=True)


def spread(values):
    far = swap(values, "chan", 2)
    return [values, swap(values, "chan", 1), far, swap(far, "chan", 1)]


def collect(pieces):
    far = pieces[2] + swap(pieces[3], "chan", 1)
    return [pieces[0], swap(pieces[1], "chan", 1), swap(far, "chan", 2)]


def pack(arrays):
    flat = jnp.concatenate([a.reshape(-1) for a in arrays])
    return jnp.pad(flat, (0, -flat.shape[0] % 1024))


def unpack(flat, arrays):
    out = []
    start = 0
    for a in arrays:
        size = math.prod(a.shape)
        out.append(flat[start : start + size].reshape(a.shape))
        start += size
    return out


def sequence_device(
    block_input,
    lengths,
    ln1_gain,
    ln1_bias,
    input_weight,
    input_bias,
    conv_w,
    conv_b,
    filt_w1,
    filt_b1,
    filt_w2,
    filt_b2,
    filt_w3,
    decay,
    skip,
    output_weight,
    output_bias,
    ln2_gain,
    ln2_bias,
    up_weight,
    up_bias,
    down_weight,
    down_bias,
    cotangent,
):
    blocks, block, model = block_input.shape
    count = lax.axis_size("chan")
    quarter = block // count
    rows = blocks * quarter
    width = decay.shape[0]
    seq_length = blocks * block
    seq_index = lax.axis_index("seq")
    chan_index = lax.axis_index("chan")
    own = chan_index.astype(jnp.int32).reshape(1)
    length = lax.dynamic_slice(lengths, (seq_index,), (1,))
    tables = wave_tables(block)
    row = lambda v: v.reshape(1, -1)

    def own_rows(values):
        part = lax.dynamic_slice_in_dim(values, chan_index * quarter, quarter, 1)
        return transpose_blocks(part)

    place_values = jnp.arange(seq_length, dtype=jnp.int32).astype(F32)
    features = position_features(place_values, seq_length, filt_w1.shape[0])
    kernel, filter_pull = jax.vjp(
        partial(implicit_filter, features, place_values), filt_w1, filt_b1, filt_w2, filt_b2, filt_w3, decay
    )
    k_spec = filter_spectrum(kernel.reshape(blocks, block, width), tables)
    weight = jnp.transpose(input_weight, (1, 0, 2))

    x_own = own_rows(block_input)
    side = (seq_index % 2).astype(jnp.int32)

    def half_of(values, axis):
        half = values.shape[axis] // 2
        return lax.dynamic_slice_in_dim(values, side * half, half, axis)

    up_far = swap(half_of(up_weight, 0), "chan", 2)
    up_bias_parts = [swap(up_bias, "chan", k) if k else up_bias for k in range(count)]
    x_own, k_spec, weight, up_far, up_bias_parts, cotangent_home = meet(
        x_own, k_spec, weight, up_far, up_bias_parts, cotangent
    )
    x_far = swap(x_own, "chan", 2)
    x_parts = [x_own, swap(x_own, "chan", 1), x_far, swap(x_far, "chan", 1)]
    cot_own = own_rows(cotangent_home)
    x_rows = x_own.reshape(rows, model)
    x_parts[2], out_home, down_home, up_far = meet(x_parts[2], output_weight, down_weight, up_far)
    out_far = swap(out_home, "chan", 2)
    down_far = swap(half_of(down_home, 1), "chan", 2)
    up_other = swap(up_far, "seq", 1)
    x_parts[0], cot_own = meet(x_parts[0], cot_own)
    cot_own = cot_own.reshape(rows, model)

    (normed_high, normed_low, proj, conv, s_spec), mixed = mixer_forward(
        own, length, x_parts, row(ln1_gain), row(ln1_bias), weight, input_bias, conv_w, conv_b, row(skip), k_spec, tables
    )
    *mixed, down_far, out_far, up_other = meet(*mixed, down_far, out_far, up_other)
    mixed = [m if k == 0 else swap(m, "chan", k) for k, m in enumerate(mixed)]
    down_other = swap(down_far, "seq", 1)
    out_3 = swap(out_far, "chan", 1)
    *mixed, out_3 = meet(*mixed, out_3)
    out_parts = [output_weight, swap(output_weight, "chan", 1), out_far, out_3]
    up_parts = [[up_weight], [swap(up_weight, "chan", 1)], [up_far, up_other]]
    up_parts.append([swap(u, "chan", 1) for u in up_parts[2]])
    down_side = swap(down_far, "chan", 1)

    hidden, *rest = hidden_forward(
        mixed, out_parts, x_rows, cot_own, row(output_bias), row(ln2_gain), row(ln2_bias)
    )
    rest, down_other, down_side = meet(rest, down_other, down_side)
    normed2, turned, cot_parts = rest[0:2], rest[2:4], rest[4:6]
    down_parts = [[down_weight], [swap(down_weight, "chan", 1)], [down_far, down_other]]
    down_parts.append([down_side, swap(down_other, "chan", 1)])

    def units(k, sums):
        return feed_forward(
            side.reshape(1), normed2, turned, cot_parts, up_parts[k], row(up_bias_parts[k]), down_parts[k], sums
        )

    bias_grads = [None] * count
    sums, (up_3, down_3, bias_grads[3]) = units(3, None)
    up_3, down_3 = swap(up_3, "chan", 1), swap(down_3, "chan", 1)
    sums, (up_2, down_2, bias_grads[2]) = units(2, sums)
    *sums, up_2, up_3, down_2, down_3 = meet(*sums, up_2, up_3, down_2, down_3)

    third = model // 3
    far_up = lambda i: up_2[i * third : (i + 1) * third] + up_3[i * third : (i + 1) * third]
    leaving_2, staying_2 = split_rows(down_2, "seq", 1)
    leaving_3, staying_3 = split_rows(down_3, "seq", 1)
    far_ups = [swap(up_2[: 2 * third] + up_3[: 2 * third], "chan", 2)]
    came = swap(leaving_2 + leaving_3, "seq", 1)
    sums, near_bias, (up_1, up_0), (down_1, down_0) = feed_forward_pair(
        normed2, turned, cot_parts, [up_parts[1][0], up_parts[0][0]], [row(up_bias_parts[1]), row(up_bias_parts[0])],
        [down_parts[1][0], down_parts[0][0]], sums,
    )
    bias_grads[1], bias_grads[0] = jnp.split(near_bias, 2, 1)
    *sums, far_ups[0], came, up_1, down_1 = meet(*sums, far_ups[0], came, up_1, down_1)
    down_1, up_1 = swap(down_1, "chan", 1), swap(up_1, "chan", 1)
    far_ups.append(swap(up_2[2 * third :] + up_3[2 * third :], "chan", 2))
    leaving, far_staying = split_rows(staying_2 + staying_3 + came, "seq", 2)
    far_came = swap(leaving, "seq", 2)
    leaving_0, staying_0 = split_rows(down_0, "seq", 1)
    leaving_1, staying_1 = split_rows(down_1, "seq", 1)
    near_leaving = leaving_0 + leaving_1
    near_leaving, *sums = meet(near_leaving, *sums)
    near_came = swap(near_leaving, "seq", 1)
    (out_rows, grad_hidden, sums2), grad_mixed, (out_near, out_far) = hidden_backward(
        hidden, sums[0], sums[1], cot_own, mixed, out_parts, row(ln2_gain), row(down_bias)
    )
    grad_hidden, far_ups[1], far_came, grad_mixed, out_rows, up_1 = meet(
        grad_hidden, far_ups[1], far_came, grad_mixed, out_rows, up_1
    )

    grad_mixed = [g if k == 0 else swap(g, "chan", k) for k, g in enumerate(grad_mixed)]
    leaving, far_staying = split_rows(far_staying + far_came, "seq", 4)
    far_came = swap(leaving, "seq", 4)
    out_blocks = transpose_blocks(out_rows.reshape(blocks, quarter, model))
    grad_up = up_0 + up_1 + jnp.concatenate(far_ups, 0)
    up_leaving, up_staying = split_rows(grad_up, "seq", 1)
    grad_mixed, up_leaving, up_staying, out_far, near_came = meet(
        grad_mixed, up_leaving, up_staying, out_far, near_came
    )

    up_came = swap(up_leaving, "seq", 1)
    leaving, near_staying = split_rows(staying_0 + staying_1 + near_came, "seq", 2)
    near_came = swap(leaving, "seq", 2)
    out_far = swap(out_far, "chan", 2)
    (g_spec, grad_proj, mixer_sums), grad_normed = mixer_backward(
        own, length, grad_mixed, proj, conv, s_spec, k_spec, conv_w, conv_b, row(skip), weight, tables
    )
    grad_normed, grad_proj, out_far, near_came, up_came, out_blocks, far_came = meet(
        grad_normed, grad_proj, out_far, near_came, up_came, out_blocks, far_came
    )

    grad_normed[3], grad_normed[1] = swap(grad_normed[3], "chan", 1), swap(grad_normed[1], "chan", 1)
    far_down = swap(far_staying + far_came, "chan", 2)
    leaving, near_staying = split_rows(near_staying + near_came, "seq", 4)
    up_leaving, up_staying = split_rows(up_staying + up_came, "seq", 2)
    far_normed, grad_proj, leaving, up_leaving = meet(
        grad_normed[2] + grad_normed[3], grad_proj, leaving, up_leaving
    )
    far_normed = swap(far_normed, "chan", 2)
    near_came, up_came = swap(leaving, "seq", 4), swap(up_leaving, "seq", 2)
    grad_in = input_weight_grad(normed_high, normed_low, grad_proj)
    grad_out = out_near[0] + out_far[0] + swap(out_near[1] + out_far[1], "chan", 1)
    g_spec, grad_in, grad_out, near_came, far_down, up_came = meet(
        g_spec, grad_in, grad_out, near_came, far_down, up_came
    )

    grad_down = near_staying + near_came + far_down
    down_came = swap(grad_down, "seq", 4)
    up_leaving, up_staying = split_rows(up_staying + up_came, "seq", 4)
    up_came = swap(up_leaving, "seq", 4)
    mixer_leaving, mixer_staying = split_rows(
        jnp.concatenate([grad_in.reshape(-1, model), grad_out], 0), "seq", 1
    )
    mixer_came = swap(mixer_leaving, "seq", 1)
    grad_kernel = filter_backward(s_spec, g_spec, tables).reshape(seq_length, width)
    grad_kernel, down_came = meet(grad_kernel, down_came)
    grad_down = join_rows(grad_down, down_came, "seq", 4)
    far_normed, up_came, grad_down = meet(far_normed, up_came, grad_down)
    down_came = swap(grad_down, "seq", 2)

    pieces = [p.reshape(rows, model) for p in (grad_normed[0], grad_normed[1], far_normed)]
    grad_x_rows, sums1 = input_backward(pieces, x_rows, grad_hidden, row(ln1_gain))
    grad_x_rows, grad_kernel, out_blocks, mixer_came, up_came, sums1 = meet(
        grad_x_rows, grad_kernel, out_blocks, mixer_came, up_came, sums1
    )

    grad_x_blocks = transpose_blocks(grad_x_rows.reshape(blocks, quarter, model))
    leaving, staying = split_rows(mixer_staying + mixer_came, "seq", 2)
    came = swap(leaving, "seq", 2)
    grad_up = up_staying + up_came
    grad_down = join_rows(grad_down, down_came, "seq", 2)
    up_came, down_came = swap(grad_up, "seq", 4), swap(grad_down, "seq", 1)
    out_far = swap(out_blocks, "chan", 2)
    grad_fw1, grad_fb1, grad_fw2, grad_fb2, grad_fw3, grad_decay = filter_pull(grad_kernel)
    up_bias_grads = jnp.take(
        jnp.concatenate(bias_grads, 0), jnp.arange(count, dtype=jnp.int32) ^ chan_index, axis=0
    )
    shared = [sums1[0], sums1[1], *[sums2[i] for i in range(4)], up_bias_grads, grad_fw1, grad_fb1, grad_fw2, grad_fb2]
    split = [mixer_sums, grad_fw3, grad_decay]
    shared_flat, split_flat = pack(shared), pack(split)
    shared_flat = shared_flat + swap(shared_flat, "chan", 1)
    side_flat = swap(shared_flat, "chan", 2)
    grad_x_blocks, came, up_came, down_came, out_far, out_blocks = meet(
        grad_x_blocks, came, up_came, down_came, out_far, out_blocks
    )

    grad_x_far = swap(grad_x_blocks, "chan", 2)
    grad_up, grad_down = join_rows(grad_up, up_came, "seq", 4), join_rows(grad_down, down_came, "seq", 1)
    up_came, up_low = swap(grad_up, "seq", 2), swap(grad_up, "seq", 1)
    leaving, staying = split_rows(staying + came, "seq", 4)
    came = swap(leaving, "seq", 4)
    came, up_came, up_low, grad_x_blocks, out_far, out_blocks, side_flat = meet(
        came, up_came, up_low, grad_x_blocks, out_far, out_blocks, side_flat
    )

    mixer_grads = staying + came
    came = swap(mixer_grads, "seq", 4)
    up_high = swap(up_came, "seq", 1)
    flat = jnp.concatenate([shared_flat + side_flat, split_flat])
    side_flat = swap(flat, "seq", 2)
    came, grad_x_far, side_flat, grad_x_blocks, out_far, out_blocks, grad_down, up_high = meet(
        came, grad_x_far, side_flat, grad_x_blocks, out_far, out_blocks, grad_down, up_high
    )

    mixer_grads = join_rows(mixer_grads, came, "seq", 4)
    came, low = swap(mixer_grads, "seq", 2), swap(mixer_grads, "seq", 1)
    grad_x_near, grad_x_side = swap(grad_x_blocks, "chan", 1), swap(grad_x_far, "chan", 1)
    flat = flat + side_flat
    side_flat = swap(flat, "seq", 4)
    came, low, side_flat, grad_x_near, grad_x_side, out_far, out_blocks = meet(
        came, low, side_flat, grad_x_near, grad_x_side, out_far, out_blocks
    )
    flat = flat + side_flat
    side_flat = swap(flat, "seq", 1)
    mixer_grads, came = join_rows(mixer_grads, came, "seq", 2), swap(came, "seq", 1)
    out_near, out_side = swap(out_blocks, "chan", 1), swap(out_far, "chan", 1)
    grad_x = put_together(own, [grad_x_blocks, grad_x_near, grad_x_far, grad_x_side])
    side_flat, out_near, out_side, grad_x = meet(side_flat, out_near, out_side, grad_x)
    flat = flat + side_flat
    grad_up = join_rows(join_rows(grad_up, up_came, "seq", 2), join_rows(up_low, up_high, "seq", 2), "seq", 1)
    output = put_together(own, [out_blocks, out_near, out_far, out_side])
    cut = shared_flat.shape[0]
    grad_ln1_gain, grad_ln1_bias, grad_ln2_gain, grad_ln2_bias, grad_b_out, grad_b_fc2, up_bias_grads, *filt = unpack(
        flat[:cut], shared
    )
    mixer_sums, grad_fw3, grad_decay = unpack(flat[cut:], split)
    grad_b_fc1 = lax.dynamic_slice_in_dim(up_bias_grads, chan_index, 1, 0)[0]
    grad_skip = mixer_sums[0]
    grad_conv_b = mixer_sums[1:4]
    grad_conv_w = mixer_sums[4:13].reshape(3, 3, width)
    grad_b_in = mixer_sums[13:16]
    small = (
        [grad_ln1_gain, grad_ln1_bias, grad_ln2_gain, grad_ln2_bias, grad_b_out, grad_b_fc2, grad_b_fc1]
        + [*filt, grad_fw3, grad_decay, grad_skip, grad_conv_b, grad_conv_w, grad_b_in]
    )
    output, grad_up, came, small = meet(output, grad_up, came, small)
    grad_ln1_gain, grad_ln1_bias, grad_ln2_gain, grad_ln2_bias, grad_b_out, grad_b_fc2, grad_b_fc1 = small[:7]
    *filt, grad_fw3, grad_decay, grad_skip, grad_conv_b, grad_conv_w, grad_b_in = small[7:]
    mixer_grads = join_rows(mixer_grads, join_rows(low, came, "seq", 2), "seq", 1)
    grad_in = jnp.transpose(mixer_grads[: 3 * width].reshape(3, width, model), (2, 0, 1))
    grad_out = mixer_grads[3 * width :]
    return (
        output,
        grad_x,
        grad_ln1_gain,
        grad_ln1_bias,
        grad_in,
        grad_b_in,
        grad_conv_w,
        grad_conv_b,
        *filt,
        grad_fw3,
        grad_decay,
        grad_skip,
        grad_out,
        grad_b_out,
        grad_ln2_gain,
        grad_ln2_bias,
        grad_up,
        grad_b_fc1,
        grad_down,
        grad_b_fc2,
    )


def solution(mesh):
    in_specs = (
        P(None, "seq", None),
        P(),
        P(),
        P(),
        P(None, None, "chan"),
        P(None, "chan"),
        P(None, None, "chan"),
        P(None, "chan"),
        P(),
        P(),
        P(),
        P(),
        P(None, "chan"),
        P("chan"),
        P("chan"),
        P("chan", None),
        P(),
        P(),
        P(),
        P(None, "chan"),
        P("chan"),
        P("chan", None),
        P(),
        P(None, "seq", None),
    )
    out_specs = (
        P(None, "seq", None),
        P(None, "seq", None),
        P(),
        P(),
        P(None, None, "chan"),
        P(None, "chan"),
        P(None, None, "chan"),
        P(None, "chan"),
        P(),
        P(),
        P(),
        P(),
        P(None, "chan"),
        P("chan"),
        P("chan"),
        P("chan", None),
        P(),
        P(),
        P(),
        P(None, "chan"),
        P("chan"),
        P("chan", None),
        P(),
    )
    chan = mesh.shape["chan"]

    def step(*arrays):
        sequences, seq_length = arrays[0].shape[:2]
        whole_sequences = sequences == mesh.shape["seq"] and chan == 4 and seq_length % (64 * sequences) == 0
        body = sequence_device if whole_sequences else spectral_device
        return jax.shard_map(
            body, mesh=mesh, in_specs=in_specs, out_specs=out_specs, check_vma=False
        )(*arrays)

    return step
```
